128 devices in a mesh: scan: 16 (over y_lo, x, core), obj: 8 (over z, y_hi).
Axes of the slice: x: 4, y: 4 (y_hi: 2, y_lo: 2; y = y_hi * 2 + y_lo), z: 4, core: 2. Of those that a mesh axis runs over, the one named last changes fastest.
Arguments:
- object_field: float32 [2, 1024, 2048], P(None, 'obj', 'scan'), may hold values from -6 to 6
- probe_modes: float32 [4, 256, 512], replicated, may hold values from -2 to 2
- patterns: bfloat16 [256, 256, 256], P(('scan', 'obj')), may hold values from 0.02 to 27, as said below
- gain_map: float32 [256, 256], replicated, may hold values from 0.25 to 1.75
- defect_mask: int32 [256, 256], replicated, may hold values 0 or 1
- probe_centres: int32 [256, 2], P(('scan', 'obj')), may hold values from 0 to 127
- live_counts: int32 [128], P(('scan', 'obj')), may hold values from 1 to 2, 192 in all
Outputs:
- object_field: float32 [2, 1024, 2048], P(None, 'obj', 'scan')
- step_sizes: float32 [2], replicated
- patch_energies: float32 [2, 256], P(None, ('scan', 'obj'))
The draws below stay inside these ranges and needn't reach their ends.
Inputs may be any that keep to these rules, and one draw needn't show every extreme that they name: `patterns`: raw detector counts, positive. `live_counts`: some device has all 2 slots live.
All inputs are finite; a program needn't handle non-finite values.
Results may differ from the reference program's by a relative error of at most 0.004.
Values sent between devices are 32-bit elements; how exact they have to be, the bound alone decides.
A program may use at most 64 MiB of HBM per device.

```python
import math
import jax
import jax.numpy as jnp
import numpy as np
from jax import lax

P_SIZE = 256
MODES = 4
TILE = 128
POS_DEV = 2
ITERS = 2
BLOCKS = 128
POSITIONS = 256
NR = 1024
NC = 2048
N_SCAN = 16
N_OBJ = 8


def draw_patterns(key, part):
    key = jax.random.fold_in(key, 11)
    exposure = 3.0 ** (jnp.arange(POSITIONS, dtype=jnp.float32) / POSITIONS)
    base_counts = jnp.exp(jax.random.uniform(key, (POSITIONS, P_SIZE, P_SIZE), jnp.float32, -3.0, 1.4))
    return (base_counts * exposure[:, None, None]).astype(jnp.bfloat16)


def place_ends(result, key, least, largest):
    place = [jax.random.randint(jax.random.fold_in(key, axis), (), 0, length) for axis, length in enumerate(result.shape)]
    longest = result.shape.index(max(result.shape))
    beside = place[:longest] + [(place[longest] + 1) % result.shape[longest]] + place[longest + 1:]
    return result.at[tuple(place)].set(least).at[tuple(beside)].set(largest)


def block_levels(own_key, dims, pieces, least, largest):
    loudness, own = 1.0, jax.random.fold_in(own_key, 6)
    for axis_at, parts in pieces:
        heights = jnp.exp(jax.random.uniform(jax.random.fold_in(own, axis_at), (parts,), jnp.float32, least / len(pieces), largest / len(pieces)))
        loudness = loudness * jnp.repeat(heights, dims[axis_at] // parts).reshape([-1 if axis == axis_at else 1 for axis in range(len(dims))])
    return loudness


def length_profile(number_of, total, reach, skew):
    weights = [(1 << 20) // math.isqrt(standing ** skew) + 1 for standing in range(2, number_of + 1)]
    rest, holding = total - reach - (number_of - 1), [1] * (number_of - 1)
    while rest > 0:
        candidates = [i for i in range(number_of - 1) if holding[i] < reach]
        whole, budget = sum([weights[i] for i in candidates]), rest
        for i in candidates:
            extra = min(reach - holding[i], max(1, budget * weights[i] // whole), rest)
            holding[i] = holding[i] + extra
            rest = rest - extra
    return np.array([reach] + holding)


def ragged_sizes(stream_key, amount, total, limit, lean):
    if amount == 2:
        one = jax.random.randint(stream_key, (), max(1, total - limit), min(limit, total - 1) + 1)
        return jnp.stack([one, total - one])
    tallies = jnp.asarray(length_profile(amount, total, limit, lean), jnp.int32)
    twos = (amount - 1) // 2
    donor, taker = tallies[1:1 + 2 * twos:2], tallies[2:2 + 2 * twos:2]
    room = jnp.minimum(donor - 1, limit - taker)
    passed = jax.random.randint(jax.random.fold_in(stream_key, 1), (twos,), 0, 1 << 20) % (room + 1)
    tallies = tallies.at[1:1 + 2 * twos:2].set(donor - passed).at[2:2 + 2 * twos:2].set(taker + passed)
    return tallies[jax.random.permutation(jax.random.fold_in(stream_key, 2), amount)]


def scatter_about(key, extent, spread, most, split=(), held_as=jnp.bfloat16):
    entries = spread * jax.random.normal(key, extent, jnp.float32)
    if split:
        entries = entries * block_levels(key, extent, split, -0.22, 0.18)
    return jnp.clip(entries, -most, most).astype(held_as)


def setup_inputs(seed: int = 0) -> dict:
    keys = jax.random.split(jax.random.key(seed), 8)
    return {
        "object_field": scatter_about(keys[0], (2, NR, NC), 1.0, 6.0, ((1, 8), (2, 16)), jnp.float32),
        "probe_modes": scatter_about(keys[1], (MODES, P_SIZE, 2 * P_SIZE), 0.25, 2.0, (), jnp.float32),
        "patterns": draw_patterns(jax.random.fold_in(keys[7], 71), 0),
        "gain_map": jnp.clip(1.0 + 0.15 * jax.random.normal(keys[3], (P_SIZE, P_SIZE), jnp.float32), 0.25, 1.75),
        "defect_mask": place_ends((jax.random.randint(keys[4], (P_SIZE, P_SIZE), 0, 16) < 1).astype(jnp.int32), jax.random.fold_in(keys[4], 1), 0, 1),
        "probe_centres": place_ends(jax.random.randint(keys[5], (POSITIONS, 2), 0, TILE), jax.random.fold_in(keys[5], 1), 0, TILE - 1).astype(jnp.int32),
        "live_counts": ragged_sizes(keys[6], BLOCKS, 3 * POS_DEV * BLOCKS // 4, POS_DEV, 2).astype(jnp.int32),
    }


def transform_table(pattern_size, direction_sign):
    indices = jnp.arange(pattern_size, dtype=jnp.int32)
    phase_int = indices[:, None] * indices[None, :] % pattern_size
    angles = phase_int.astype(jnp.float32) * (2.0 * 3.141592653589793 / pattern_size)
    norm_factor = pattern_size ** (-0.5)
    real_part = jnp.cos(angles) * norm_factor
    imag_part = -direction_sign * jnp.sin(angles) * norm_factor
    upper_rows = jnp.concatenate([real_part, imag_part], axis=1)
    lower_rows = jnp.concatenate([-imag_part, real_part], axis=1)
    return jnp.concatenate([upper_rows, lower_rows], axis=0).astype(jnp.bfloat16)

def apply_table(field_data, dft_table):
    wave_shape = field_data.shape
    flat_rows = field_data.reshape(-1, wave_shape[-1])
    return jnp.dot(flat_rows, dft_table, preferred_element_type=jnp.float32).reshape(wave_shape)

def transpose_split(field_data):
    batch_count = field_data.shape[0]
    pattern_size = field_data.shape[1]
    reshaped = field_data.reshape(batch_count, pattern_size, 2, pattern_size)
    return reshaped.transpose(0, 3, 2, 1).reshape(batch_count, pattern_size, 2 * pattern_size)

def split_product(first_field, second_field):
    half_width = first_field.shape[-1] // 2
    real_a = first_field[..., :half_width]
    imag_a = first_field[..., half_width:]
    real_b = second_field[..., :half_width]
    imag_b = second_field[..., half_width:]
    return jnp.concatenate([real_a * real_b - imag_a * imag_b, real_a * imag_b + imag_a * real_b], axis=-1)

def conjugate_split(field_data):
    half_width = field_data.shape[-1] // 2
    return jnp.concatenate([field_data[..., :half_width], -field_data[..., half_width:]], axis=-1)

def detector_amplitude(raw_counts, gain_map, defect_mask):
    corrected = raw_counts.astype(jnp.float32) * gain_map
    neighbour_mean = 0.25 * (jnp.roll(corrected, 1, axis=1) + jnp.roll(corrected, -1, axis=1) + jnp.roll(corrected, 1, axis=2) + jnp.roll(corrected, -1, axis=2))
    filled = jnp.where(defect_mask[None] == 1, neighbour_mean, corrected)
    return jnp.swapaxes(jnp.sqrt(filled), 1, 2)

def exit_residual(patch_split, probe_modes, amplitude_t, forward, inverse):
    exit_wave = split_product(patch_split[:, None], probe_modes[None])
    wave_shape = exit_wave.shape
    pattern_size = wave_shape[-2]
    flat_waves = exit_wave.reshape(-1, pattern_size, 2 * pattern_size)
    half_rows = apply_table(flat_waves.astype(jnp.bfloat16), forward).astype(jnp.bfloat16)
    far_field = apply_table(transpose_split(half_rows), forward).reshape(wave_shape)
    model_power = lax.optimization_barrier(jnp.sum(far_field[..., :pattern_size] ** 2 + far_field[..., pattern_size:] ** 2, axis=1))
    ratios = amplitude_t / jnp.sqrt(jnp.maximum(model_power, 0.25))
    revised = (far_field * jnp.concatenate([ratios, ratios], axis=-1)[:, None]).astype(jnp.bfloat16)
    back_rows = apply_table(revised.reshape(-1, pattern_size, 2 * pattern_size), inverse).astype(jnp.bfloat16)
    back_wave = apply_table(transpose_split(back_rows), inverse).reshape(wave_shape)
    residual_wave = back_wave - exit_wave
    return lax.optimization_barrier(jnp.sum(split_product(residual_wave, conjugate_split(probe_modes)[None]), axis=1))

def reference(object_field, probe_modes, patterns, gain_map, defect_mask, probe_centres, live_counts):
    forward = transform_table(P_SIZE, 1.0)
    inverse = transform_table(P_SIZE, -1.0)
    half_width = P_SIZE // 2
    rows_all = TILE * N_OBJ
    cols_all = TILE * N_SCAN
    slot_ids = jnp.arange(POSITIONS, dtype=jnp.int32)
    block_index = slot_ids // POS_DEV
    slot_index = slot_ids % POS_DEV
    alive_flags = (slot_index < live_counts[block_index]).astype(jnp.float32)
    live_total = jnp.sum(alive_flags)
    start_rows = block_index % N_OBJ * TILE + probe_centres[:, 0] - half_width
    start_cols = block_index // N_OBJ * TILE + probe_centres[:, 1] - half_width
    offsets = jnp.arange(P_SIZE, dtype=jnp.int32)
    probe_power = lax.optimization_barrier(jnp.sum(probe_modes[..., :P_SIZE] ** 2 + probe_modes[..., P_SIZE:] ** 2, axis=0))
    step_list = []
    energy_list = []
    for iteration in range(ITERS):
        current = object_field

        def accumulate(carry_pair, scan_item):
            gradient, coverage = carry_pair
            raw_counts, start_row, start_col, alive_flag = scan_item
            row_index = (start_row + offsets) % rows_all
            col_index = (start_col + offsets) % cols_all
            patch_data = current[:, row_index][:, :, col_index]
            patch_split = jnp.concatenate([patch_data[0], patch_data[1]], axis=-1)[None]
            amplitude_t = detector_amplitude(raw_counts[None], gain_map, defect_mask)
            update_term = exit_residual(patch_split, probe_modes, amplitude_t, forward, inverse)[0] * alive_flag
            update_pair = jnp.stack([update_term[:, :P_SIZE], update_term[:, P_SIZE:]])
            gradient = gradient.at[:, row_index[:, None], col_index[None, :]].add(update_pair)
            coverage = coverage.at[row_index[:, None], col_index[None, :]].add(probe_power * alive_flag)
            return ((gradient, coverage), None)
        start_pair = (jnp.zeros((2, rows_all, cols_all), jnp.float32), jnp.zeros((rows_all, cols_all), jnp.float32))
        totals = lax.scan(accumulate, start_pair, (patterns, start_rows, start_cols, alive_flags))[0]
        gradient, coverage = totals
        direction = gradient / (coverage + 0.5)[None]
        numerator = jnp.sum(direction * gradient)

        def measure(running_total, scan_item):
            start_row, start_col, alive_flag = scan_item
            row_index = (start_row + offsets) % rows_all
            col_index = (start_col + offsets) % cols_all
            patch_data = direction[:, row_index][:, :, col_index]
            term_value = alive_flag * jnp.sum(probe_power * lax.optimization_barrier(jnp.sum(patch_data * patch_data, axis=0)))
            return (running_total + term_value, term_value)
        denominator, energies = lax.scan(measure, jnp.zeros((), jnp.float32), (start_rows, start_cols, alive_flags))
        step_size = numerator / denominator
        step_list.append(step_size)
        energy_list.append(energies * (live_total / denominator))
        object_field = object_field + step_size * direction
    return (object_field, jnp.stack(step_list), jnp.stack(energy_list))
```

```python
import functools

import jax
import jax.numpy as jnp
import numpy as np
from jax import lax
from jax.experimental import pallas as pl
from jax.experimental.pallas import tpu as pltpu
from jax.sharding import PartitionSpec as P

ITERS = 2
MESH = pl.DeviceIdType.MESH
AROUND = [(k, c) for k in (-1, 0, 1) for c in (-1, 0, 1)]


def transform_tables(size):
    indices = np.arange(size, dtype=np.int32)
    phase = (indices[:, None] * indices[None, :] % size).astype(np.float32)
    angles = phase * np.float32(2.0 * 3.141592653589793 / size)
    norm = np.float32(size ** (-0.5))
    cosine, sine = np.cos(angles) * norm, np.sin(angles) * norm
    first = np.block([[cosine, -sine], [sine, cosine]])
    second = np.block([[cosine, sine], [-sine, cosine]])
    return jnp.asarray(np.stack([first, second])).astype(jnp.bfloat16)


def kernel(
    n_scan, n_obj,
    object_ref, probe_ref, patterns_ref, gain_ref, mask_ref, table_ref, centres_ref, live_ref,
    object_out, steps_out, energies_out,
    info, extended, direction_ext, amplitude, power_pad, shifted, coverage, patch, stacked, far, update,
    deposit, fold, fold_x, fold_y, direction, energy_send, energy_recv, sums_x, sums_y,
    info_sem, halo_sem, fold_sem, energy_sem, sums_sem,
):
    tile = object_ref.shape[1]
    size = gain_ref.shape[0]
    modes = probe_ref.shape[0]
    slots = patterns_ref.shape[0]
    extent = tile + size
    my_scan, my_obj = lax.axis_index("scan"), lax.axis_index("obj")

    def at(k, c):
        return {
            "scan": lax.rem(my_scan + (c + n_scan), n_scan),
            "obj": lax.rem(my_obj + (k + n_obj), n_obj),
        }

    def remote(source, target, sems, index, device):
        return pltpu.make_async_remote_copy(
            src_ref=source, dst_ref=target, send_sem=sems.at[(0,) + index],
            recv_sem=sems.at[(1,) + index], device_id=device, device_id_type=MESH,
        )

    partners = [(0, c) for c in range(1, n_scan)] + [(k, 0) for k in range(1, n_obj)]
    partners += [(k, c) for k, c in AROUND if k and c]
    barrier = pltpu.get_barrier_semaphore()
    for k, c in partners:
        pl.semaphore_signal(barrier, inc=1, device_id=at(k, c), device_id_type=MESH)
    pl.semaphore_wait(barrier, len(partners))

    for slot in range(slots):
        info[4, 2 * slot] = centres_ref[slot, 0]
        info[4, 2 * slot + 1] = centres_ref[slot, 1]
    info[4, 2 * slots] = live_ref[0]
    info_copies = [
        remote(info.at[4], info.at[8 - n], info_sem, (n,), at(k, c))
        for n, (k, c) in enumerate(AROUND) if n != 4
    ]

    top, middle, bottom = pl.ds(0, tile), pl.ds(tile, tile), pl.ds(2 * tile, tile)

    def start_gather(source, wide, phase):
        down = remote(source, wide.at[1, :, top, :], halo_sem, (phase, 0), at(1, 0))
        up = remote(source, wide.at[1, :, bottom, :], halo_sem, (phase, 1), at(-1, 0))
        down.start()
        up.start()
        wide[1, :, middle, :] = source[...]

        def sideways(rows, first):
            right = remote(wide.at[1, :, rows, :], wide.at[0, :, rows, :], halo_sem, (phase, first), at(0, 1))
            left = remote(wide.at[1, :, rows, :], wide.at[2, :, rows, :], halo_sem, (phase, first + 1), at(0, -1))
            right.start()
            left.start()
            return [right, left]

        return down, up, sideways, sideways(middle, 2)

    def finish_gather(state):
        down, up, sideways, copies = state
        down.wait_recv()
        copies = copies + sideways(top, 4)
        up.wait_recv()
        copies = copies + sideways(bottom, 6)
        for copy in copies:
            copy.wait()
        down.wait_send()
        up.wait_send()

    state = start_gather(object_ref, extended, 0)
    for copy in info_copies:
        copy.start()

    gain, defect = gain_ref[...], mask_ref[...] == 1
    for slot in range(slots):
        corrected = patterns_ref[slot].astype(jnp.float32) * gain
        mean = 0.25 * (
            pltpu.roll(corrected, 1, 0) + pltpu.roll(corrected, size - 1, 0)
            + pltpu.roll(corrected, 1, 1) + pltpu.roll(corrected, size - 1, 1)
        )
        amplitude[slot] = jnp.sqrt(jnp.where(defect, mean, corrected))
    power = jnp.zeros((size, size), jnp.float32)
    for mode in range(modes):
        power = power + probe_ref[mode, :, :size] ** 2 + probe_ref[mode, :, size:] ** 2
    power_pad[...] = jnp.zeros_like(power_pad)
    for half in range(2):
        power_pad[half, tile : tile + size, :] = power[:, half * tile : (half + 1) * tile]
    for slot in range(slots):
        for column in range(3):
            for plane in range(2):
                zeros = jnp.zeros((tile, tile), jnp.float32)
                deposit[slot, column, plane, :tile, :] = zeros
                deposit[slot, column, plane, tile + size :, :] = zeros
    lane = lax.broadcasted_iota(jnp.int32, (tile, tile), 1)

    for copy in info_copies:
        copy.wait()
    total = jnp.zeros((tile, tile), jnp.float32)
    for n, (k, c) in enumerate(AROUND):
        for slot in range(slots):
            row, column = info[n, 2 * slot], info[n, 2 * slot + 1]
            alive = (slot < info[n, 2 * slots]).astype(jnp.float32)
            rows = pl.ds(2 * tile - tile * k - row, tile)
            low, high = (pltpu.roll(power_pad[half, rows, :], column, 1) for half in range(2))
            if c == 0:
                moved = jnp.where(lane < column, low, high)
            elif c < 0:
                moved = jnp.where(lane < column, high, 0.0)
            else:
                moved = jnp.where(lane < column, 0.0, low)
            shifted[n, slot] = moved
            total = total + moved * alive
    coverage[...] = total
    finish_gather(state)

    wide_lane = lax.broadcasted_iota(jnp.int32, (size, tile), 1)

    def one_slot(slot, carry):
        row, column = centres_ref[slot, 0], centres_ref[slot, 1]
        back_shift = lax.rem(tile - column, tile)
        near = wide_lane < tile - column
        for plane in range(2):
            first, second, third = (
                pltpu.roll(extended[block, plane, pl.ds(row, size), :], back_shift, 1) for block in range(3)
            )
            patch[plane, :, :tile] = jnp.where(near, first, second)
            patch[plane, :, tile:] = jnp.where(near, second, third)
        for mode in range(modes):
            real, imag = patch[0], patch[1]
            probe_real, probe_imag = probe_ref[mode, :, :size], probe_ref[mode, :, size:]
            exit_wave = jnp.concatenate(
                [real * probe_real - imag * probe_imag, real * probe_imag + imag * probe_real], axis=1
            ).astype(jnp.bfloat16)
            half = jnp.dot(exit_wave, table_ref[0], preferred_element_type=jnp.float32).astype(jnp.bfloat16)
            stacked[mode, :size, :] = half[:, :size]
            stacked[mode, size:, :] = half[:, size:]
            far[mode] = jnp.dot(table_ref[1], stacked[mode], preferred_element_type=jnp.float32)
        model = jnp.zeros((size, size), jnp.float32)
        for mode in range(modes):
            model = model + far[mode, :size, :] ** 2 + far[mode, size:, :] ** 2
        ratio = amplitude[slot] * lax.rsqrt(jnp.maximum(model, 0.25))
        power = jnp.concatenate([power_pad[half, tile : tile + size, :] for half in range(2)], axis=1)
        update[0] = -power * patch[0]
        update[1] = -power * patch[1]
        for mode in range(modes):
            stacked[mode, :size, :] = (far[mode, :size, :] * ratio).astype(jnp.bfloat16)
            stacked[mode, size:, :] = (far[mode, size:, :] * ratio).astype(jnp.bfloat16)
            back = jnp.dot(table_ref[0], stacked[mode], preferred_element_type=jnp.float32).astype(jnp.bfloat16)
            back = jnp.concatenate([back[:size], back[size:]], axis=1)
            wave = jnp.dot(back, table_ref[1], preferred_element_type=jnp.float32)
            real, imag = wave[:, :size], wave[:, size:]
            probe_real, probe_imag = probe_ref[mode, :, :size], probe_ref[mode, :, size:]
            update[0] += real * probe_real + imag * probe_imag
            update[1] += imag * probe_real - real * probe_imag
        alive = (slot < live_ref[0]).astype(jnp.float32)
        far_lane = wide_lane < column
        for plane in range(2):
            low = pltpu.roll(update[plane, :, :tile] * alive, column, 1)
            high = pltpu.roll(update[plane, :, tile:] * alive, column, 1)
            deposit[slot, 0, plane, tile : tile + size, :] = jnp.where(far_lane, 0.0, low)
            deposit[slot, 1, plane, tile : tile + size, :] = jnp.where(far_lane, low, high)
            deposit[slot, 2, plane, tile : tile + size, :] = jnp.where(far_lane, high, 0.0)
        return carry

    row_id = lax.broadcasted_iota(jnp.int32, (8, tile), 0)

    def as_row(value, row):
        return jnp.where(row_id == row, jnp.sum(value, axis=0, keepdims=True), 0.0)

    steps, energies = [], []
    live_number = (live_ref[0]).astype(jnp.float32)
    for iteration in range(ITERS):
        lax.fori_loop(0, slots, one_slot, 0)

        for column in (0, 2, 1):
            for plane in range(2):
                summed = deposit[0, column, plane, pl.ds(tile - centres_ref[0, 0], extent), :]
                for slot in range(1, slots):
                    summed = summed + deposit[slot, column, plane, pl.ds(tile - centres_ref[slot, 0], extent), :]
                fold[iteration, column, plane] = summed
        sides = []
        for place, rows in enumerate((top, bottom, middle)):
            right = remote(
                fold.at[iteration, 2, :, rows, :], fold_x.at[iteration, 0, :, rows, :],
                fold_sem, (iteration, 2 * place), at(0, 1),
            )
            left = remote(
                fold.at[iteration, 0, :, rows, :], fold_x.at[iteration, 1, :, rows, :],
                fold_sem, (iteration, 2 * place + 1), at(0, -1),
            )
            right.start()
            left.start()
            sides.append((rows, right, left))

        def add_sides(side):
            rows, right, left = side
            right.wait_recv()
            left.wait_recv()
            fold[iteration, 1, :, rows, :] = (
                fold[iteration, 1, :, rows, :] + fold_x[iteration, 0, :, rows, :] + fold_x[iteration, 1, :, rows, :]
            )

        add_sides(sides[0])
        up = remote(fold.at[iteration, 1, :, top, :], fold_y.at[iteration, 0], fold_sem, (iteration, 6), at(-1, 0))
        up.start()
        add_sides(sides[1])
        down = remote(fold.at[iteration, 1, :, bottom, :], fold_y.at[iteration, 1], fold_sem, (iteration, 7), at(1, 0))
        down.start()
        add_sides(sides[2])
        up.wait_recv()
        down.wait_recv()
        gradient = fold[iteration, 1, :, middle, :] + fold_y[iteration, 0] + fold_y[iteration, 1]
        cover = coverage[...]
        moved = gradient / (cover + 0.5)[None]
        direction[iteration] = moved
        last = iteration == ITERS - 1
        if not last:
            state = start_gather(direction.at[iteration], direction_ext, 1 + iteration)

        squares = moved[0] * moved[0] + moved[1] * moved[1]
        sums_x[iteration, my_scan] = (
            as_row(moved[0] * gradient[0] + moved[1] * gradient[1], 0)
            + as_row(cover * squares, 1) + jnp.where(row_id == 2, live_number, 0.0)
        )
        sums = []
        for other in range(1, n_scan):
            mine = sums_x.at[iteration, my_scan]
            sums.append(remote(mine, mine, sums_sem, (iteration, other), at(0, other)))
            sums[-1].start()
        energy_copies = []
        for n, (k, c) in enumerate(AROUND):
            block = jnp.zeros((8, tile), jnp.float32)
            for slot in range(slots):
                block = block + as_row(squares * shifted[n, slot], slot)
            if n == 4:
                energy_recv[iteration, n] = block
            else:
                energy_send[iteration, n] = block
                copy = remote(
                    energy_send.at[iteration, n], energy_recv.at[iteration, n],
                    energy_sem, (iteration, n), at(k, c),
                )
                copy.start()
                energy_copies.append(copy)
        for copy in sums:
            copy.wait()
        sums_y[iteration, my_obj] = jnp.sum(sums_x[iteration], axis=0)
        sums = []
        for other in range(1, n_obj):
            mine = sums_y.at[iteration, my_obj]
            sums.append(remote(mine, mine, sums_sem, (iteration, n_scan + other), at(other, 0)))
            sums[-1].start()
        for copy in energy_copies:
            copy.wait()
        energy = jnp.sum(energy_recv[iteration], axis=0)
        energy = jnp.sum(energy, axis=1, keepdims=True)
        for copy in sums:
            copy.wait()
        everywhere = jnp.sum(sums_y[iteration], axis=0)
        rows = jnp.sum(everywhere, axis=1, keepdims=True)
        step = rows[0:1] / rows[1:2]
        steps.append(step)
        live_total = rows[2:3] * (1.0 / tile)
        energies.append(energy * (live_total / rows[1:2]))
        for rows, right, left in sides:
            right.wait_send()
            left.wait_send()
        up.wait_send()
        down.wait_send()
        if not last:
            finish_gather(state)
            extended[...] = extended[...] + step.reshape(1, 1, 1, 1) * direction_ext[...]
        else:
            object_out[...] = extended[1, :, middle, :] + step.reshape(1, 1, 1) * direction[iteration]
    for iteration in range(ITERS):
        steps_out[iteration] = steps[iteration][0, 0]
        for slot in range(slots):
            alive = (slot < live_ref[0]).astype(jnp.float32)
            energies_out[iteration, slot] = energies[iteration][slot, 0] * alive


def on_device(n_scan, n_obj, object_field, probe_modes, patterns, gain_map, defect_mask, probe_centres, live_counts):
    tile = object_field.shape[1]
    modes, size = probe_modes.shape[0], probe_modes.shape[1]
    slots = patterns.shape[0]
    extent = tile + size
    table = transform_tables(size)
    f32 = jnp.float32
    vmem, smem = pl.BlockSpec(memory_space=pltpu.VMEM), pl.BlockSpec(memory_space=pltpu.SMEM)
    flops = ITERS * slots * modes * 4 * 2 * size * (2 * size) ** 2
    outputs = pl.pallas_call(
        functools.partial(kernel, n_scan, n_obj),
        out_shape=(
            jax.ShapeDtypeStruct(object_field.shape, f32),
            jax.ShapeDtypeStruct((ITERS,), f32),
            jax.ShapeDtypeStruct((ITERS, slots), f32),
        ),
        in_specs=[vmem] * 6 + [smem] * 2,
        out_specs=(vmem, smem, smem),
        scratch_shapes=[
            pltpu.SMEM((9, 128), jnp.int32),
            pltpu.VMEM((3, 2, extent, tile), f32),
            pltpu.VMEM((3, 2, extent, tile), f32),
            pltpu.VMEM((slots, size, size), f32),
            pltpu.VMEM((2, size + 2 * tile, tile), f32),
            pltpu.VMEM((9, slots, tile, tile), f32),
            pltpu.VMEM((tile, tile), f32),
            pltpu.VMEM((2, size, size), f32),
            pltpu.VMEM((modes, 2 * size, size), jnp.bfloat16),
            pltpu.VMEM((modes, 2 * size, size), f32),
            pltpu.VMEM((2, size, size), f32),
            pltpu.VMEM((slots, 3, 2, size + 2 * tile, tile), f32),
            pltpu.VMEM((ITERS, 3, 2, extent, tile), f32),
            pltpu.VMEM((ITERS, 2, 2, extent, tile), f32),
            pltpu.VMEM((ITERS, 2, 2, tile, tile), f32),
            pltpu.VMEM((ITERS, 2, tile, tile), f32),
            pltpu.VMEM((ITERS, 9, 8, tile), f32),
            pltpu.VMEM((ITERS, 9, 8, tile), f32),
            pltpu.VMEM((ITERS, n_scan, 8, tile), f32),
            pltpu.VMEM((ITERS, n_obj, 8, tile), f32),
            pltpu.SemaphoreType.DMA((2, 9)),
            pltpu.SemaphoreType.DMA((2, ITERS, 8)),
            pltpu.SemaphoreType.DMA((2, ITERS, 8)),
            pltpu.SemaphoreType.DMA((2, ITERS, 9)),
            pltpu.SemaphoreType.DMA((2, ITERS, n_scan + n_obj)),
        ],
        compiler_params=pltpu.CompilerParams(
            collective_id=0, has_side_effects=True, vmem_limit_bytes=48 * 1024 * 1024
        ),
        cost_estimate=pl.CostEstimate(flops=flops, bytes_accessed=8 * 1024 * 1024, transcendentals=0),
    )(object_field, probe_modes, patterns, gain_map, defect_mask, table, probe_centres, live_counts)
    return tuple(outputs)


def solution(mesh):
    placed = (
        P(None, "obj", "scan"),
        P(),
        P(("scan", "obj"), None, None),
        P(),
        P(),
        P(("scan", "obj"), None),
        P(("scan", "obj")),
    )
    return jax.shard_map(
        functools.partial(on_device, mesh.shape["scan"], mesh.shape["obj"]),
        mesh=mesh,
        in_specs=placed,
        out_specs=(P(None, "obj", "scan"), P(), P(None, ("scan", "obj"))),
        check_vma=False,
    )
```

```python
import functools

import jax
import jax.numpy as jnp
import numpy as np
from jax import lax
from jax.experimental import pallas as pl
from jax.experimental.pallas import tpu as pltpu
from jax.sharding import PartitionSpec as P

ITERS = 2
MESH = pl.DeviceIdType.MESH
AROUND = [(k, c) for k in (-1, 0, 1) for c in (-1, 0, 1)]


def transform_tables(size):
    indices = np.arange(size, dtype=np.int32)
    phase = (indices[:, None] * indices[None, :] % size).astype(np.float32)
    angles = phase * np.float32(2.0 * 3.141592653589793 / size)
    norm = np.float32(size ** (-0.5))
    cosine, sine = np.cos(angles) * norm, np.sin(angles) * norm
    first = np.block([[cosine, -sine], [sine, cosine]])
    second = np.block([[cosine, sine], [-sine, cosine]])
    return jnp.asarray(np.stack([first, second])).astype(jnp.bfloat16)


def kernel(
    n_scan, n_obj,
    object_hbm, probe_hbm, patterns_hbm, gain_hbm, mask_hbm, table_hbm, centres_hbm, live_hbm,
    object_out, steps_out, energies_out,
    probe_ref, patterns_ref, gain_ref, mask_ref, table_ref, centres_ref, live_ref,
    info, extended, direction_ext, amplitude, power_pad, shifted, coverage, patch, stacked, far, update,
    deposit, fold, fold_x, fold_y, energy_send, energy_recv, sums_x, sums_y,
    load_sem, info_sem, halo_sem, fold_sem, energy_sem, sums_sem,
):
    tile = object_hbm.shape[1]
    size = gain_ref.shape[0]
    modes = probe_ref.shape[0]
    slots = patterns_ref.shape[0]
    my_scan, my_obj = lax.axis_index("scan"), lax.axis_index("obj")
    top, middle, bottom = pl.ds(0, tile), pl.ds(tile, tile), pl.ds(2 * tile, tile)

    def at(k, c):
        return {
            "scan": lax.rem(my_scan + (c + n_scan), n_scan),
            "obj": lax.rem(my_obj + (k + n_obj), n_obj),
        }

    def remote(source, target, sems, index, device):
        return pltpu.make_async_remote_copy(
            src_ref=source, dst_ref=target, send_sem=sems.at[(0,) + index],
            recv_sem=sems.at[(1,) + index], device_id=device, device_id_type=MESH,
        )

    pairs = (
        (object_hbm, extended.at[1, :, middle, :]), (centres_hbm, centres_ref), (live_hbm, live_ref),
        (patterns_hbm, patterns_ref), (gain_hbm, gain_ref), (mask_hbm, mask_ref),
        (probe_hbm, probe_ref), (table_hbm, table_ref),
    )
    loads = [
        pltpu.make_async_copy(source, target, load_sem.at[n]) for n, (source, target) in enumerate(pairs)
    ]
    for load in loads:
        load.start()

    partners = [(0, c) for c in range(1, n_scan)] + [(k, 0) for k in range(1, n_obj)]
    partners += [(k, c) for k, c in AROUND if k and c]
    barrier = pltpu.get_barrier_semaphore()
    for k, c in partners:
        pl.semaphore_signal(barrier, inc=1, device_id=at(k, c), device_id_type=MESH)
    pl.semaphore_wait(barrier, len(partners))

    def start_gather(wide, phase):
        along = []
        for plane in range(2):
            mine = wide.at[1, plane, middle, :]
            along.append(remote(mine, wide.at[1, plane, top, :], halo_sem, (phase, 2 * plane), at(1, 0)))
            along.append(remote(mine, wide.at[1, plane, bottom, :], halo_sem, (phase, 2 * plane + 1), at(-1, 0)))
        for copy in along:
            copy.start()
        return along, [send_sideways(wide, phase, plane, middle, 4 + 2 * plane) for plane in range(2)]

    def send_sideways(wide, phase, plane, rows, first):
        mine = wide.at[1, plane, rows, :]
        pair = (
            remote(mine, wide.at[0, plane, rows, :], halo_sem, (phase, first), at(0, 1)),
            remote(mine, wide.at[2, plane, rows, :], halo_sem, (phase, first + 1), at(0, -1)),
        )
        for copy in pair:
            copy.start()
        return pair

    def pass_on(wide, phase, along, beside):
        beside = list(beside)
        for n, copy in enumerate(along):
            copy.wait_recv()
            beside.append(send_sideways(wide, phase, n // 2, bottom if n % 2 else top, 8 + 2 * n))
        return beside

    def finish_gather(along, beside):
        for pair in beside:
            for copy in pair:
                copy.wait()
        for copy in along:
            copy.wait_send()

    loads[0].wait()
    along, beside = start_gather(extended, 0)

    loads[1].wait()
    loads[2].wait()
    for slot in range(slots):
        info[4, 2 * slot] = centres_ref[slot, 0]
        info[4, 2 * slot + 1] = centres_ref[slot, 1]
    info[4, 2 * slots] = live_ref[0]
    info_copies = [
        remote(info.at[4], info.at[8 - n], info_sem, (n,), at(k, c))
        for n, (k, c) in enumerate(AROUND) if n != 4
    ]
    for copy in info_copies:
        copy.start()

    for load in loads[3:6]:
        load.wait()
    gain, defect = gain_ref[...], mask_ref[...] == 1
    for slot in range(slots):
        corrected = patterns_ref[slot].astype(jnp.float32) * gain
        mean = 0.25 * (
            pltpu.roll(corrected, 1, 0) + pltpu.roll(corrected, size - 1, 0)
            + pltpu.roll(corrected, 1, 1) + pltpu.roll(corrected, size - 1, 1)
        )
        amplitude[slot] = jnp.sqrt(jnp.where(defect, mean, corrected))
    loads[6].wait()
    power = jnp.zeros((size, size), jnp.float32)
    for mode in range(modes):
        power = power + probe_ref[mode, :, :size] ** 2 + probe_ref[mode, :, size:] ** 2
    power_pad[...] = jnp.zeros_like(power_pad)
    for half in range(2):
        power_pad[half, tile : tile + size, :] = power[:, half * tile : (half + 1) * tile]
    for slot in range(slots):
        for column in range(3):
            for plane in range(2):
                zeros = jnp.zeros((tile, tile), jnp.float32)
                deposit[slot, column, plane, :tile, :] = zeros
                deposit[slot, column, plane, tile + size :, :] = zeros
    beside = pass_on(extended, 0, along, beside)
    loads[7].wait()

    for copy in info_copies:
        copy.wait()
    lane = lax.broadcasted_iota(jnp.int32, (tile, tile), 1)
    total = jnp.zeros((tile, tile), jnp.float32)
    for n, (k, c) in enumerate(AROUND):
        for slot in range(slots):
            row, column = info[n, 2 * slot], info[n, 2 * slot + 1]
            alive = (slot < info[n, 2 * slots]).astype(jnp.float32)
            rows = pl.ds(2 * tile - tile * k - row, tile)
            low, high = (pltpu.roll(power_pad[half, rows, :], column, 1) for half in range(2))
            if c == 0:
                moved = jnp.where(lane < column, low, high)
            elif c < 0:
                moved = jnp.where(lane < column, high, 0.0)
            else:
                moved = jnp.where(lane < column, 0.0, low)
            shifted[n, slot] = moved
            total = total + moved * alive
    coverage[...] = total
    finish_gather(along, beside)

    wide_lane = lax.broadcasted_iota(jnp.int32, (size, tile), 1)

    def one_slot(slot, carry):
        row, column = centres_ref[slot, 0], centres_ref[slot, 1]
        back_shift = lax.rem(tile - column, tile)
        near = wide_lane < tile - column
        for plane in range(2):
            first, second, third = (
                pltpu.roll(extended[block, plane, pl.ds(row, size), :], back_shift, 1) for block in range(3)
            )
            patch[plane, :, :tile] = jnp.where(near, first, second)
            patch[plane, :, tile:] = jnp.where(near, second, third)
        for mode in range(modes):
            real, imag = patch[0], patch[1]
            probe_real, probe_imag = probe_ref[mode, :, :size], probe_ref[mode, :, size:]
            exit_wave = jnp.concatenate(
                [real * probe_real - imag * probe_imag, real * probe_imag + imag * probe_real], axis=1
            ).astype(jnp.bfloat16)
            half = jnp.dot(exit_wave, table_ref[0], preferred_element_type=jnp.float32).astype(jnp.bfloat16)
            stacked[mode, :size, :] = half[:, :size]
            stacked[mode, size:, :] = half[:, size:]
            far[mode] = jnp.dot(table_ref[1], stacked[mode], preferred_element_type=jnp.float32)
        model = jnp.zeros((size, size), jnp.float32)
        for mode in range(modes):
            model = model + far[mode, :size, :] ** 2 + far[mode, size:, :] ** 2
        ratio = amplitude[slot] * lax.rsqrt(jnp.maximum(model, 0.25))
        power = jnp.concatenate([power_pad[half, tile : tile + size, :] for half in range(2)], axis=1)
        update[0] = -power * patch[0]
        update[1] = -power * patch[1]
        for mode in range(modes):
            stacked[mode, :size, :] = (far[mode, :size, :] * ratio).astype(jnp.bfloat16)
            stacked[mode, size:, :] = (far[mode, size:, :] * ratio).astype(jnp.bfloat16)
            back = jnp.dot(table_ref[0], stacked[mode], preferred_element_type=jnp.float32).astype(jnp.bfloat16)
            back = jnp.concatenate([back[:size], back[size:]], axis=1)
            wave = jnp.dot(back, table_ref[1], preferred_element_type=jnp.float32)
            real, imag = wave[:, :size], wave[:, size:]
            probe_real, probe_imag = probe_ref[mode, :, :size], probe_ref[mode, :, size:]
            update[0] += real * probe_real + imag * probe_imag
            update[1] += imag * probe_real - real * probe_imag
        alive = (slot < live_ref[0]).astype(jnp.float32)
        far_lane = wide_lane < column
        for plane in range(2):
            low = pltpu.roll(update[plane, :, :tile] * alive, column, 1)
            high = pltpu.roll(update[plane, :, tile:] * alive, column, 1)
            deposit[slot, 0, plane, tile : tile + size, :] = jnp.where(far_lane, 0.0, low)
            deposit[slot, 1, plane, tile : tile + size, :] = jnp.where(far_lane, low, high)
            deposit[slot, 2, plane, tile : tile + size, :] = jnp.where(far_lane, high, 0.0)
        return carry

    row_id = lax.broadcasted_iota(jnp.int32, (8, tile), 0)

    def as_row(value, row):
        return jnp.where(row_id == row, jnp.sum(value, axis=0, keepdims=True), 0.0)

    live_number = live_ref[0].astype(jnp.float32)

    def sum_start(table, mine, base, count, where, iteration):
        copies = []
        for other in range(1, count):
            block = table.at[iteration, mine]
            copies.append(remote(block, block, sums_sem, (iteration, base + other), where(other)))
            copies[-1].start()
        return copies

    energy_copies, scales = [], []
    for iteration in range(ITERS):
        lax.fori_loop(0, slots, one_slot, 0)

        def gathered(column, plane, block):
            summed = None
            for slot in range(slots):
                rows = pl.ds((block + 1) * tile - centres_ref[slot, 0], tile)
                term = deposit[slot, column, plane, rows, :]
                summed = term if summed is None else summed + term
            return summed

        sides = {}
        blocks = (top, middle, bottom)
        for place, (plane, block) in enumerate(((0, 0), (0, 2), (1, 0), (1, 2), (0, 1), (1, 1))):
            rows = blocks[block]
            pair = []
            for side, (column, step) in enumerate(((2, 1), (0, -1))):
                fold[iteration, column, plane, rows, :] = gathered(column, plane, block)
                copy = remote(
                    fold.at[iteration, column, plane, rows, :], fold_x.at[iteration, side, plane, rows, :],
                    fold_sem, (iteration, 2 * place + side), at(0, step),
                )
                copy.start()
                pair.append(copy)
            sides[plane, block] = pair
        for plane in range(2):
            for block in (0, 2, 1):
                fold[iteration, 1, plane, blocks[block], :] = gathered(1, plane, block)

        def add_sides(plane, block):
            rows = blocks[block]
            for copy in sides[plane, block]:
                copy.wait_recv()
            return (
                fold[iteration, 1, plane, rows, :]
                + fold_x[iteration, 0, plane, rows, :] + fold_x[iteration, 1, plane, rows, :]
            )

        folds = []
        for plane in range(2):
            for side, (block, step) in enumerate(((0, -1), (2, 1))):
                rows = blocks[block]
                fold[iteration, 1, plane, rows, :] = add_sides(plane, block)
                copy = remote(
                    fold.at[iteration, 1, plane, rows, :], fold_y.at[iteration, side, plane],
                    fold_sem, (iteration, 12 + 2 * plane + side), at(step, 0),
                )
                copy.start()
                folds.append(copy)
        own = [add_sides(plane, 1) for plane in range(2)]
        cover = coverage[...]
        gradient, moved = [], []
        for plane in range(2):
            folds[2 * plane].wait_recv()
            folds[2 * plane + 1].wait_recv()
            gradient.append(own[plane] + fold_y[iteration, 0, plane] + fold_y[iteration, 1, plane])
            moved.append(gradient[plane] / (cover + 0.5))
            direction_ext[iteration, 1, plane, middle, :] = moved[plane]
        last = iteration == ITERS - 1
        if not last:
            along, beside = start_gather(direction_ext.at[iteration], 1 + iteration)

        squares = moved[0] * moved[0] + moved[1] * moved[1]
        sums_x[iteration, my_scan] = (
            as_row(moved[0] * gradient[0] + moved[1] * gradient[1], 0)
            + as_row(cover * squares, 1) + jnp.where(row_id == 2, live_number, 0.0)
        )
        first_sums = sum_start(sums_x, my_scan, 0, n_scan, lambda other: at(0, other), iteration)
        for n, (k, c) in enumerate(AROUND):
            block = jnp.zeros((8, tile), jnp.float32)
            for slot in range(slots):
                block = block + as_row(squares * shifted[n, slot], slot)
            if n == 4:
                energy_recv[iteration, n] = block
            else:
                energy_send[iteration, n] = block
                copy = remote(
                    energy_send.at[iteration, n], energy_recv.at[iteration, n],
                    energy_sem, (iteration, n), at(k, c),
                )
                copy.start()
                energy_copies.append(copy)
        for copy in first_sums:
            copy.wait()
        sums_y[iteration, my_obj] = jnp.sum(sums_x[iteration], axis=0)
        second_sums = sum_start(sums_y, my_obj, n_scan, n_obj, lambda other: at(other, 0), iteration)
        if not last:
            beside = pass_on(direction_ext.at[iteration], 1 + iteration, along, beside)
        for pair in sides.values():
            for copy in pair:
                copy.wait_send()
        for copy in folds:
            copy.wait_send()
        for copy in second_sums:
            copy.wait()
        everywhere = jnp.sum(sums_y[iteration], axis=0)
        rows = jnp.sum(everywhere, axis=1, keepdims=True)
        step = rows[0:1] / rows[1:2]
        scales.append((step, rows[2:3] * (1.0 / tile) / rows[1:2]))
        if not last:
            finish_gather(along, beside)
            extended[...] = extended[...] + step.reshape(1, 1, 1, 1) * direction_ext[iteration]
        else:
            object_out[...] = (
                extended[1, :, middle, :] + step.reshape(1, 1, 1) * direction_ext[iteration, 1, :, middle, :]
            )
    for copy in energy_copies:
        copy.wait()
    for iteration in range(ITERS):
        step, scale = scales[iteration]
        steps_out[iteration] = step[0, 0]
        energy = jnp.sum(jnp.sum(energy_recv[iteration], axis=0), axis=1, keepdims=True) * scale
        for slot in range(slots):
            alive = (slot < live_ref[0]).astype(jnp.float32)
            energies_out[iteration, slot] = energy[slot, 0] * alive


def on_device(n_scan, n_obj, object_field, probe_modes, patterns, gain_map, defect_mask, probe_centres, live_counts):
    tile = object_field.shape[1]
    modes, size = probe_modes.shape[0], probe_modes.shape[1]
    slots = patterns.shape[0]
    extent = tile + size
    table = transform_tables(size)
    f32 = jnp.float32
    vmem, smem = pl.BlockSpec(memory_space=pltpu.VMEM), pl.BlockSpec(memory_space=pltpu.SMEM)
    hbm = pl.BlockSpec(memory_space=pltpu.HBM)
    flops = ITERS * slots * modes * 4 * 2 * size * (2 * size) ** 2
    outputs = pl.pallas_call(
        functools.partial(kernel, n_scan, n_obj),
        out_shape=(
            jax.ShapeDtypeStruct(object_field.shape, f32),
            jax.ShapeDtypeStruct((ITERS,), f32),
            jax.ShapeDtypeStruct((ITERS, slots), f32),
        ),
        in_specs=[hbm] * 8,
        out_specs=(vmem, smem, smem),
        scratch_shapes=[
            pltpu.VMEM(probe_modes.shape, f32),
            pltpu.VMEM(patterns.shape, patterns.dtype),
            pltpu.VMEM(gain_map.shape, f32),
            pltpu.VMEM(defect_mask.shape, jnp.int32),
            pltpu.VMEM(table.shape, table.dtype),
            pltpu.SMEM(probe_centres.shape, jnp.int32),
            pltpu.SMEM(live_counts.shape, jnp.int32),
            pltpu.SMEM((9, 128), jnp.int32),
            pltpu.VMEM((3, 2, extent, tile), f32),
            pltpu.VMEM((ITERS, 3, 2, extent, tile), f32),
            pltpu.VMEM((slots, size, size), f32),
            pltpu.VMEM((2, size + 2 * tile, tile), f32),
            pltpu.VMEM((9, slots, tile, tile), f32),
            pltpu.VMEM((tile, tile), f32),
            pltpu.VMEM((2, size, size), f32),
            pltpu.VMEM((modes, 2 * size, size), jnp.bfloat16),
            pltpu.VMEM((modes, 2 * size, size), f32),
            pltpu.VMEM((2, size, size), f32),
            pltpu.VMEM((slots, 3, 2, size + 2 * tile, tile), f32),
            pltpu.VMEM((ITERS, 3, 2, extent, tile), f32),
            pltpu.VMEM((ITERS, 2, 2, extent, tile), f32),
            pltpu.VMEM((ITERS, 2, 2, tile, tile), f32),
            pltpu.VMEM((ITERS, 9, 8, tile), f32),
            pltpu.VMEM((ITERS, 9, 8, tile), f32),
            pltpu.VMEM((ITERS, n_scan, 8, tile), f32),
            pltpu.VMEM((ITERS, n_obj, 8, tile), f32),
            pltpu.SemaphoreType.DMA((8,)),
            pltpu.SemaphoreType.DMA((2, 9)),
            pltpu.SemaphoreType.DMA((2, ITERS, 16)),
            pltpu.SemaphoreType.DMA((2, ITERS, 16)),
            pltpu.SemaphoreType.DMA((2, ITERS, 9)),
            pltpu.SemaphoreType.DMA((2, ITERS, n_scan + n_obj)),
        ],
        compiler_params=pltpu.CompilerParams(
            collective_id=0, has_side_effects=True, vmem_limit_bytes=62 * 1024 * 1024
        ),
        cost_estimate=pl.CostEstimate(flops=flops, bytes_accessed=8 * 1024 * 1024, transcendentals=0),
    )(object_field, probe_modes, patterns, gain_map, defect_mask, table, probe_centres, live_counts)
    return tuple(outputs)


def solution(mesh):
    placed = (
        P(None, "obj", "scan"),
        P(),
        P(("scan", "obj"), None, None),
        P(),
        P(),
        P(("scan", "obj"), None),
        P(("scan", "obj")),
    )
    return jax.shard_map(
        functools.partial(on_device, mesh.shape["scan"], mesh.shape["obj"]),
        mesh=mesh,
        in_specs=placed,
        out_specs=(P(None, "obj", "scan"), P(), P(None, ("scan", "obj"))),
        check_vma=False,
    )
```

```python
import functools

import jax
import jax.numpy as jnp
import numpy as np
from jax import lax
from jax.experimental import pallas as pl
from jax.experimental.pallas import tpu as pltpu
from jax.sharding import PartitionSpec as P

ITERS = 2
MESH = pl.DeviceIdType.MESH
AROUND = [(k, c) for k in (-1, 0, 1) for c in (-1, 0, 1)]


def transform_tables(size):
    indices = np.arange(size, dtype=np.int32)
    phase = (indices[:, None] * indices[None, :] % size).astype(np.float32)
    angles = phase * np.float32(2.0 * 3.141592653589793 / size)
    norm = np.float32(size ** (-0.5))
    cosine, sine = np.cos(angles) * norm, np.sin(angles) * norm
    first = np.block([[cosine, -sine], [sine, cosine]])
    second = np.block([[cosine, sine], [-sine, cosine]])
    return jnp.asarray(np.stack([first, second])).astype(jnp.bfloat16)


def kernel(
    n_scan, n_obj,
    object_hbm, probe_hbm, patterns_hbm, gain_hbm, mask_hbm, table_hbm, centres_hbm, live_hbm,
    object_out, steps_out, energies_out,
    probe_ref, patterns_ref, gain_ref, mask_ref, table_ref, centres_ref, live_ref,
    info, extended, direction_ext, amplitude, power_pad, shifted, coverage, patch, waves, stacked, far, update,
    deposit, fold, fold_x, fold_y, fold_z, energy_send, energy_recv, sums_x, sums_y,
    load_sem, info_sem, halo_sem, fold_sem, energy_sem, sums_sem,
):
    tile = object_hbm.shape[1]
    size = gain_ref.shape[0]
    modes = probe_ref.shape[0]
    slots = patterns_ref.shape[0]
    my_scan, my_obj = lax.axis_index("scan"), lax.axis_index("obj")
    top, middle, bottom = pl.ds(0, tile), pl.ds(tile, tile), pl.ds(2 * tile, tile)

    def at(k, c):
        return {
            "scan": lax.rem(my_scan + (c + n_scan), n_scan),
            "obj": lax.rem(my_obj + (k + n_obj), n_obj),
        }

    def remote(source, target, sems, index, device):
        return pltpu.make_async_remote_copy(
            src_ref=source, dst_ref=target, send_sem=sems.at[(0,) + index],
            recv_sem=sems.at[(1,) + index], device_id=device, device_id_type=MESH,
        )

    pairs = (
        (object_hbm, extended.at[1, :, middle, :]), (centres_hbm, centres_ref), (live_hbm, live_ref),
        (patterns_hbm, patterns_ref), (gain_hbm, gain_ref), (mask_hbm, mask_ref),
        (probe_hbm, probe_ref), (table_hbm, table_ref),
    )
    loads = [
        pltpu.make_async_copy(source, target, load_sem.at[n]) for n, (source, target) in enumerate(pairs)
    ]
    for load in loads:
        load.start()

    partners = [(0, c) for c in range(1, n_scan)] + [(k, 0) for k in range(1, n_obj)]
    partners += [(k, c) for k, c in AROUND if k and c]
    barrier = pltpu.get_barrier_semaphore()
    for k, c in partners:
        pl.semaphore_signal(barrier, inc=1, device_id=at(k, c), device_id_type=MESH)
    pl.semaphore_wait(barrier, len(partners))

    odd = lax.rem(my_obj, 2)
    near_start = pl.multiple_of(2 * tile * (1 - odd), tile)
    far_start = pl.multiple_of(2 * tile * odd, tile)
    near, far_rows = pl.ds(near_start, tile), pl.ds(far_start, tile)
    pair_step, pass_step = 1 - 2 * odd, 2 - 4 * odd

    def send_sideways(wide, phase, plane, rows, first):
        mine = wide.at[1, plane, rows, :]
        pair = (
            remote(mine, wide.at[0, plane, rows, :], halo_sem, (phase, first), at(0, 1)),
            remote(mine, wide.at[2, plane, rows, :], halo_sem, (phase, first + 1), at(0, -1)),
        )
        for copy in pair:
            copy.start()
        return pair

    def start_gather(wide, phase):
        direct = [
            remote(
                wide.at[1, plane, middle, :], wide.at[1, plane, far_rows, :],
                halo_sem, (phase, plane), at(pair_step, 0),
            )
            for plane in range(2)
        ]
        for copy in direct:
            copy.start()
        return direct, [send_sideways(wide, phase, plane, middle, 4 + 2 * plane) for plane in range(2)]

    def pass_near(wide, phase, direct, beside):
        passed = []
        for plane in range(2):
            direct[plane].wait_recv()
            passed.append(remote(
                wide.at[1, plane, near, :], wide.at[1, plane, far_rows, :],
                halo_sem, (phase, 2 + plane), at(pass_step, 0),
            ))
            passed[plane].start()
            beside.append(send_sideways(wide, phase, plane, near, 8 + 2 * plane))
        return passed

    def pass_far(wide, phase, passed, beside):
        for plane in range(2):
            passed[plane].wait_recv()
            beside.append(send_sideways(wide, phase, plane, far_rows, 12 + 2 * plane))

    def finish_gather(direct, passed, beside):
        for pair in beside:
            for copy in pair:
                copy.wait()
        for copy in direct + passed:
            copy.wait_send()

    loads[0].wait()
    direct, beside = start_gather(extended, 0)

    loads[1].wait()
    loads[2].wait()
    for slot in range(slots):
        info[4, 2 * slot] = centres_ref[slot, 0]
        info[4, 2 * slot + 1] = centres_ref[slot, 1]
    info[4, 2 * slots] = live_ref[0]
    info_copies = [
        remote(info.at[4], info.at[8 - n], info_sem, (n,), at(k, c))
        for n, (k, c) in enumerate(AROUND) if n != 4
    ]
    for copy in info_copies:
        copy.start()

    for load in loads[3:6]:
        load.wait()
    gain, defect = gain_ref[...], mask_ref[...] == 1
    for slot in range(slots):
        corrected = patterns_ref[slot].astype(jnp.float32) * gain
        mean = 0.25 * (
            pltpu.roll(corrected, 1, 0) + pltpu.roll(corrected, size - 1, 0)
            + pltpu.roll(corrected, 1, 1) + pltpu.roll(corrected, size - 1, 1)
        )
        amplitude[slot] = jnp.sqrt(jnp.where(defect, mean, corrected))
    loads[6].wait()
    power = jnp.zeros((size, size), jnp.float32)
    for mode in range(modes):
        power = power + probe_ref[mode, :, :size] ** 2 + probe_ref[mode, :, size:] ** 2
    power_pad[...] = jnp.zeros_like(power_pad)
    for half in range(2):
        power_pad[half, tile : tile + size, :] = power[:, half * tile : (half + 1) * tile]
    for slot in range(slots):
        for column in range(3):
            for plane in range(2):
                zeros = jnp.zeros((tile, tile), jnp.float32)
                deposit[slot, column, plane, :tile, :] = zeros
                deposit[slot, column, plane, tile + size :, :] = zeros
    passed = pass_near(extended, 0, direct, beside)
    loads[7].wait()

    for copy in info_copies:
        copy.wait()
    pass_far(extended, 0, passed, beside)
    lane = lax.broadcasted_iota(jnp.int32, (tile, tile), 1)
    total = jnp.zeros((tile, tile), jnp.float32)
    for n, (k, c) in enumerate(AROUND):
        for slot in range(slots):
            row, column = info[n, 2 * slot], info[n, 2 * slot + 1]
            alive = (slot < info[n, 2 * slots]).astype(jnp.float32)
            rows = pl.ds(2 * tile - tile * k - row, tile)
            low, high = (pltpu.roll(power_pad[half, rows, :], column, 1) for half in range(2))
            if c == 0:
                moved = jnp.where(lane < column, low, high)
            elif c < 0:
                moved = jnp.where(lane < column, high, 0.0)
            else:
                moved = jnp.where(lane < column, 0.0, low)
            shifted[n, slot] = moved
            total = total + moved * alive
    coverage[...] = total
    finish_gather(direct, passed, beside)

    wide_lane = lax.broadcasted_iota(jnp.int32, (size, tile), 1)

    def one_slot(slot, carry):
        row, column = centres_ref[slot, 0], centres_ref[slot, 1]
        back_shift = lax.rem(tile - column, tile)
        near = wide_lane < tile - column
        for plane in range(2):
            first, second, third = (
                pltpu.roll(extended[block, plane, pl.ds(row, size), :], back_shift, 1) for block in range(3)
            )
            patch[plane, :, :tile] = jnp.where(near, first, second)
            patch[plane, :, tile:] = jnp.where(near, second, third)
        for mode in range(modes):
            real, imag = patch[0], patch[1]
            probe_real, probe_imag = probe_ref[mode, :, :size], probe_ref[mode, :, size:]
            waves[mode, :, :size] = (real * probe_real - imag * probe_imag).astype(jnp.bfloat16)
            waves[mode, :, size:] = (real * probe_imag + imag * probe_real).astype(jnp.bfloat16)
        for mode in range(modes):
            half = jnp.dot(waves[mode], table_ref[0], preferred_element_type=jnp.float32).astype(jnp.bfloat16)
            stacked[mode, :size, :] = half[:, :size]
            stacked[mode, size:, :] = half[:, size:]
        for mode in range(modes):
            far[mode] = jnp.dot(table_ref[1], stacked[mode], preferred_element_type=jnp.float32)
        model = jnp.zeros((size, size), jnp.float32)
        for mode in range(modes):
            model = model + far[mode, :size, :] ** 2 + far[mode, size:, :] ** 2
        ratio = amplitude[slot] * lax.rsqrt(jnp.maximum(model, 0.25))
        for mode in range(modes):
            stacked[mode, :size, :] = (far[mode, :size, :] * ratio).astype(jnp.bfloat16)
            stacked[mode, size:, :] = (far[mode, size:, :] * ratio).astype(jnp.bfloat16)
        for mode in range(modes):
            back = jnp.dot(table_ref[0], stacked[mode], preferred_element_type=jnp.float32).astype(jnp.bfloat16)
            waves[mode, :, :size] = back[:size]
            waves[mode, :, size:] = back[size:]
        power = jnp.concatenate([power_pad[half, tile : tile + size, :] for half in range(2)], axis=1)
        update[0] = -power * patch[0]
        update[1] = -power * patch[1]
        for mode in range(modes):
            wave = jnp.dot(waves[mode], table_ref[1], preferred_element_type=jnp.float32)
            real, imag = wave[:, :size], wave[:, size:]
            probe_real, probe_imag = probe_ref[mode, :, :size], probe_ref[mode, :, size:]
            update[0] += real * probe_real + imag * probe_imag
            update[1] += imag * probe_real - real * probe_imag
        alive = (slot < live_ref[0]).astype(jnp.float32)
        far_lane = wide_lane < column
        for plane in range(2):
            low = pltpu.roll(update[plane, :, :tile] * alive, column, 1)
            high = pltpu.roll(update[plane, :, tile:] * alive, column, 1)
            deposit[slot, 0, plane, tile : tile + size, :] = jnp.where(far_lane, 0.0, low)
            deposit[slot, 1, plane, tile : tile + size, :] = jnp.where(far_lane, low, high)
            deposit[slot, 2, plane, tile : tile + size, :] = jnp.where(far_lane, high, 0.0)
        return carry

    row_id = lax.broadcasted_iota(jnp.int32, (8, tile), 0)

    def as_row(value, row):
        return jnp.where(row_id == row, jnp.sum(value, axis=0, keepdims=True), 0.0)

    live_number = live_ref[0].astype(jnp.float32)

    def sum_start(table, mine, base, count, where, iteration):
        copies = []
        for other in range(1, count):
            block = table.at[iteration, mine]
            copies.append(remote(block, block, sums_sem, (iteration, base + other), where(other)))
            copies[-1].start()
        return copies

    energy_copies, scales = [], []
    for iteration in range(ITERS):
        lax.fori_loop(0, slots, one_slot, 0)

        def gathered(column, plane, start):
            summed = None
            for slot in range(slots):
                term = deposit[slot, column, plane, pl.ds(start + tile - centres_ref[slot, 0], tile), :]
                summed = term if summed is None else summed + term
            return summed

        sides = {}
        starts = {"far": far_start, "near": near_start, "middle": tile}
        for place, (name, plane) in enumerate((name, plane) for name in starts for plane in range(2)):
            rows = pl.ds(starts[name], tile)
            pair = []
            for side, (column, step) in enumerate(((2, 1), (0, -1))):
                fold[iteration, column, plane, rows, :] = gathered(column, plane, starts[name])
                copy = remote(
                    fold.at[iteration, column, plane, rows, :], fold_x.at[iteration, side, plane, rows, :],
                    fold_sem, (iteration, 2 * place + side), at(0, step),
                )
                copy.start()
                pair.append(copy)
            sides[name, plane] = pair
        for name in starts:
            for plane in range(2):
                fold[iteration, 1, plane, pl.ds(starts[name], tile), :] = gathered(1, plane, starts[name])

        def add_sides(name, plane):
            rows = pl.ds(starts[name], tile)
            for copy in sides[name, plane]:
                copy.wait_recv()
            return (
                fold[iteration, 1, plane, rows, :]
                + fold_x[iteration, 0, plane, rows, :] + fold_x[iteration, 1, plane, rows, :]
            )

        passed_on, folds = [], []
        for plane in range(2):
            fold[iteration, 1, plane, far_rows, :] = add_sides("far", plane)
            passed_on.append(remote(
                fold.at[iteration, 1, plane, far_rows, :], fold_z.at[iteration, plane],
                fold_sem, (iteration, 12 + plane), at(-pass_step, 0),
            ))
            passed_on[plane].start()
        for plane in range(2):
            total = add_sides("near", plane)
            passed_on[plane].wait_recv()
            fold[iteration, 1, plane, near, :] = total + fold_z[iteration, plane]
            folds.append(remote(
                fold.at[iteration, 1, plane, near, :], fold_y.at[iteration, plane],
                fold_sem, (iteration, 14 + plane), at(pair_step, 0),
            ))
            folds[plane].start()
        own = [add_sides("middle", plane) for plane in range(2)]
        cover = coverage[...]
        gradient, moved = [], []
        for plane in range(2):
            folds[plane].wait_recv()
            gradient.append(own[plane] + fold_y[iteration, plane])
            moved.append(gradient[plane] / (cover + 0.5))
            direction_ext[iteration, 1, plane, middle, :] = moved[plane]
        last = iteration == ITERS - 1
        if not last:
            direct, beside = start_gather(direction_ext.at[iteration], 1 + iteration)

        squares = moved[0] * moved[0] + moved[1] * moved[1]
        sums_x[iteration, my_scan] = (
            as_row(moved[0] * gradient[0] + moved[1] * gradient[1], 0)
            + as_row(cover * squares, 1) + jnp.where(row_id == 2, live_number, 0.0)
        )
        first_sums = sum_start(sums_x, my_scan, 0, n_scan, lambda other: at(0, other), iteration)
        if not last:
            passed = pass_near(direction_ext.at[iteration], 1 + iteration, direct, beside)
        for n, (k, c) in enumerate(AROUND):
            block = jnp.zeros((8, tile), jnp.float32)
            for slot in range(slots):
                block = block + as_row(squares * shifted[n, slot], slot)
            if n == 4:
                energy_recv[iteration, n] = block
            else:
                energy_send[iteration, n] = block
                copy = remote(
                    energy_send.at[iteration, n], energy_recv.at[iteration, n],
                    energy_sem, (iteration, n), at(k, c),
                )
                copy.start()
                energy_copies.append(copy)
        for copy in first_sums:
            copy.wait()
        sums_y[iteration, my_obj] = jnp.sum(sums_x[iteration], axis=0)
        second_sums = sum_start(sums_y, my_obj, n_scan, n_obj, lambda other: at(other, 0), iteration)
        if not last:
            pass_far(direction_ext.at[iteration], 1 + iteration, passed, beside)
        for pair in sides.values():
            for copy in pair:
                copy.wait_send()
        for copy in folds + passed_on:
            copy.wait_send()
        for copy in second_sums:
            copy.wait()
        everywhere = jnp.sum(sums_y[iteration], axis=0)
        rows = jnp.sum(everywhere, axis=1, keepdims=True)
        step = rows[0:1] / rows[1:2]
        scales.append((step, rows[2:3] * (1.0 / tile) / rows[1:2]))
        if not last:
            finish_gather(direct, passed, beside)
            extended[...] = extended[...] + step.reshape(1, 1, 1, 1) * direction_ext[iteration]
        else:
            object_out[...] = (
                extended[1, :, middle, :] + step.reshape(1, 1, 1) * direction_ext[iteration, 1, :, middle, :]
            )
    for copy in energy_copies:
        copy.wait()
    for iteration in range(ITERS):
        step, scale = scales[iteration]
        steps_out[iteration] = step[0, 0]
        energy = jnp.sum(jnp.sum(energy_recv[iteration], axis=0), axis=1, keepdims=True) * scale
        for slot in range(slots):
            alive = (slot < live_ref[0]).astype(jnp.float32)
            energies_out[iteration, slot] = energy[slot, 0] * alive


def on_device(n_scan, n_obj, object_field, probe_modes, patterns, gain_map, defect_mask, probe_centres, live_counts):
    tile = object_field.shape[1]
    modes, size = probe_modes.shape[0], probe_modes.shape[1]
    slots = patterns.shape[0]
    extent = tile + size
    table = transform_tables(size)
    f32 = jnp.float32
    vmem, smem = pl.BlockSpec(memory_space=pltpu.VMEM), pl.BlockSpec(memory_space=pltpu.SMEM)
    hbm = pl.BlockSpec(memory_space=pltpu.HBM)
    flops = ITERS * slots * modes * 4 * 2 * size * (2 * size) ** 2
    outputs = pl.pallas_call(
        functools.partial(kernel, n_scan, n_obj),
        out_shape=(
            jax.ShapeDtypeStruct(object_field.shape, f32),
            jax.ShapeDtypeStruct((ITERS,), f32),
            jax.ShapeDtypeStruct((ITERS, slots), f32),
        ),
        in_specs=[hbm] * 8,
        out_specs=(vmem, smem, smem),
        scratch_shapes=[
            pltpu.VMEM(probe_modes.shape, f32),
            pltpu.VMEM(patterns.shape, patterns.dtype),
            pltpu.VMEM(gain_map.shape, f32),
            pltpu.VMEM(defect_mask.shape, jnp.int32),
            pltpu.VMEM(table.shape, table.dtype),
            pltpu.SMEM(probe_centres.shape, jnp.int32),
            pltpu.SMEM(live_counts.shape, jnp.int32),
            pltpu.SMEM((9, 128), jnp.int32),
            pltpu.VMEM((3, 2, extent, tile), f32),
            pltpu.VMEM((ITERS, 3, 2, extent, tile), f32),
            pltpu.VMEM((slots, size, size), f32),
            pltpu.VMEM((2, size + 2 * tile, tile), f32),
            pltpu.VMEM((9, slots, tile, tile), f32),
            pltpu.VMEM((tile, tile), f32),
            pltpu.VMEM((2, size, size), f32),
            pltpu.VMEM((modes, size, 2 * size), jnp.bfloat16),
            pltpu.VMEM((modes, 2 * size, size), jnp.bfloat16),
            pltpu.VMEM((modes, 2 * size, size), f32),
            pltpu.VMEM((2, size, size), f32),
            pltpu.VMEM((slots, 3, 2, size + 2 * tile, tile), f32),
            pltpu.VMEM((ITERS, 3, 2, extent, tile), f32),
            pltpu.VMEM((ITERS, 2, 2, extent, tile), f32),
            pltpu.VMEM((ITERS, 2, tile, tile), f32),
            pltpu.VMEM((ITERS, 2, tile, tile), f32),
            pltpu.VMEM((ITERS, 9, 8, tile), f32),
            pltpu.VMEM((ITERS, 9, 8, tile), f32),
            pltpu.VMEM((ITERS, n_scan, 8, tile), f32),
            pltpu.VMEM((ITERS, n_obj, 8, tile), f32),
            pltpu.SemaphoreType.DMA((8,)),
            pltpu.SemaphoreType.DMA((2, 9)),
            pltpu.SemaphoreType.DMA((2, ITERS, 16)),
            pltpu.SemaphoreType.DMA((2, ITERS, 16)),
            pltpu.SemaphoreType.DMA((2, ITERS, 9)),
            pltpu.SemaphoreType.DMA((2, ITERS, n_scan + n_obj)),
        ],
        compiler_params=pltpu.CompilerParams(
            collective_id=0, has_side_effects=True, vmem_limit_bytes=55000 * 1024
        ),
        cost_estimate=pl.CostEstimate(flops=flops, bytes_accessed=8 * 1024 * 1024, transcendentals=0),
    )(object_field, probe_modes, patterns, gain_map, defect_mask, table, probe_centres, live_counts)
    return tuple(outputs)


def solution(mesh):
    placed = (
        P(None, "obj", "scan"),
        P(),
        P(("scan", "obj"), None, None),
        P(),
        P(),
        P(("scan", "obj"), None),
        P(("scan", "obj")),
    )
    return jax.shard_map(
        functools.partial(on_device, mesh.shape["scan"], mesh.shape["obj"]),
        mesh=mesh,
        in_specs=placed,
        out_specs=(P(None, "obj", "scan"), P(), P(None, ("scan", "obj"))),
        check_vma=False,
    )
```

```python
import functools

import jax
import jax.numpy as jnp
import numpy as np
from jax import lax
from jax.experimental import pallas as pl
from jax.experimental.pallas import tpu as pltpu
from jax.sharding import PartitionSpec as P

ITERS = 2
MESH = pl.DeviceIdType.MESH
AROUND = [(k, c) for k in (-1, 0, 1) for c in (-1, 0, 1)]


def transform_tables(size):
    indices = np.arange(size, dtype=np.int32)
    phase = (indices[:, None] * indices[None, :] % size).astype(np.float32)
    angles = phase * np.float32(2.0 * 3.141592653589793 / size)
    norm = np.float32(size ** (-0.5))
    cosine, sine = np.cos(angles) * norm, np.sin(angles) * norm
    tables = []
    for first in range(2):
        c, s = cosine[: size // 2, first::2], sine[: size // 2, first::2]
        tables.append(np.block([[c, -s], [s, c]]))
    for first in range(2):
        c, s = cosine[first::2, : size // 2], sine[first::2, : size // 2]
        tables.append(np.block([[c, s], [-s, c]]))
    return jnp.asarray(np.stack(tables)).astype(jnp.bfloat16)


def kernel(
    n_scan, n_obj,
    object_hbm, probe_hbm, patterns_hbm, gain_hbm, mask_hbm, table_hbm, centres_hbm, live_hbm,
    object_out, steps_out, energies_out,
    probe_ref, patterns_ref, gain_ref, mask_ref, table_ref, centres_ref, live_ref,
    info, extended, direction_ext, amplitude, power_pad, shifted, coverage, patch, waves, stacked, far, update,
    deposit, fold, fold_x, fold_y, fold_z, energy_send, energy_recv, sums_x, sums_y,
    load_sem, info_sem, halo_sem, fold_sem, energy_sem, sums_sem,
):
    tile = object_hbm.shape[1]
    size = gain_ref.shape[0]
    modes = probe_ref.shape[0]
    slots = patterns_ref.shape[0]
    my_scan, my_obj = lax.axis_index("scan"), lax.axis_index("obj")
    top, middle, bottom = pl.ds(0, tile), pl.ds(tile, tile), pl.ds(2 * tile, tile)

    def at(k, c):
        return {
            "scan": lax.rem(my_scan + (c + n_scan), n_scan),
            "obj": lax.rem(my_obj + (k + n_obj), n_obj),
        }

    def remote(source, target, sems, index, device):
        return pltpu.make_async_remote_copy(
            src_ref=source, dst_ref=target, send_sem=sems.at[(0,) + index],
            recv_sem=sems.at[(1,) + index], device_id=device, device_id_type=MESH,
        )

    pairs = (
        (object_hbm, extended.at[1, :, middle, :]), (centres_hbm, centres_ref), (live_hbm, live_ref),
        (patterns_hbm, patterns_ref), (gain_hbm, gain_ref), (mask_hbm, mask_ref),
        (probe_hbm, probe_ref), (table_hbm, table_ref),
    )
    loads = [
        pltpu.make_async_copy(source, target, load_sem.at[n]) for n, (source, target) in enumerate(pairs)
    ]
    for load in loads:
        load.start()

    partners = [(0, c) for c in range(1, n_scan)] + [(k, 0) for k in range(1, n_obj)]
    partners += [(k, c) for k, c in AROUND if k and c]
    barrier = pltpu.get_barrier_semaphore()
    for k, c in partners:
        pl.semaphore_signal(barrier, inc=1, device_id=at(k, c), device_id_type=MESH)
    pl.semaphore_wait(barrier, len(partners))

    odd = lax.rem(my_obj, 2)
    near_start = pl.multiple_of(2 * tile * (1 - odd), tile)
    far_start = pl.multiple_of(2 * tile * odd, tile)
    near, far_rows = pl.ds(near_start, tile), pl.ds(far_start, tile)
    pair_step, pass_step = 1 - 2 * odd, 2 - 4 * odd

    def send_sideways(wide, phase, plane, rows, first):
        mine = wide.at[1, plane, rows, :]
        pair = (
            remote(mine, wide.at[0, plane, rows, :], halo_sem, (phase, first), at(0, 1)),
            remote(mine, wide.at[2, plane, rows, :], halo_sem, (phase, first + 1), at(0, -1)),
        )
        for copy in pair:
            copy.start()
        return pair

    def start_gather(wide, phase):
        direct = [
            remote(
                wide.at[1, plane, middle, :], wide.at[1, plane, far_rows, :],
                halo_sem, (phase, plane), at(pair_step, 0),
            )
            for plane in range(2)
        ]
        for copy in direct:
            copy.start()
        return direct, [send_sideways(wide, phase, plane, middle, 4 + 2 * plane) for plane in range(2)]

    def pass_near(wide, phase, direct, beside):
        passed = []
        for plane in range(2):
            direct[plane].wait_recv()
            passed.append(remote(
                wide.at[1, plane, near, :], wide.at[1, plane, far_rows, :],
                halo_sem, (phase, 2 + plane), at(pass_step, 0),
            ))
            passed[plane].start()
            beside.append(send_sideways(wide, phase, plane, near, 8 + 2 * plane))
        return passed

    def pass_far(wide, phase, passed, beside):
        for plane in range(2):
            passed[plane].wait_recv()
            beside.append(send_sideways(wide, phase, plane, far_rows, 12 + 2 * plane))

    def finish_gather(direct, passed, beside):
        for pair in beside:
            for copy in pair:
                copy.wait()
        for copy in direct + passed:
            copy.wait_send()

    loads[0].wait()
    direct, beside = start_gather(extended, 0)

    loads[1].wait()
    loads[2].wait()
    for slot in range(slots):
        info[4, 2 * slot] = centres_ref[slot, 0]
        info[4, 2 * slot + 1] = centres_ref[slot, 1]
    info[4, 2 * slots] = live_ref[0]
    info_copies = [
        remote(info.at[4], info.at[8 - n], info_sem, (n,), at(k, c))
        for n, (k, c) in enumerate(AROUND) if n != 4
    ]
    for copy in info_copies:
        copy.start()

    for load in loads[3:6]:
        load.wait()
    gain, defect = gain_ref[...], mask_ref[...] == 1
    for slot in range(slots):
        corrected = patterns_ref[slot].astype(jnp.float32) * gain
        mean = 0.25 * (
            pltpu.roll(corrected, 1, 0) + pltpu.roll(corrected, size - 1, 0)
            + pltpu.roll(corrected, 1, 1) + pltpu.roll(corrected, size - 1, 1)
        )
        amplitude[slot] = jnp.sqrt(jnp.where(defect, mean, corrected))
    loads[6].wait()
    power = jnp.zeros((size, size), jnp.float32)
    for mode in range(modes):
        power = power + probe_ref[mode, :, :size] ** 2 + probe_ref[mode, :, size:] ** 2
    power_pad[...] = jnp.zeros_like(power_pad)
    for half in range(2):
        power_pad[half, tile : tile + size, :] = power[:, half * tile : (half + 1) * tile]
    for slot in range(slots):
        for column in range(3):
            for plane in range(2):
                zeros = jnp.zeros((tile, tile), jnp.float32)
                deposit[slot, column, plane, :tile, :] = zeros
                deposit[slot, column, plane, tile + size :, :] = zeros
    passed = pass_near(extended, 0, direct, beside)
    loads[7].wait()

    place = lax.broadcasted_iota(jnp.int32, (size, size), 0)
    taken = lax.broadcasted_iota(jnp.int32, (size, size), 1)
    half_size = size // 2
    by_row = jnp.where(place < half_size, 2 * place, 2 * place - (size - 1)) == taken
    by_column = jnp.where(taken < half_size, 2 * taken, 2 * taken - (size - 1)) == place
    by_row, by_column = by_row.astype(jnp.float32), by_column.astype(jnp.float32)
    for slot in range(slots):
        ordered = jnp.dot(amplitude[slot], by_column, precision=lax.Precision.HIGHEST)
        amplitude[slot] = jnp.dot(by_row, ordered, precision=lax.Precision.HIGHEST)

    for copy in info_copies:
        copy.wait()
    pass_far(extended, 0, passed, beside)
    lane = lax.broadcasted_iota(jnp.int32, (tile, tile), 1)
    total = jnp.zeros((tile, tile), jnp.float32)
    for n, (k, c) in enumerate(AROUND):
        for slot in range(slots):
            row, column = info[n, 2 * slot], info[n, 2 * slot + 1]
            alive = (slot < info[n, 2 * slots]).astype(jnp.float32)
            rows = pl.ds(2 * tile - tile * k - row, tile)
            low, high = (pltpu.roll(power_pad[half, rows, :], column, 1) for half in range(2))
            if c == 0:
                moved = jnp.where(lane < column, low, high)
            elif c < 0:
                moved = jnp.where(lane < column, high, 0.0)
            else:
                moved = jnp.where(lane < column, 0.0, low)
            shifted[n, slot] = moved
            total = total + moved * alive
    coverage[...] = total
    finish_gather(direct, passed, beside)

    wide_lane = lax.broadcasted_iota(jnp.int32, (size, tile), 1)

    def product(left, right):
        return jnp.dot(left, right, preferred_element_type=jnp.float32)

    def take_patch(slot):
        row, column = centres_ref[slot, 0], centres_ref[slot, 1]
        back_shift = lax.rem(tile - column, tile)
        close = wide_lane < tile - column
        for plane in range(2):
            first, second, third = (
                pltpu.roll(extended[block, plane, pl.ds(row, size), :], back_shift, 1) for block in range(3)
            )
            patch[slot, plane, :, :tile] = jnp.where(close, first, second)
            patch[slot, plane, :, tile:] = jnp.where(close, second, third)

    def exit_waves(slot):
        for mode in range(modes):
            real, imag = patch[slot, 0], patch[slot, 1]
            probe_real, probe_imag = probe_ref[mode, :, :size], probe_ref[mode, :, size:]
            for part, wave in enumerate((real * probe_real - imag * probe_imag, real * probe_imag + imag * probe_real)):
                low, high = wave[:, :tile], wave[:, tile:]
                first = part * tile
                waves[slot, mode, :, first : first + tile] = (low + high).astype(jnp.bfloat16)
                waves[slot, mode, :, size + first : size + first + tile] = (low - high).astype(jnp.bfloat16)

    def along_columns(slot):
        for mode in range(modes):
            for parity in range(2):
                half = product(waves[slot, mode, :, parity * size : (parity + 1) * size], table_ref[parity])
                lanes = slice(parity * tile, (parity + 1) * tile)
                for place, value in enumerate((half[:tile] + half[tile:], half[:tile] - half[tile:])):
                    value = value.astype(jnp.bfloat16)
                    stacked[slot, mode, place * size : place * size + tile, lanes] = value[:, :tile]
                    stacked[slot, mode, place * size + tile : (place + 1) * size, lanes] = value[:, tile:]

    def along_rows(slot):
        for mode in range(modes):
            for parity in range(2):
                rows = slice(parity * size, (parity + 1) * size)
                far[slot, mode, rows, :] = product(table_ref[2 + parity], stacked[slot, mode, rows, :])

    def revise(slot):
        for parity in range(2):
            parts = [slice(parity * size + part * tile, parity * size + (part + 1) * tile) for part in range(2)]
            model = jnp.zeros((tile, size), jnp.float32)
            for mode in range(modes):
                model = model + far[slot, mode, parts[0], :] ** 2 + far[slot, mode, parts[1], :] ** 2
            ratio = amplitude[slot, parity * tile : (parity + 1) * tile, :] * lax.rsqrt(jnp.maximum(model, 0.25))
            for mode in range(modes):
                for part in parts:
                    stacked[slot, mode, part, :] = (far[slot, mode, part, :] * ratio).astype(jnp.bfloat16)

    def back_along_rows(slot):
        for mode in range(modes):
            even = product(table_ref[0], stacked[slot, mode, :size, :])
            odd = product(table_ref[1], stacked[slot, mode, size:, :])
            for rows, value in ((slice(0, tile), even + odd), (slice(tile, size), even - odd)):
                value = value.astype(jnp.bfloat16)
                for parity in range(2):
                    lanes = slice(parity * tile, (parity + 1) * tile)
                    waves[slot, mode, rows, parity * size : parity * size + tile] = value[:tile, lanes]
                    waves[slot, mode, rows, parity * size + tile : (parity + 1) * size] = value[tile:, lanes]

    def back_along_columns(slot):
        for plane in range(2):
            for half in range(2):
                lanes = slice(half * tile, (half + 1) * tile)
                update[slot, plane, :, lanes] = -power_pad[half, tile : tile + size, :] * patch[slot, plane, :, lanes]
        for mode in range(modes):
            even = product(waves[slot, mode, :, :size], table_ref[2])
            odd = product(waves[slot, mode, :, size:], table_ref[3])
            for half, wave in enumerate((even + odd, even - odd)):
                real, imag = wave[:, :tile], wave[:, tile:]
                lanes = slice(half * tile, (half + 1) * tile)
                probe_real = probe_ref[mode, :, lanes]
                probe_imag = probe_ref[mode, :, size + half * tile : size + (half + 1) * tile]
                update[slot, 0, :, lanes] += real * probe_real + imag * probe_imag
                update[slot, 1, :, lanes] += imag * probe_real - real * probe_imag

    def put_deposit(slot):
        column = centres_ref[slot, 1]
        alive = jnp.where(slot < live_ref[0], 1.0, 0.0)
        before = wide_lane < column
        for plane in range(2):
            low = pltpu.roll(update[slot, plane, :, :tile] * alive, column, 1)
            high = pltpu.roll(update[slot, plane, :, tile:] * alive, column, 1)
            deposit[slot, 0, plane, tile : tile + size, :] = jnp.where(before, 0.0, low)
            deposit[slot, 1, plane, tile : tile + size, :] = jnp.where(before, low, high)
            deposit[slot, 2, plane, tile : tile + size, :] = jnp.where(before, high, 0.0)

    stages = (
        take_patch, exit_waves, along_columns, along_rows, revise, back_along_rows, back_along_columns, put_deposit
    )

    row_id = lax.broadcasted_iota(jnp.int32, (8, tile), 0)

    def as_row(value, row):
        return jnp.where(row_id == row, jnp.sum(value, axis=0, keepdims=True), 0.0)

    live_number = live_ref[0].astype(jnp.float32)

    def sum_start(table, mine, base, count, where, iteration):
        copies = []
        for other in range(1, count):
            block = table.at[iteration, mine]
            copies.append(remote(block, block, sums_sem, (iteration, base + other), where(other)))
            copies[-1].start()
        return copies

    energy_copies, scales = [], []
    for iteration in range(ITERS):
        for stage in stages:
            for slot in range(slots):
                stage(slot)

        def gathered(column, plane, start):
            summed = None
            for slot in range(slots):
                term = deposit[slot, column, plane, pl.ds(start + tile - centres_ref[slot, 0], tile), :]
                summed = term if summed is None else summed + term
            return summed

        sides = {}
        starts = {"far": far_start, "near": near_start, "middle": tile}
        for place, (name, plane) in enumerate((name, plane) for name in starts for plane in range(2)):
            rows = pl.ds(starts[name], tile)
            pair = []
            for side, (column, step) in enumerate(((2, 1), (0, -1))):
                fold[iteration, column, plane, rows, :] = gathered(column, plane, starts[name])
                copy = remote(
                    fold.at[iteration, column, plane, rows, :], fold_x.at[iteration, side, plane, rows, :],
                    fold_sem, (iteration, 2 * place + side), at(0, step),
                )
                copy.start()
                pair.append(copy)
            sides[name, plane] = pair
        for name in starts:
            for plane in range(2):
                fold[iteration, 1, plane, pl.ds(starts[name], tile), :] = gathered(1, plane, starts[name])

        def add_sides(name, plane):
            rows = pl.ds(starts[name], tile)
            for copy in sides[name, plane]:
                copy.wait_recv()
            return (
                fold[iteration, 1, plane, rows, :]
                + fold_x[iteration, 0, plane, rows, :] + fold_x[iteration, 1, plane, rows, :]
            )

        passed_on, folds = [], []
        for plane in range(2):
            fold[iteration, 1, plane, far_rows, :] = add_sides("far", plane)
            passed_on.append(remote(
                fold.at[iteration, 1, plane, far_rows, :], fold_z.at[iteration, plane],
                fold_sem, (iteration, 12 + plane), at(-pass_step, 0),
            ))
            passed_on[plane].start()
        for plane in range(2):
            total = add_sides("near", plane)
            passed_on[plane].wait_recv()
            fold[iteration, 1, plane, near, :] = total + fold_z[iteration, plane]
            folds.append(remote(
                fold.at[iteration, 1, plane, near, :], fold_y.at[iteration, plane],
                fold_sem, (iteration, 14 + plane), at(pair_step, 0),
            ))
            folds[plane].start()
        own = [add_sides("middle", plane) for plane in range(2)]
        cover = coverage[...]
        gradient, moved = [], []
        for plane in range(2):
            folds[plane].wait_recv()
            gradient.append(own[plane] + fold_y[iteration, plane])
            moved.append(gradient[plane] / (cover + 0.5))
            direction_ext[iteration, 1, plane, middle, :] = moved[plane]
        last = iteration == ITERS - 1
        if not last:
            direct, beside = start_gather(direction_ext.at[iteration], 1 + iteration)

        squares = moved[0] * moved[0] + moved[1] * moved[1]
        sums_x[iteration, my_scan] = (
            as_row(moved[0] * gradient[0] + moved[1] * gradient[1], 0)
            + as_row(cover * squares, 1) + jnp.where(row_id == 2, live_number, 0.0)
        )
        first_sums = sum_start(sums_x, my_scan, 0, n_scan, lambda other: at(0, other), iteration)
        if not last:
            passed = pass_near(direction_ext.at[iteration], 1 + iteration, direct, beside)
        for n, (k, c) in enumerate(AROUND):
            block = jnp.zeros((8, tile), jnp.float32)
            for slot in range(slots):
                block = block + as_row(squares * shifted[n, slot], slot)
            if n == 4:
                energy_recv[iteration, n] = block
            else:
                energy_send[iteration, n] = block
                copy = remote(
                    energy_send.at[iteration, n], energy_recv.at[iteration, n],
                    energy_sem, (iteration, n), at(k, c),
                )
                copy.start()
                energy_copies.append(copy)
        for copy in first_sums:
            copy.wait()
        sums_y[iteration, my_obj] = jnp.sum(sums_x[iteration], axis=0)
        second_sums = sum_start(sums_y, my_obj, n_scan, n_obj, lambda other: at(other, 0), iteration)
        if not last:
            pass_far(direction_ext.at[iteration], 1 + iteration, passed, beside)
        for pair in sides.values():
            for copy in pair:
                copy.wait_send()
        for copy in folds + passed_on:
            copy.wait_send()
        for copy in second_sums:
            copy.wait()
        everywhere = jnp.sum(sums_y[iteration], axis=0)
        rows = jnp.sum(everywhere, axis=1, keepdims=True)
        step = rows[0:1] / rows[1:2]
        scales.append((step, rows[2:3] * (1.0 / tile) / rows[1:2]))
        if not last:
            finish_gather(direct, passed, beside)
            extended[...] = extended[...] + step.reshape(1, 1, 1, 1) * direction_ext[iteration]
        else:
            object_out[...] = (
                extended[1, :, middle, :] + step.reshape(1, 1, 1) * direction_ext[iteration, 1, :, middle, :]
            )
    for copy in energy_copies:
        copy.wait()
    for iteration in range(ITERS):
        step, scale = scales[iteration]
        steps_out[iteration] = step[0, 0]
        energy = jnp.sum(jnp.sum(energy_recv[iteration], axis=0), axis=1, keepdims=True) * scale
        for slot in range(slots):
            alive = (slot < live_ref[0]).astype(jnp.float32)
            energies_out[iteration, slot] = energy[slot, 0] * alive


def on_device(n_scan, n_obj, object_field, probe_modes, patterns, gain_map, defect_mask, probe_centres, live_counts):
    tile = object_field.shape[1]
    modes, size = probe_modes.shape[0], probe_modes.shape[1]
    slots = patterns.shape[0]
    extent = tile + size
    table = transform_tables(size)
    f32 = jnp.float32
    vmem, smem = pl.BlockSpec(memory_space=pltpu.VMEM), pl.BlockSpec(memory_space=pltpu.SMEM)
    hbm = pl.BlockSpec(memory_space=pltpu.HBM)
    flops = ITERS * slots * modes * 4 * 2 * (2 * size) * size * size
    outputs = pl.pallas_call(
        functools.partial(kernel, n_scan, n_obj),
        out_shape=(
            jax.ShapeDtypeStruct(object_field.shape, f32),
            jax.ShapeDtypeStruct((ITERS,), f32),
            jax.ShapeDtypeStruct((ITERS, slots), f32),
        ),
        in_specs=[hbm] * 8,
        out_specs=(vmem, smem, smem),
        scratch_shapes=[
            pltpu.VMEM(probe_modes.shape, f32),
            pltpu.VMEM(patterns.shape, patterns.dtype),
            pltpu.VMEM(gain_map.shape, f32),
            pltpu.VMEM(defect_mask.shape, jnp.int32),
            pltpu.VMEM(table.shape, table.dtype),
            pltpu.SMEM(probe_centres.shape, jnp.int32),
            pltpu.SMEM(live_counts.shape, jnp.int32),
            pltpu.SMEM((9, 128), jnp.int32),
            pltpu.VMEM((3, 2, extent, tile), f32),
            pltpu.VMEM((ITERS, 3, 2, extent, tile), f32),
            pltpu.VMEM((slots, size, size), f32),
            pltpu.VMEM((2, size + 2 * tile, tile), f32),
            pltpu.VMEM((9, slots, tile, tile), f32),
            pltpu.VMEM((tile, tile), f32),
            pltpu.VMEM((slots, 2, size, size), f32),
            pltpu.VMEM((slots, modes, size, 2 * size), jnp.bfloat16),
            pltpu.VMEM((slots, modes, 2 * size, size), jnp.bfloat16),
            pltpu.VMEM((slots, modes, 2 * size, size), f32),
            pltpu.VMEM((slots, 2, size, size), f32),
            pltpu.VMEM((slots, 3, 2, size + 2 * tile, tile), f32),
            pltpu.VMEM((ITERS, 3, 2, extent, tile), f32),
            pltpu.VMEM((ITERS, 2, 2, extent, tile), f32),
            pltpu.VMEM((ITERS, 2, tile, tile), f32),
            pltpu.VMEM((ITERS, 2, tile, tile), f32),
            pltpu.VMEM((ITERS, 9, 8, tile), f32),
            pltpu.VMEM((ITERS, 9, 8, tile), f32),
            pltpu.VMEM((ITERS, n_scan, 8, tile), f32),
            pltpu.VMEM((ITERS, n_obj, 8, tile), f32),
            pltpu.SemaphoreType.DMA((8,)),
            pltpu.SemaphoreType.DMA((2, 9)),
            pltpu.SemaphoreType.DMA((2, ITERS, 16)),
            pltpu.SemaphoreType.DMA((2, ITERS, 16)),
            pltpu.SemaphoreType.DMA((2, ITERS, 9)),
            pltpu.SemaphoreType.DMA((2, ITERS, n_scan + n_obj)),
        ],
        compiler_params=pltpu.CompilerParams(
            collective_id=0, has_side_effects=True, vmem_limit_bytes=55000 * 1024
        ),
        cost_estimate=pl.CostEstimate(flops=flops, bytes_accessed=8 * 1024 * 1024, transcendentals=0),
    )(object_field, probe_modes, patterns, gain_map, defect_mask, table, probe_centres, live_counts)
    return tuple(outputs)


def solution(mesh):
    placed = (
        P(None, "obj", "scan"),
        P(),
        P(("scan", "obj"), None, None),
        P(),
        P(),
        P(("scan", "obj"), None),
        P(("scan", "obj")),
    )
    return jax.shard_map(
        functools.partial(on_device, mesh.shape["scan"], mesh.shape["obj"]),
        mesh=mesh,
        in_specs=placed,
        out_specs=(P(None, "obj", "scan"), P(), P(None, ("scan", "obj"))),
        check_vma=False,
    )
```

```python
import functools

import jax
import jax.numpy as jnp
import numpy as np
from jax import lax
from jax.experimental import pallas as pl
from jax.experimental.pallas import tpu as pltpu
from jax.sharding import PartitionSpec as P

ITERS = 2
MESH = pl.DeviceIdType.MESH
AROUND = [(k, c) for k in (-1, 0, 1) for c in (-1, 0, 1)]


def transform_tables(size):
    indices = np.arange(size, dtype=np.int32)
    phase = (indices[:, None] * indices[None, :] % size).astype(np.float32)
    angles = phase * np.float32(2.0 * 3.141592653589793 / size)
    norm = np.float32(size ** (-0.5))
    cosine, sine = np.cos(angles) * norm, np.sin(angles) * norm
    tables = []
    for first in range(2):
        c, s = cosine[: size // 2, first::2], sine[: size // 2, first::2]
        tables.append(np.block([[c, -s], [s, c]]))
    for first in range(2):
        c, s = cosine[first::2, : size // 2], sine[first::2, : size // 2]
        tables.append(np.block([[c, s], [-s, c]]))
    return jnp.asarray(np.stack(tables)).astype(jnp.bfloat16)


def kernel(
    n_scan, n_obj,
    object_hbm, probe_hbm, patterns_hbm, gain_hbm, mask_hbm, table_hbm, centres_hbm, live_hbm,
    object_out, steps_out, energies_out,
    probe_ref, patterns_ref, gain_ref, mask_ref, table_ref, centres_ref, live_ref,
    info, extended, direction_ext, amplitude, power_pad, shifted, coverage, patch, waves, stacked, far, update,
    deposit, fold, fold_x, fold_y, fold_z, corner_y, corner_z, energy_send, energy_recv, sums_x, sums_y,
    load_sem, info_sem, halo_sem, fold_sem, energy_sem, sums_sem,
):
    tile = object_hbm.shape[1]
    size = gain_ref.shape[0]
    modes = probe_ref.shape[0]
    slots = patterns_ref.shape[0]
    my_scan, my_obj = lax.axis_index("scan"), lax.axis_index("obj")
    top, middle, bottom = pl.ds(0, tile), pl.ds(tile, tile), pl.ds(2 * tile, tile)

    def at(k, c):
        return {
            "scan": lax.rem(my_scan + (c + n_scan), n_scan),
            "obj": lax.rem(my_obj + (k + n_obj), n_obj),
        }

    def remote(source, target, sems, index, device):
        return pltpu.make_async_remote_copy(
            src_ref=source, dst_ref=target, send_sem=sems.at[(0,) + index],
            recv_sem=sems.at[(1,) + index], device_id=device, device_id_type=MESH,
        )

    pairs = (
        (object_hbm, extended.at[1, :, middle, :]), (centres_hbm, centres_ref), (live_hbm, live_ref),
        (patterns_hbm, patterns_ref), (gain_hbm, gain_ref), (mask_hbm, mask_ref),
        (probe_hbm, probe_ref), (table_hbm, table_ref),
    )
    loads = [
        pltpu.make_async_copy(source, target, load_sem.at[n]) for n, (source, target) in enumerate(pairs)
    ]
    for load in loads:
        load.start()

    partners = [(0, c) for c in range(1, n_scan)] + [(k, 0) for k in range(1, n_obj)]
    partners += [(k, c) for k, c in AROUND if k and c]
    barrier = pltpu.get_barrier_semaphore()
    for k, c in partners:
        pl.semaphore_signal(barrier, inc=1, device_id=at(k, c), device_id_type=MESH)
    pl.semaphore_wait(barrier, len(partners))

    odd = lax.rem(my_obj, 2)
    near_start = pl.multiple_of(2 * tile * (1 - odd), tile)
    far_start = pl.multiple_of(2 * tile * odd, tile)
    near, far_rows = pl.ds(near_start, tile), pl.ds(far_start, tile)
    pair_step, pass_step = 1 - 2 * odd, 2 - 4 * odd

    run = n_scan // 2
    turn_right, turn_left = lax.rem(my_scan, run) == run - 1, lax.rem(my_scan, run) == 0
    on_right, on_left = jnp.logical_not(turn_right), jnp.logical_not(turn_left)
    turns = ((2, 1, turn_right), (0, -1, turn_left))

    def when(condition, act):
        if condition is None:
            act()
        else:
            pl.when(condition)(act)

    class Copy:
        def __init__(self, copy, sends=None, receives=None):
            self.start = lambda: when(sends, copy.start)
            self.wait_send = lambda: when(sends, copy.wait_send)
            self.wait_recv = lambda: when(receives, copy.wait_recv)

        def wait(self):
            self.wait_recv()
            self.wait_send()

    def send_sideways(wide, phase, plane, rows, first, corner):
        mine = wide.at[1, plane, rows, :]
        pair = (
            Copy(
                remote(mine, wide.at[0, plane, rows, :], halo_sem, (phase, first), at(0, 1)),
                *((on_right, on_left) if corner else ()),
            ),
            Copy(
                remote(mine, wide.at[2, plane, rows, :], halo_sem, (phase, first + 1), at(0, -1)),
                *((on_left, on_right) if corner else ()),
            ),
        )
        for copy in pair:
            copy.start()
        return pair

    def start_gather(wide, phase):
        direct, corners = [], []
        for plane in range(2):
            mine = wide.at[1, plane, middle, :]
            direct.append(remote(
                mine, wide.at[1, plane, far_rows, :], halo_sem, (phase, plane), at(pair_step, 0)
            ))
            direct[plane].start()
            corners.append([
                Copy(
                    remote(
                        mine, wide.at[2 - column, plane, far_rows, :],
                        halo_sem, (phase, 16 + 2 * plane + side), at(pair_step, step),
                    ),
                    turn, turns[1 - side][2],
                )
                for side, (column, step, turn) in enumerate(turns)
            ])
            for copy in corners[plane]:
                copy.start()
        beside = [send_sideways(wide, phase, plane, middle, 4 + 2 * plane, False) for plane in range(2)]
        return direct, corners, beside

    def pass_near(wide, phase, state):
        direct, corners, beside = state
        passed = []
        for plane in range(2):
            direct[plane].wait_recv()
            passed.append(Copy(remote(
                wide.at[1, plane, near, :], wide.at[1, plane, far_rows, :],
                halo_sem, (phase, 2 + plane), at(pass_step, 0),
            )))
            passed[-1].start()
            beside.append(send_sideways(wide, phase, plane, near, 8 + 2 * plane, True))
        for plane in range(2):
            for side, (column, step, turn) in enumerate(turns):
                corners[plane][1 - side].wait_recv()
                passed.append(Copy(
                    remote(
                        wide.at[column, plane, near, :], wide.at[column, plane, far_rows, :],
                        halo_sem, (phase, 20 + 2 * plane + side), at(pass_step, 0),
                    ),
                    turn, turn,
                ))
                passed[-1].start()
        return passed

    def pass_far(wide, phase, state, passed):
        for plane in range(2):
            passed[plane].wait_recv()
            state[2].append(send_sideways(wide, phase, plane, far_rows, 12 + 2 * plane, True))

    def finish_gather(state, passed):
        direct, corners, beside = state
        for pair in beside:
            for copy in pair:
                copy.wait()
        for copy in passed[2:]:
            copy.wait_recv()
        for copy in direct + passed + corners[0] + corners[1]:
            copy.wait_send()

    loads[0].wait()
    state = start_gather(extended, 0)

    loads[1].wait()
    loads[2].wait()
    for slot in range(slots):
        info[4, 2 * slot] = centres_ref[slot, 0]
        info[4, 2 * slot + 1] = centres_ref[slot, 1]
    info[4, 2 * slots] = live_ref[0]
    info_copies = [
        remote(info.at[4], info.at[8 - n], info_sem, (n,), at(k, c))
        for n, (k, c) in enumerate(AROUND) if n != 4
    ]
    for copy in info_copies:
        copy.start()

    for load in loads[3:6]:
        load.wait()
    gain, defect = gain_ref[...], mask_ref[...] == 1
    for slot in range(slots):
        corrected = patterns_ref[slot].astype(jnp.float32) * gain
        mean = 0.25 * (
            pltpu.roll(corrected, 1, 0) + pltpu.roll(corrected, size - 1, 0)
            + pltpu.roll(corrected, 1, 1) + pltpu.roll(corrected, size - 1, 1)
        )
        amplitude[slot] = jnp.sqrt(jnp.where(defect, mean, corrected))
    loads[6].wait()
    power = jnp.zeros((size, size), jnp.float32)
    for mode in range(modes):
        power = power + probe_ref[mode, :, :size] ** 2 + probe_ref[mode, :, size:] ** 2
    power_pad[...] = jnp.zeros_like(power_pad)
    for half in range(2):
        power_pad[half, tile : tile + size, :] = power[:, half * tile : (half + 1) * tile]
    for slot in range(slots):
        for column in range(3):
            for plane in range(2):
                zeros = jnp.zeros((tile, tile), jnp.float32)
                deposit[slot, column, plane, :tile, :] = zeros
                deposit[slot, column, plane, tile + size :, :] = zeros
    passed = pass_near(extended, 0, state)
    loads[7].wait()

    place = lax.broadcasted_iota(jnp.int32, (size, size), 0)
    taken = lax.broadcasted_iota(jnp.int32, (size, size), 1)
    half_size = size // 2
    by_row = jnp.where(place < half_size, 2 * place, 2 * place - (size - 1)) == taken
    by_column = jnp.where(taken < half_size, 2 * taken, 2 * taken - (size - 1)) == place
    by_row, by_column = by_row.astype(jnp.float32), by_column.astype(jnp.float32)
    for slot in range(slots):
        ordered = jnp.dot(amplitude[slot], by_column, precision=lax.Precision.HIGHEST)
        amplitude[slot] = jnp.dot(by_row, ordered, precision=lax.Precision.HIGHEST)

    for copy in info_copies:
        copy.wait()
    pass_far(extended, 0, state, passed)
    lane = lax.broadcasted_iota(jnp.int32, (tile, tile), 1)
    total = jnp.zeros((tile, tile), jnp.float32)
    for n, (k, c) in enumerate(AROUND):
        for slot in range(slots):
            row, column = info[n, 2 * slot], info[n, 2 * slot + 1]
            alive = (slot < info[n, 2 * slots]).astype(jnp.float32)
            rows = pl.ds(2 * tile - tile * k - row, tile)
            low, high = (pltpu.roll(power_pad[half, rows, :], column, 1) for half in range(2))
            if c == 0:
                moved = jnp.where(lane < column, low, high)
            elif c < 0:
                moved = jnp.where(lane < column, high, 0.0)
            else:
                moved = jnp.where(lane < column, 0.0, low)
            shifted[n, slot] = moved
            total = total + moved * alive
    coverage[...] = total
    finish_gather(state, passed)

    wide_lane = lax.broadcasted_iota(jnp.int32, (size, tile), 1)

    def product(left, right):
        return jnp.dot(left, right, preferred_element_type=jnp.float32)

    def take_patch(slot):
        row, column = centres_ref[slot, 0], centres_ref[slot, 1]
        back_shift = lax.rem(tile - column, tile)
        close = wide_lane < tile - column
        for plane in range(2):
            first, second, third = (
                pltpu.roll(extended[block, plane, pl.ds(row, size), :], back_shift, 1) for block in range(3)
            )
            patch[slot, plane, :, :tile] = jnp.where(close, first, second)
            patch[slot, plane, :, tile:] = jnp.where(close, second, third)

    def exit_waves(slot):
        for mode in range(modes):
            real, imag = patch[slot, 0], patch[slot, 1]
            probe_real, probe_imag = probe_ref[mode, :, :size], probe_ref[mode, :, size:]
            for part, wave in enumerate((real * probe_real - imag * probe_imag, real * probe_imag + imag * probe_real)):
                low, high = wave[:, :tile], wave[:, tile:]
                first = part * tile
                waves[slot, mode, :, first : first + tile] = (low + high).astype(jnp.bfloat16)
                waves[slot, mode, :, size + first : size + first + tile] = (low - high).astype(jnp.bfloat16)

    def along_columns(slot):
        for mode in range(modes):
            for parity in range(2):
                half = product(waves[slot, mode, :, parity * size : (parity + 1) * size], table_ref[parity])
                lanes = slice(parity * tile, (parity + 1) * tile)
                for place, value in enumerate((half[:tile] + half[tile:], half[:tile] - half[tile:])):
                    value = value.astype(jnp.bfloat16)
                    stacked[slot, mode, place * size : place * size + tile, lanes] = value[:, :tile]
                    stacked[slot, mode, place * size + tile : (place + 1) * size, lanes] = value[:, tile:]

    def along_rows(slot):
        for mode in range(modes):
            for parity in range(2):
                rows = slice(parity * size, (parity + 1) * size)
                far[slot, mode, rows, :] = product(table_ref[2 + parity], stacked[slot, mode, rows, :])

    def revise(slot):
        for parity in range(2):
            parts = [slice(parity * size + part * tile, parity * size + (part + 1) * tile) for part in range(2)]
            model = jnp.zeros((tile, size), jnp.float32)
            for mode in range(modes):
                model = model + far[slot, mode, parts[0], :] ** 2 + far[slot, mode, parts[1], :] ** 2
            ratio = amplitude[slot, parity * tile : (parity + 1) * tile, :] * lax.rsqrt(jnp.maximum(model, 0.25))
            for mode in range(modes):
                for part in parts:
                    stacked[slot, mode, part, :] = (far[slot, mode, part, :] * ratio).astype(jnp.bfloat16)

    def back_along_rows(slot):
        for mode in range(modes):
            even = product(table_ref[0], stacked[slot, mode, :size, :])
            odd = product(table_ref[1], stacked[slot, mode, size:, :])
            for rows, value in ((slice(0, tile), even + odd), (slice(tile, size), even - odd)):
                value = value.astype(jnp.bfloat16)
                for parity in range(2):
                    lanes = slice(parity * tile, (parity + 1) * tile)
                    waves[slot, mode, rows, parity * size : parity * size + tile] = value[:tile, lanes]
                    waves[slot, mode, rows, parity * size + tile : (parity + 1) * size] = value[tile:, lanes]

    def back_along_columns(slot):
        for plane in range(2):
            for half in range(2):
                lanes = slice(half * tile, (half + 1) * tile)
                update[slot, plane, :, lanes] = -power_pad[half, tile : tile + size, :] * patch[slot, plane, :, lanes]
        for mode in range(modes):
            even = product(waves[slot, mode, :, :size], table_ref[2])
            odd = product(waves[slot, mode, :, size:], table_ref[3])
            for half, wave in enumerate((even + odd, even - odd)):
                real, imag = wave[:, :tile], wave[:, tile:]
                lanes = slice(half * tile, (half + 1) * tile)
                probe_real = probe_ref[mode, :, lanes]
                probe_imag = probe_ref[mode, :, size + half * tile : size + (half + 1) * tile]
                update[slot, 0, :, lanes] += real * probe_real + imag * probe_imag
                update[slot, 1, :, lanes] += imag * probe_real - real * probe_imag

    def put_deposit(slot):
        column = centres_ref[slot, 1]
        alive = jnp.where(slot < live_ref[0], 1.0, 0.0)
        before = wide_lane < column
        for plane in range(2):
            low = pltpu.roll(update[slot, plane, :, :tile] * alive, column, 1)
            high = pltpu.roll(update[slot, plane, :, tile:] * alive, column, 1)
            deposit[slot, 0, plane, tile : tile + size, :] = jnp.where(before, 0.0, low)
            deposit[slot, 1, plane, tile : tile + size, :] = jnp.where(before, low, high)
            deposit[slot, 2, plane, tile : tile + size, :] = jnp.where(before, high, 0.0)

    stages = (
        take_patch, exit_waves, along_columns, along_rows, revise, back_along_rows, back_along_columns, put_deposit
    )

    row_id = lax.broadcasted_iota(jnp.int32, (8, tile), 0)

    def as_row(value, row):
        return jnp.where(row_id == row, jnp.sum(value, axis=0, keepdims=True), 0.0)

    live_number = live_ref[0].astype(jnp.float32)

    def sum_start(table, mine, base, count, where, iteration):
        copies = []
        for other in range(1, count):
            block = table.at[iteration, mine]
            copies.append(remote(block, block, sums_sem, (iteration, base + other), where(other)))
            copies[-1].start()
        return copies

    energy_copies, scales = [], []
    for iteration in range(ITERS):
        for stage in stages:
            for slot in range(slots):
                stage(slot)

        def gathered(column, plane, start):
            summed = None
            for slot in range(slots):
                term = deposit[slot, column, plane, pl.ds(start + tile - centres_ref[slot, 0], tile), :]
                summed = term if summed is None else summed + term
            return summed

        sides, corners = {}, []
        starts = {"far": far_start, "near": near_start, "middle": tile}
        for place, (name, plane) in enumerate((name, plane) for name in starts for plane in range(2)):
            rows = pl.ds(starts[name], tile)
            pair = []
            for side, (column, step, turn) in enumerate(turns):
                fold[iteration, column, plane, rows, :] = gathered(column, plane, starts[name])
                if name == "far":
                    corners.append(Copy(
                        remote(
                            fold.at[iteration, column, plane, rows, :], corner_z.at[iteration, side, plane],
                            fold_sem, (iteration, 16 + 2 * plane + side), at(-pass_step, 0),
                        ),
                        turn, turn,
                    ))
                    corners[-1].start()
                copy = Copy(
                    remote(
                        fold.at[iteration, column, plane, rows, :], fold_x.at[iteration, side, plane, rows, :],
                        fold_sem, (iteration, 2 * place + side), at(0, step),
                    ),
                    *(() if name == "middle" else ((on_right, on_left), (on_left, on_right))[side]),
                )
                copy.start()
                pair.append(copy)
            sides[name, plane] = pair
        for name in starts:
            for plane in range(2):
                fold[iteration, 1, plane, pl.ds(starts[name], tile), :] = gathered(1, plane, starts[name])

        def add_sides(name, plane):
            rows = pl.ds(starts[name], tile)
            for side, copy in enumerate(sides[name, plane]):
                def add(side=side):
                    fold[iteration, 1, plane, rows, :] += fold_x[iteration, side, plane, rows, :]

                copy.wait_recv()
                when(None if name == "middle" else (on_left, on_right)[side], add)

        passed_on, folds, straight = [], [], []
        for plane in range(2):
            add_sides("far", plane)
            passed_on.append(remote(
                fold.at[iteration, 1, plane, far_rows, :], fold_z.at[iteration, plane],
                fold_sem, (iteration, 12 + plane), at(-pass_step, 0),
            ))
            passed_on[plane].start()
        for plane in range(2):
            for side, (column, step, turn) in enumerate(turns):
                def add_corner(plane=plane, side=side, column=column):
                    fold[iteration, column, plane, near, :] += corner_z[iteration, side, plane]

                corners[2 * plane + side].wait_recv()
                when(turn, add_corner)
                straight.append(Copy(
                    remote(
                        fold.at[iteration, column, plane, near, :], corner_y.at[iteration, side, plane],
                        fold_sem, (iteration, 20 + 2 * plane + side), at(pair_step, step),
                    ),
                    turn, turns[1 - side][2],
                ))
                straight[-1].start()
        for plane in range(2):
            add_sides("near", plane)
            passed_on[plane].wait_recv()
            fold[iteration, 1, plane, near, :] += fold_z[iteration, plane]
            folds.append(remote(
                fold.at[iteration, 1, plane, near, :], fold_y.at[iteration, plane],
                fold_sem, (iteration, 14 + plane), at(pair_step, 0),
            ))
            folds[plane].start()
        for plane in range(2):
            add_sides("middle", plane)
        for plane in range(2):
            for side in range(2):
                def add_straight(plane=plane, side=side):
                    fold[iteration, 1, plane, middle, :] += corner_y[iteration, side, plane]

                straight[2 * plane + side].wait_recv()
                when(turns[1 - side][2], add_straight)
        cover = coverage[...]
        gradient, moved = [], []
        for plane in range(2):
            folds[plane].wait_recv()
            gradient.append(fold[iteration, 1, plane, middle, :] + fold_y[iteration, plane])
            moved.append(gradient[plane] / (cover + 0.5))
            direction_ext[iteration, 1, plane, middle, :] = moved[plane]
        last = iteration == ITERS - 1
        if not last:
            state = start_gather(direction_ext.at[iteration], 1 + iteration)

        squares = moved[0] * moved[0] + moved[1] * moved[1]
        sums_x[iteration, my_scan] = (
            as_row(moved[0] * gradient[0] + moved[1] * gradient[1], 0)
            + as_row(cover * squares, 1) + jnp.where(row_id == 2, live_number, 0.0)
        )
        first_sums = sum_start(sums_x, my_scan, 0, n_scan, lambda other: at(0, other), iteration)
        if not last:
            passed = pass_near(direction_ext.at[iteration], 1 + iteration, state)
        for n, (k, c) in enumerate(AROUND):
            block = jnp.zeros((8, tile), jnp.float32)
            for slot in range(slots):
                block = block + as_row(squares * shifted[n, slot], slot)
            if n == 4:
                energy_recv[iteration, n] = block
            else:
                energy_send[iteration, n] = block
                copy = remote(
                    energy_send.at[iteration, n], energy_recv.at[iteration, n],
                    energy_sem, (iteration, n), at(k, c),
                )
                copy.start()
                energy_copies.append(copy)
        for copy in first_sums:
            copy.wait()
        sums_y[iteration, my_obj] = jnp.sum(sums_x[iteration], axis=0)
        second_sums = sum_start(sums_y, my_obj, n_scan, n_obj, lambda other: at(other, 0), iteration)
        if not last:
            pass_far(direction_ext.at[iteration], 1 + iteration, state, passed)
        for pair in sides.values():
            for copy in pair:
                copy.wait_send()
        for copy in folds + passed_on + corners + straight:
            copy.wait_send()
        for copy in second_sums:
            copy.wait()
        everywhere = jnp.sum(sums_y[iteration], axis=0)
        rows = jnp.sum(everywhere, axis=1, keepdims=True)
        step = rows[0:1] / rows[1:2]
        scales.append((step, rows[2:3] * (1.0 / tile) / rows[1:2]))
        if not last:
            finish_gather(state, passed)
            extended[...] = extended[...] + step.reshape(1, 1, 1, 1) * direction_ext[iteration]
        else:
            object_out[...] = (
                extended[1, :, middle, :] + step.reshape(1, 1, 1) * direction_ext[iteration, 1, :, middle, :]
            )
    for copy in energy_copies:
        copy.wait()
    for iteration in range(ITERS):
        step, scale = scales[iteration]
        steps_out[iteration] = step[0, 0]
        energy = jnp.sum(jnp.sum(energy_recv[iteration], axis=0), axis=1, keepdims=True) * scale
        for slot in range(slots):
            alive = (slot < live_ref[0]).astype(jnp.float32)
            energies_out[iteration, slot] = energy[slot, 0] * alive


def on_device(n_scan, n_obj, object_field, probe_modes, patterns, gain_map, defect_mask, probe_centres, live_counts):
    tile = object_field.shape[1]
    modes, size = probe_modes.shape[0], probe_modes.shape[1]
    slots = patterns.shape[0]
    extent = tile + size
    table = transform_tables(size)
    f32 = jnp.float32
    vmem, smem = pl.BlockSpec(memory_space=pltpu.VMEM), pl.BlockSpec(memory_space=pltpu.SMEM)
    hbm = pl.BlockSpec(memory_space=pltpu.HBM)
    flops = ITERS * slots * modes * 4 * 2 * (2 * size) * size * size
    outputs = pl.pallas_call(
        functools.partial(kernel, n_scan, n_obj),
        out_shape=(
            jax.ShapeDtypeStruct(object_field.shape, f32),
            jax.ShapeDtypeStruct((ITERS,), f32),
            jax.ShapeDtypeStruct((ITERS, slots), f32),
        ),
        in_specs=[hbm] * 8,
        out_specs=(vmem, smem, smem),
        scratch_shapes=[
            pltpu.VMEM(probe_modes.shape, f32),
            pltpu.VMEM(patterns.shape, patterns.dtype),
            pltpu.VMEM(gain_map.shape, f32),
            pltpu.VMEM(defect_mask.shape, jnp.int32),
            pltpu.VMEM(table.shape, table.dtype),
            pltpu.SMEM(probe_centres.shape, jnp.int32),
            pltpu.SMEM(live_counts.shape, jnp.int32),
            pltpu.SMEM((9, 128), jnp.int32),
            pltpu.VMEM((3, 2, extent, tile), f32),
            pltpu.VMEM((ITERS, 3, 2, extent, tile), f32),
            pltpu.VMEM((slots, size, size), f32),
            pltpu.VMEM((2, size + 2 * tile, tile), f32),
            pltpu.VMEM((9, slots, tile, tile), f32),
            pltpu.VMEM((tile, tile), f32),
            pltpu.VMEM((slots, 2, size, size), f32),
            pltpu.VMEM((slots, modes, size, 2 * size), jnp.bfloat16),
            pltpu.VMEM((slots, modes, 2 * size, size), jnp.bfloat16),
            pltpu.VMEM((slots, modes, 2 * size, size), f32),
            pltpu.VMEM((slots, 2, size, size), f32),
            pltpu.VMEM((slots, 3, 2, size + 2 * tile, tile), f32),
            pltpu.VMEM((ITERS, 3, 2, extent, tile), f32),
            pltpu.VMEM((ITERS, 2, 2, extent, tile), f32),
            pltpu.VMEM((ITERS, 2, tile, tile), f32),
            pltpu.VMEM((ITERS, 2, tile, tile), f32),
            pltpu.VMEM((ITERS, 2, 2, tile, tile), f32),
            pltpu.VMEM((ITERS, 2, 2, tile, tile), f32),
            pltpu.VMEM((ITERS, 9, 8, tile), f32),
            pltpu.VMEM((ITERS, 9, 8, tile), f32),
            pltpu.VMEM((ITERS, n_scan, 8, tile), f32),
            pltpu.VMEM((ITERS, n_obj, 8, tile), f32),
            pltpu.SemaphoreType.DMA((8,)),
            pltpu.SemaphoreType.DMA((2, 9)),
            pltpu.SemaphoreType.DMA((2, ITERS, 24)),
            pltpu.SemaphoreType.DMA((2, ITERS, 24)),
            pltpu.SemaphoreType.DMA((2, ITERS, 9)),
            pltpu.SemaphoreType.DMA((2, ITERS, n_scan + n_obj)),
        ],
        compiler_params=pltpu.CompilerParams(
            collective_id=0, has_side_effects=True, vmem_limit_bytes=55000 * 1024
        ),
        cost_estimate=pl.CostEstimate(flops=flops, bytes_accessed=8 * 1024 * 1024, transcendentals=0),
    )(object_field, probe_modes, patterns, gain_map, defect_mask, table, probe_centres, live_counts)
    return tuple(outputs)


def solution(mesh):
    placed = (
        P(None, "obj", "scan"),
        P(),
        P(("scan", "obj"), None, None),
        P(),
        P(),
        P(("scan", "obj"), None),
        P(("scan", "obj")),
    )
    return jax.shard_map(
        functools.partial(on_device, mesh.shape["scan"], mesh.shape["obj"]),
        mesh=mesh,
        in_specs=placed,
        out_specs=(P(None, "obj", "scan"), P(), P(None, ("scan", "obj"))),
        check_vma=False,
    )
```

```python
import functools

import jax
import jax.numpy as jnp
import numpy as np
from jax import lax
from jax.experimental import pallas as pl
from jax.experimental.pallas import tpu as pltpu
from jax.sharding import PartitionSpec as P

ITERS = 2
PARTS = 2
MESH = pl.DeviceIdType.MESH
AROUND = [(k, c) for k in (-1, 0, 1) for c in (-1, 0, 1)]


def transform_tables(size):
    indices = np.arange(size, dtype=np.int32)
    phase = (indices[:, None] * indices[None, :] % size).astype(np.float32)
    angles = phase * np.float32(2.0 * 3.141592653589793 / size)
    norm = np.float32(size ** (-0.5))
    cosine, sine = np.cos(angles) * norm, np.sin(angles) * norm
    tables = []
    for first in range(2):
        c, s = cosine[: size // 2, first::2], sine[: size // 2, first::2]
        tables.append(np.block([[c, -s], [s, c]]))
    for first in range(2):
        c, s = cosine[first::2, : size // 2], sine[first::2, : size // 2]
        tables.append(np.block([[c, s], [-s, c]]))
    return jnp.asarray(np.stack(tables)).astype(jnp.bfloat16)


def kernel(
    n_scan, n_obj,
    object_hbm, probe_hbm, patterns_hbm, gain_hbm, mask_hbm, table_hbm, centres_hbm, live_hbm,
    object_out, steps_out, energies_out,
    probe_ref, patterns_ref, gain_ref, mask_ref, table_ref, centres_ref, live_ref,
    info, extended, direction_ext, amplitude, power_pad, shifted, coverage, patch, waves, stacked, far, update,
    deposit, fold, fold_x, fold_y, fold_z, corner_y, corner_z, energy_send, energy_recv, sums_x, sums_y,
    load_sem, info_sem, halo_sem, fold_sem, energy_sem, sums_sem,
):
    tile = object_hbm.shape[1]
    size = gain_ref.shape[0]
    modes = probe_ref.shape[0]
    slots = patterns_ref.shape[0]
    my_scan, my_obj = lax.axis_index("scan"), lax.axis_index("obj")
    top, middle, bottom = pl.ds(0, tile), pl.ds(tile, tile), pl.ds(2 * tile, tile)

    def at(k, c):
        return {
            "scan": lax.rem(my_scan + (c + n_scan), n_scan),
            "obj": lax.rem(my_obj + (k + n_obj), n_obj),
        }

    def remote(source, target, sems, index, device):
        return pltpu.make_async_remote_copy(
            src_ref=source, dst_ref=target, send_sem=sems.at[(0,) + index],
            recv_sem=sems.at[(1,) + index], device_id=device, device_id_type=MESH,
        )

    pairs = (
        (object_hbm, extended.at[1, :, middle, :]), (centres_hbm, centres_ref), (live_hbm, live_ref),
        (patterns_hbm, patterns_ref), (gain_hbm, gain_ref), (mask_hbm, mask_ref),
        (probe_hbm, probe_ref), (table_hbm, table_ref),
    )
    loads = [
        pltpu.make_async_copy(source, target, load_sem.at[n]) for n, (source, target) in enumerate(pairs)
    ]
    for load in loads:
        load.start()

    partners = [(0, c) for c in range(1, n_scan)] + [(k, 0) for k in range(1, n_obj)]
    partners += [(k, c) for k, c in AROUND if k and c]
    barrier = pltpu.get_barrier_semaphore()
    for k, c in partners:
        pl.semaphore_signal(barrier, inc=1, device_id=at(k, c), device_id_type=MESH)
    pl.semaphore_wait(barrier, len(partners))

    odd = lax.rem(my_obj, 2)
    near_start = pl.multiple_of(2 * tile * (1 - odd), tile)
    far_start = pl.multiple_of(2 * tile * odd, tile)
    near, far_rows = pl.ds(near_start, tile), pl.ds(far_start, tile)
    pair_step, pass_step = 1 - 2 * odd, 2 - 4 * odd

    run = n_scan // 2
    turn_right, turn_left = lax.rem(my_scan, run) == run - 1, lax.rem(my_scan, run) == 0
    on_right, on_left = jnp.logical_not(turn_right), jnp.logical_not(turn_left)
    turns = ((2, 1, turn_right), (0, -1, turn_left))

    def when(condition, act):
        if condition is None:
            act()
        else:
            pl.when(condition)(act)

    class Copy:
        def __init__(self, copy, sends=None, receives=None):
            self.start = lambda: when(sends, copy.start)
            self.wait_send = lambda: when(sends, copy.wait_send)
            self.wait_recv = lambda: when(receives, copy.wait_recv)

        def wait(self):
            self.wait_recv()
            self.wait_send()

    def send_sideways(wide, phase, plane, rows, first, corner):
        mine = wide.at[1, plane, rows, :]
        pair = (
            Copy(
                remote(mine, wide.at[0, plane, rows, :], halo_sem, (phase, first), at(0, 1)),
                *((on_right, on_left) if corner else ()),
            ),
            Copy(
                remote(mine, wide.at[2, plane, rows, :], halo_sem, (phase, first + 1), at(0, -1)),
                *((on_left, on_right) if corner else ()),
            ),
        )
        for copy in pair:
            copy.start()
        return pair

    depth = tile // PARTS
    pieces = [(plane, part) for plane in range(2) for part in range(PARTS)]
    count = len(pieces)

    def piece_rows(start, part):
        return pl.ds(pl.multiple_of(start + part * depth, depth), depth)

    def start_gather(wide, phase):
        direct, corners = [], []
        for n, (plane, part) in enumerate(pieces):
            mine = wide.at[1, plane, piece_rows(tile, part), :]
            there = piece_rows(far_start, part)
            direct.append(remote(mine, wide.at[1, plane, there, :], halo_sem, (phase, n), at(pair_step, 0)))
            direct[n].start()
            corners.append([
                Copy(
                    remote(
                        mine, wide.at[2 - column, plane, there, :],
                        halo_sem, (phase, 8 * count + 2 * n + side), at(pair_step, step),
                    ),
                    turn, turns[1 - side][2],
                )
                for side, (column, step, turn) in enumerate(turns)
            ])
            for copy in corners[n]:
                copy.start()
        beside = [send_sideways(wide, phase, plane, middle, 2 * count + 2 * plane, False) for plane in range(2)]
        return direct, corners, beside

    def pass_near(wide, phase, state):
        direct, corners, beside = state
        passed = []
        for n, (plane, part) in enumerate(pieces):
            here, there = piece_rows(near_start, part), piece_rows(far_start, part)
            direct[n].wait_recv()
            passed.append(Copy(remote(
                wide.at[1, plane, here, :], wide.at[1, plane, there, :],
                halo_sem, (phase, count + n), at(pass_step, 0),
            )))
            passed[-1].start()
            beside.append(send_sideways(wide, phase, plane, here, 4 * count + 2 * n, True))
        for n, (plane, part) in enumerate(pieces):
            here, there = piece_rows(near_start, part), piece_rows(far_start, part)
            for side, (column, step, turn) in enumerate(turns):
                corners[n][1 - side].wait_recv()
                passed.append(Copy(
                    remote(
                        wide.at[column, plane, here, :], wide.at[column, plane, there, :],
                        halo_sem, (phase, 10 * count + 2 * n + side), at(pass_step, 0),
                    ),
                    turn, turn,
                ))
                passed[-1].start()
        return passed

    def pass_far(wide, phase, state, passed):
        for n, (plane, part) in enumerate(pieces):
            passed[n].wait_recv()
            state[2].append(send_sideways(wide, phase, plane, piece_rows(far_start, part), 6 * count + 2 * n, True))

    def finish_gather(state, passed):
        direct, corners, beside = state
        for pair in beside:
            for copy in pair:
                copy.wait()
        for copy in passed[count:]:
            copy.wait_recv()
        for copy in direct + passed + [copy for pair in corners for copy in pair]:
            copy.wait_send()

    loads[0].wait()
    state = start_gather(extended, 0)

    loads[1].wait()
    loads[2].wait()
    for slot in range(slots):
        info[4, 2 * slot] = centres_ref[slot, 0]
        info[4, 2 * slot + 1] = centres_ref[slot, 1]
    info[4, 2 * slots] = live_ref[0]
    info_copies = [
        remote(info.at[4], info.at[8 - n], info_sem, (n,), at(k, c))
        for n, (k, c) in enumerate(AROUND) if n != 4
    ]
    for copy in info_copies:
        copy.start()

    for load in loads[3:6]:
        load.wait()
    gain, defect = gain_ref[...], mask_ref[...] == 1
    for slot in range(slots):
        corrected = patterns_ref[slot].astype(jnp.float32) * gain
        mean = 0.25 * (
            pltpu.roll(corrected, 1, 0) + pltpu.roll(corrected, size - 1, 0)
            + pltpu.roll(corrected, 1, 1) + pltpu.roll(corrected, size - 1, 1)
        )
        amplitude[slot] = jnp.sqrt(jnp.where(defect, mean, corrected))
    loads[6].wait()
    power = jnp.zeros((size, size), jnp.float32)
    for mode in range(modes):
        power = power + probe_ref[mode, :, :size] ** 2 + probe_ref[mode, :, size:] ** 2
    power_pad[...] = jnp.zeros_like(power_pad)
    for half in range(2):
        power_pad[half, tile : tile + size, :] = power[:, half * tile : (half + 1) * tile]
    for slot in range(slots):
        for column in range(3):
            for plane in range(2):
                zeros = jnp.zeros((tile, tile), jnp.float32)
                deposit[slot, column, plane, :tile, :] = zeros
                deposit[slot, column, plane, tile + size :, :] = zeros
    passed = pass_near(extended, 0, state)
    loads[7].wait()

    place = lax.broadcasted_iota(jnp.int32, (size, size), 0)
    taken = lax.broadcasted_iota(jnp.int32, (size, size), 1)
    half_size = size // 2
    by_row = jnp.where(place < half_size, 2 * place, 2 * place - (size - 1)) == taken
    by_column = jnp.where(taken < half_size, 2 * taken, 2 * taken - (size - 1)) == place
    by_row, by_column = by_row.astype(jnp.float32), by_column.astype(jnp.float32)
    for slot in range(slots):
        ordered = jnp.dot(amplitude[slot], by_column, precision=lax.Precision.HIGHEST)
        amplitude[slot] = jnp.dot(by_row, ordered, precision=lax.Precision.HIGHEST)

    for copy in info_copies:
        copy.wait()
    pass_far(extended, 0, state, passed)
    lane = lax.broadcasted_iota(jnp.int32, (tile, tile), 1)
    total = jnp.zeros((tile, tile), jnp.float32)
    for n, (k, c) in enumerate(AROUND):
        for slot in range(slots):
            row, column = info[n, 2 * slot], info[n, 2 * slot + 1]
            alive = (slot < info[n, 2 * slots]).astype(jnp.float32)
            rows = pl.ds(2 * tile - tile * k - row, tile)
            low, high = (pltpu.roll(power_pad[half, rows, :], column, 1) for half in range(2))
            if c == 0:
                moved = jnp.where(lane < column, low, high)
            elif c < 0:
                moved = jnp.where(lane < column, high, 0.0)
            else:
                moved = jnp.where(lane < column, 0.0, low)
            shifted[n, slot] = moved
            total = total + moved * alive
    coverage[...] = total
    finish_gather(state, passed)

    wide_lane = lax.broadcasted_iota(jnp.int32, (size, tile), 1)

    def product(left, right):
        return jnp.dot(left, right, preferred_element_type=jnp.float32)

    def take_patch(slot):
        row, column = centres_ref[slot, 0], centres_ref[slot, 1]
        back_shift = lax.rem(tile - column, tile)
        close = wide_lane < tile - column
        for plane in range(2):
            first, second, third = (
                pltpu.roll(extended[block, plane, pl.ds(row, size), :], back_shift, 1) for block in range(3)
            )
            patch[slot, plane, :, :tile] = jnp.where(close, first, second)
            patch[slot, plane, :, tile:] = jnp.where(close, second, third)

    def exit_waves(slot):
        for mode in range(modes):
            real, imag = patch[slot, 0], patch[slot, 1]
            probe_real, probe_imag = probe_ref[mode, :, :size], probe_ref[mode, :, size:]
            for part, wave in enumerate((real * probe_real - imag * probe_imag, real * probe_imag + imag * probe_real)):
                low, high = wave[:, :tile], wave[:, tile:]
                first = part * tile
                waves[slot, mode, :, first : first + tile] = (low + high).astype(jnp.bfloat16)
                waves[slot, mode, :, size + first : size + first + tile] = (low - high).astype(jnp.bfloat16)

    def along_columns(slot):
        for mode in range(modes):
            for parity in range(2):
                half = product(waves[slot, mode, :, parity * size : (parity + 1) * size], table_ref[parity])
                lanes = slice(parity * tile, (parity + 1) * tile)
                for place, value in enumerate((half[:tile] + half[tile:], half[:tile] - half[tile:])):
                    value = value.astype(jnp.bfloat16)
                    stacked[slot, mode, place * size : place * size + tile, lanes] = value[:, :tile]
                    stacked[slot, mode, place * size + tile : (place + 1) * size, lanes] = value[:, tile:]

    def along_rows(slot):
        for mode in range(modes):
            for parity in range(2):
                rows = slice(parity * size, (parity + 1) * size)
                far[slot, mode, rows, :] = product(table_ref[2 + parity], stacked[slot, mode, rows, :])

    def revise(slot):
        for parity in range(2):
            parts = [slice(parity * size + part * tile, parity * size + (part + 1) * tile) for part in range(2)]
            model = jnp.zeros((tile, size), jnp.float32)
            for mode in range(modes):
                model = model + far[slot, mode, parts[0], :] ** 2 + far[slot, mode, parts[1], :] ** 2
            ratio = amplitude[slot, parity * tile : (parity + 1) * tile, :] * lax.rsqrt(jnp.maximum(model, 0.25))
            for mode in range(modes):
                for part in parts:
                    stacked[slot, mode, part, :] = (far[slot, mode, part, :] * ratio).astype(jnp.bfloat16)

    def back_along_rows(slot):
        for mode in range(modes):
            even = product(table_ref[0], stacked[slot, mode, :size, :])
            odd = product(table_ref[1], stacked[slot, mode, size:, :])
            for rows, value in ((slice(0, tile), even + odd), (slice(tile, size), even - odd)):
                value = value.astype(jnp.bfloat16)
                for parity in range(2):
                    lanes = slice(parity * tile, (parity + 1) * tile)
                    waves[slot, mode, rows, parity * size : parity * size + tile] = value[:tile, lanes]
                    waves[slot, mode, rows, parity * size + tile : (parity + 1) * size] = value[tile:, lanes]

    def back_along_columns(slot):
        for plane in range(2):
            for half in range(2):
                lanes = slice(half * tile, (half + 1) * tile)
                update[slot, plane, :, lanes] = -power_pad[half, tile : tile + size, :] * patch[slot, plane, :, lanes]
        for mode in range(modes):
            even = product(waves[slot, mode, :, :size], table_ref[2])
            odd = product(waves[slot, mode, :, size:], table_ref[3])
            for half, wave in enumerate((even + odd, even - odd)):
                real, imag = wave[:, :tile], wave[:, tile:]
                lanes = slice(half * tile, (half + 1) * tile)
                probe_real = probe_ref[mode, :, lanes]
                probe_imag = probe_ref[mode, :, size + half * tile : size + (half + 1) * tile]
                update[slot, 0, :, lanes] += real * probe_real + imag * probe_imag
                update[slot, 1, :, lanes] += imag * probe_real - real * probe_imag

    def put_deposit(slot):
        column = centres_ref[slot, 1]
        alive = jnp.where(slot < live_ref[0], 1.0, 0.0)
        before = wide_lane < column
        for plane in range(2):
            low = pltpu.roll(update[slot, plane, :, :tile] * alive, column, 1)
            high = pltpu.roll(update[slot, plane, :, tile:] * alive, column, 1)
            deposit[slot, 0, plane, tile : tile + size, :] = jnp.where(before, 0.0, low)
            deposit[slot, 1, plane, tile : tile + size, :] = jnp.where(before, low, high)
            deposit[slot, 2, plane, tile : tile + size, :] = jnp.where(before, high, 0.0)

    stages = (
        take_patch, exit_waves, along_columns, along_rows, revise, back_along_rows, back_along_columns, put_deposit
    )

    row_id = lax.broadcasted_iota(jnp.int32, (8, tile), 0)

    def as_row(value, row):
        return jnp.where(row_id == row, jnp.sum(value, axis=0, keepdims=True), 0.0)

    live_number = live_ref[0].astype(jnp.float32)

    def sum_start(table, mine, base, count, where, iteration):
        copies = []
        for other in range(1, count):
            block = table.at[iteration, mine]
            copies.append(remote(block, block, sums_sem, (iteration, base + other), where(other)))
            copies[-1].start()
        return copies

    energy_copies, scales = [[] for _ in range(ITERS)], []

    def put_results(iteration):
        for copy in energy_copies[iteration]:
            copy.wait()
        step, scale = scales[iteration]
        steps_out[iteration] = step[0, 0]
        energy = jnp.sum(jnp.sum(energy_recv[iteration], axis=0), axis=1, keepdims=True) * scale
        for slot in range(slots):
            alive = (slot < live_ref[0]).astype(jnp.float32)
            energies_out[iteration, slot] = energy[slot, 0] * alive

    for iteration in range(ITERS):
        for stage in stages:
            for slot in range(slots):
                stage(slot)

        def gathered(column, plane, start, length):
            summed = None
            for slot in range(slots):
                term = deposit[slot, column, plane, pl.ds(start + tile - centres_ref[slot, 0], length), :]
                summed = term if summed is None else summed + term
            return summed

        sides, corners = {}, []
        outer = [(name, *piece) for name in ("far", "near") for piece in pieces]
        starts = {"far": far_start, "near": near_start, "middle": tile}
        for place, (name, plane, part) in enumerate(outer + [("middle", 0, None), ("middle", 1, None)]):
            if name == "middle":
                rows, start, length = middle, tile, tile
            else:
                rows, start, length = piece_rows(starts[name], part), starts[name] + part * depth, depth
            pair = []
            for side, (column, step, turn) in enumerate(turns):
                fold[iteration, column, plane, rows, :] = gathered(column, plane, start, length)
                if name == "far":
                    corners.append(Copy(
                        remote(
                            fold.at[iteration, column, plane, rows, :],
                            corner_z.at[iteration, side, plane, piece_rows(0, part), :],
                            fold_sem, (iteration, 8 * count + 2 * place + side), at(-pass_step, 0),
                        ),
                        turn, turn,
                    ))
                    corners[-1].start()
                copy = Copy(
                    remote(
                        fold.at[iteration, column, plane, rows, :], fold_x.at[iteration, side, plane, rows, :],
                        fold_sem, (iteration, 2 * place + side), at(0, step),
                    ),
                    *(() if name == "middle" else ((on_right, on_left), (on_left, on_right))[side]),
                )
                copy.start()
                pair.append(copy)
            sides[name, plane, part] = pair
        for name in starts:
            for plane in range(2):
                fold[iteration, 1, plane, pl.ds(starts[name], tile), :] = gathered(1, plane, starts[name], tile)

        def add_sides(name, plane, part):
            rows = middle if name == "middle" else piece_rows(starts[name], part)
            for side, copy in enumerate(sides[name, plane, part]):
                def add(side=side):
                    fold[iteration, 1, plane, rows, :] += fold_x[iteration, side, plane, rows, :]

                copy.wait_recv()
                when(None if name == "middle" else (on_left, on_right)[side], add)

        passed_on, folds, straight = [], [], []
        for n, (plane, part) in enumerate(pieces):
            add_sides("far", plane, part)
            passed_on.append(remote(
                fold.at[iteration, 1, plane, piece_rows(far_start, part), :],
                fold_z.at[iteration, plane, piece_rows(0, part), :],
                fold_sem, (iteration, 6 * count + n), at(-pass_step, 0),
            ))
            passed_on[n].start()
        for n, (plane, part) in enumerate(pieces):
            here, rows = piece_rows(0, part), piece_rows(near_start, part)
            for side, (column, step, turn) in enumerate(turns):
                def add_corner(plane=plane, side=side, column=column, here=here, rows=rows):
                    fold[iteration, column, plane, rows, :] += corner_z[iteration, side, plane, here, :]

                corners[2 * n + side].wait_recv()
                when(turn, add_corner)
                straight.append(Copy(
                    remote(
                        fold.at[iteration, column, plane, rows, :], corner_y.at[iteration, side, plane, here, :],
                        fold_sem, (iteration, 10 * count + 2 * n + side), at(pair_step, step),
                    ),
                    turn, turns[1 - side][2],
                ))
                straight[-1].start()
        for n, (plane, part) in enumerate(pieces):
            here, rows = piece_rows(0, part), piece_rows(near_start, part)
            add_sides("near", plane, part)
            passed_on[n].wait_recv()
            fold[iteration, 1, plane, rows, :] += fold_z[iteration, plane, here, :]
            folds.append(remote(
                fold.at[iteration, 1, plane, rows, :], fold_y.at[iteration, plane, here, :],
                fold_sem, (iteration, 7 * count + n), at(pair_step, 0),
            ))
            folds[n].start()
        for plane in range(2):
            add_sides("middle", plane, None)
        for n, (plane, part) in enumerate(pieces):
            here, rows = piece_rows(0, part), piece_rows(tile, part)
            for side in range(2):
                def add_straight(plane=plane, side=side, here=here, rows=rows):
                    fold[iteration, 1, plane, rows, :] += corner_y[iteration, side, plane, here, :]

                straight[2 * n + side].wait_recv()
                when(turns[1 - side][2], add_straight)
        cover = coverage[...]
        gradient, moved = [], []
        for plane in range(2):
            for part in range(PARTS):
                folds[plane * PARTS + part].wait_recv()
            gradient.append(fold[iteration, 1, plane, middle, :] + fold_y[iteration, plane])
            moved.append(gradient[plane] / (cover + 0.5))
            direction_ext[iteration, 1, plane, middle, :] = moved[plane]
        last = iteration == ITERS - 1
        if not last:
            state = start_gather(direction_ext.at[iteration], 1 + iteration)

        squares = moved[0] * moved[0] + moved[1] * moved[1]
        sums_x[iteration, my_scan] = (
            as_row(moved[0] * gradient[0] + moved[1] * gradient[1], 0)
            + as_row(cover * squares, 1) + jnp.where(row_id == 2, live_number, 0.0)
        )
        first_sums = sum_start(sums_x, my_scan, 0, n_scan, lambda other: at(0, other), iteration)
        if not last:
            passed = pass_near(direction_ext.at[iteration], 1 + iteration, state)
        for n, (k, c) in enumerate(AROUND):
            block = jnp.zeros((8, tile), jnp.float32)
            for slot in range(slots):
                block = block + as_row(squares * shifted[n, slot], slot)
            if n == 4:
                energy_recv[iteration, n] = block
            else:
                energy_send[iteration, n] = block
                copy = remote(
                    energy_send.at[iteration, n], energy_recv.at[iteration, n],
                    energy_sem, (iteration, n), at(k, c),
                )
                copy.start()
                energy_copies[iteration].append(copy)
        if last:
            for earlier in range(iteration):
                put_results(earlier)
        for copy in first_sums:
            copy.wait()
        sums_y[iteration, my_obj] = jnp.sum(sums_x[iteration], axis=0)
        second_sums = sum_start(sums_y, my_obj, n_scan, n_obj, lambda other: at(other, 0), iteration)
        if not last:
            pass_far(direction_ext.at[iteration], 1 + iteration, state, passed)
        for pair in sides.values():
            for copy in pair:
                copy.wait_send()
        for copy in folds + passed_on + corners + straight:
            copy.wait_send()
        for copy in second_sums:
            copy.wait()
        everywhere = jnp.sum(sums_y[iteration], axis=0)
        rows = jnp.sum(everywhere, axis=1, keepdims=True)
        step = rows[0:1] / rows[1:2]
        scales.append((step, rows[2:3] * (1.0 / tile) / rows[1:2]))
        if not last:
            finish_gather(state, passed)
            extended[...] = extended[...] + step.reshape(1, 1, 1, 1) * direction_ext[iteration]
        else:
            object_out[...] = (
                extended[1, :, middle, :] + step.reshape(1, 1, 1) * direction_ext[iteration, 1, :, middle, :]
            )
    put_results(ITERS - 1)


def on_device(n_scan, n_obj, object_field, probe_modes, patterns, gain_map, defect_mask, probe_centres, live_counts):
    tile = object_field.shape[1]
    modes, size = probe_modes.shape[0], probe_modes.shape[1]
    slots = patterns.shape[0]
    extent = tile + size
    table = transform_tables(size)
    f32 = jnp.float32
    vmem, smem = pl.BlockSpec(memory_space=pltpu.VMEM), pl.BlockSpec(memory_space=pltpu.SMEM)
    hbm = pl.BlockSpec(memory_space=pltpu.HBM)
    flops = ITERS * slots * modes * 4 * 2 * (2 * size) * size * size
    outputs = pl.pallas_call(
        functools.partial(kernel, n_scan, n_obj),
        out_shape=(
            jax.ShapeDtypeStruct(object_field.shape, f32),
            jax.ShapeDtypeStruct((ITERS,), f32),
            jax.ShapeDtypeStruct((ITERS, slots), f32),
        ),
        in_specs=[hbm] * 8,
        out_specs=(vmem, smem, smem),
        scratch_shapes=[
            pltpu.VMEM(probe_modes.shape, f32),
            pltpu.VMEM(patterns.shape, patterns.dtype),
            pltpu.VMEM(gain_map.shape, f32),
            pltpu.VMEM(defect_mask.shape, jnp.int32),
            pltpu.VMEM(table.shape, table.dtype),
            pltpu.SMEM(probe_centres.shape, jnp.int32),
            pltpu.SMEM(live_counts.shape, jnp.int32),
            pltpu.SMEM((9, 128), jnp.int32),
            pltpu.VMEM((3, 2, extent, tile), f32),
            pltpu.VMEM((ITERS, 3, 2, extent, tile), f32),
            pltpu.VMEM((slots, size, size), f32),
            pltpu.VMEM((2, size + 2 * tile, tile), f32),
            pltpu.VMEM((9, slots, tile, tile), f32),
            pltpu.VMEM((tile, tile), f32),
            pltpu.VMEM((slots, 2, size, size), f32),
            pltpu.VMEM((slots, modes, size, 2 * size), jnp.bfloat16),
            pltpu.VMEM((slots, modes, 2 * size, size), jnp.bfloat16),
            pltpu.VMEM((slots, modes, 2 * size, size), f32),
            pltpu.VMEM((slots, 2, size, size), f32),
            pltpu.VMEM((slots, 3, 2, size + 2 * tile, tile), f32),
            pltpu.VMEM((ITERS, 3, 2, extent, tile), f32),
            pltpu.VMEM((ITERS, 2, 2, extent, tile), f32),
            pltpu.VMEM((ITERS, 2, tile, tile), f32),
            pltpu.VMEM((ITERS, 2, tile, tile), f32),
            pltpu.VMEM((ITERS, 2, 2, tile, tile), f32),
            pltpu.VMEM((ITERS, 2, 2, tile, tile), f32),
            pltpu.VMEM((ITERS, 9, 8, tile), f32),
            pltpu.VMEM((ITERS, 9, 8, tile), f32),
            pltpu.VMEM((ITERS, n_scan, 8, tile), f32),
            pltpu.VMEM((ITERS, n_obj, 8, tile), f32),
            pltpu.SemaphoreType.DMA((8,)),
            pltpu.SemaphoreType.DMA((2, 9)),
            pltpu.SemaphoreType.DMA((2, ITERS, 24 * PARTS)),
            pltpu.SemaphoreType.DMA((2, ITERS, 24 * PARTS)),
            pltpu.SemaphoreType.DMA((2, ITERS, 9)),
            pltpu.SemaphoreType.DMA((2, ITERS, n_scan + n_obj)),
        ],
        compiler_params=pltpu.CompilerParams(
            collective_id=0, has_side_effects=True, vmem_limit_bytes=55000 * 1024
        ),
        cost_estimate=pl.CostEstimate(flops=flops, bytes_accessed=8 * 1024 * 1024, transcendentals=0),
    )(object_field, probe_modes, patterns, gain_map, defect_mask, table, probe_centres, live_counts)
    return tuple(outputs)


def solution(mesh):
    placed = (
        P(None, "obj", "scan"),
        P(),
        P(("scan", "obj"), None, None),
        P(),
        P(),
        P(("scan", "obj"), None),
        P(("scan", "obj")),
    )
    return jax.shard_map(
        functools.partial(on_device, mesh.shape["scan"], mesh.shape["obj"]),
        mesh=mesh,
        in_specs=placed,
        out_specs=(P(None, "obj", "scan"), P(), P(None, ("scan", "obj"))),
        check_vma=False,
    )
```

```python
import functools

import jax
import jax.numpy as jnp
import numpy as np
from jax import lax
from jax.experimental import pallas as pl
from jax.experimental.pallas import tpu as pltpu
from jax.sharding import PartitionSpec as P

ITERS = 2
PARTS = 2
MESH = pl.DeviceIdType.MESH
AROUND = [(k, c) for k in (-1, 0, 1) for c in (-1, 0, 1)]


def transform_tables(size):
    indices = np.arange(size, dtype=np.int32)
    phase = (indices[:, None] * indices[None, :] % size).astype(np.float32)
    angles = phase * np.float32(2.0 * 3.141592653589793 / size)
    norm = np.float32(size ** (-0.5))
    cosine, sine = np.cos(angles) * norm, np.sin(angles) * norm
    tables = []
    for first in range(2):
        c, s = cosine[: size // 2, first::2], sine[: size // 2, first::2]
        tables.append(np.block([[c, -s], [s, c]]))
    for first in range(2):
        c, s = cosine[first::2, : size // 2], sine[first::2, : size // 2]
        tables.append(np.block([[c, s], [-s, c]]))
    return jnp.asarray(np.stack(tables)).astype(jnp.bfloat16)


def kernel(
    n_scan, n_obj,
    object_hbm, probe_hbm, patterns_hbm, gain_hbm, mask_hbm, table_hbm, centres_hbm, live_hbm,
    object_out, steps_out, energies_out,
    probe_ref, patterns_ref, gain_ref, mask_ref, table_ref, centres_ref, live_ref,
    info, extended, direction_ext, amplitude, power_pad, shifted, coverage, patch, waves, stacked, far,
    deposit, fold, fold_x, fold_y, fold_z, corner_y, corner_z, energy_send, energy_recv, sums_x, sums_y,
    load_sem, info_sem, halo_sem, fold_sem, energy_sem, sums_sem,
):
    tile = object_hbm.shape[1]
    size = gain_ref.shape[0]
    modes = probe_ref.shape[0]
    slots = patterns_ref.shape[0]
    my_scan, my_obj = lax.axis_index("scan"), lax.axis_index("obj")
    top, middle, bottom = pl.ds(0, tile), pl.ds(tile, tile), pl.ds(2 * tile, tile)

    def at(k, c):
        return {
            "scan": lax.rem(my_scan + (c + n_scan), n_scan),
            "obj": lax.rem(my_obj + (k + n_obj), n_obj),
        }

    def remote(source, target, sems, index, device):
        return pltpu.make_async_remote_copy(
            src_ref=source, dst_ref=target, send_sem=sems.at[(0,) + index],
            recv_sem=sems.at[(1,) + index], device_id=device, device_id_type=MESH,
        )

    pairs = (
        (object_hbm, extended.at[1, :, middle, :]), (centres_hbm, centres_ref), (live_hbm, live_ref),
        (patterns_hbm, patterns_ref), (gain_hbm, gain_ref), (mask_hbm, mask_ref),
        (probe_hbm, probe_ref), (table_hbm, table_ref),
    )
    loads = [
        pltpu.make_async_copy(source, target, load_sem.at[n]) for n, (source, target) in enumerate(pairs)
    ]
    partners = [(0, c) for c in range(1, n_scan)] + [(k, 0) for k in range(1, n_obj)]
    partners += [(k, c) for k, c in AROUND if k and c]
    barrier = pltpu.get_barrier_semaphore()
    for k, c in partners:
        pl.semaphore_signal(barrier, inc=1, device_id=at(k, c), device_id_type=MESH)
    for load in loads:
        load.start()
    pl.semaphore_wait(barrier, len(partners))

    odd = lax.rem(my_obj, 2)
    near_start = pl.multiple_of(2 * tile * (1 - odd), tile)
    far_start = pl.multiple_of(2 * tile * odd, tile)
    near, far_rows = pl.ds(near_start, tile), pl.ds(far_start, tile)
    pair_step, pass_step = 1 - 2 * odd, 2 - 4 * odd

    run = n_scan // 2
    turn_right, turn_left = lax.rem(my_scan, run) == run - 1, lax.rem(my_scan, run) == 0
    on_right, on_left = jnp.logical_not(turn_right), jnp.logical_not(turn_left)
    turns = ((2, 1, turn_right), (0, -1, turn_left))

    def when(condition, act):
        if condition is None:
            act()
        else:
            pl.when(condition)(act)

    class Copy:
        def __init__(self, copy, sends=None, receives=None):
            self.start = lambda: when(sends, copy.start)
            self.wait_send = lambda: when(sends, copy.wait_send)
            self.wait_recv = lambda: when(receives, copy.wait_recv)

        def wait(self):
            self.wait_recv()
            self.wait_send()

    def send_sideways(wide, phase, plane, rows, first, corner):
        mine = wide.at[1, plane, rows, :]
        pair = (
            Copy(
                remote(mine, wide.at[0, plane, rows, :], halo_sem, (phase, first), at(0, 1)),
                *((on_right, on_left) if corner else ()),
            ),
            Copy(
                remote(mine, wide.at[2, plane, rows, :], halo_sem, (phase, first + 1), at(0, -1)),
                *((on_left, on_right) if corner else ()),
            ),
        )
        for copy in pair:
            copy.start()
        return pair

    depth = tile // PARTS
    pieces = [(plane, part) for plane in range(2) for part in range(PARTS)]
    count = len(pieces)

    def piece_rows(start, part):
        return pl.ds(pl.multiple_of(start + part * depth, depth), depth)

    def start_gather(wide, phase):
        direct, corners = [], []
        for n, (plane, part) in enumerate(pieces):
            mine = wide.at[1, plane, piece_rows(tile, part), :]
            there = piece_rows(far_start, part)
            direct.append(remote(mine, wide.at[1, plane, there, :], halo_sem, (phase, n), at(pair_step, 0)))
            direct[n].start()
            corners.append([
                Copy(
                    remote(
                        mine, wide.at[2 - column, plane, there, :],
                        halo_sem, (phase, 8 * count + 2 * n + side), at(pair_step, step),
                    ),
                    turn, turns[1 - side][2],
                )
                for side, (column, step, turn) in enumerate(turns)
            ])
            for copy in corners[n]:
                copy.start()
        beside = [send_sideways(wide, phase, plane, middle, 2 * count + 2 * plane, False) for plane in range(2)]
        return direct, corners, beside

    def pass_near(wide, phase, state):
        direct, corners, beside = state
        passed = []
        for n, (plane, part) in enumerate(pieces):
            here, there = piece_rows(near_start, part), piece_rows(far_start, part)
            direct[n].wait_recv()
            passed.append(Copy(remote(
                wide.at[1, plane, here, :], wide.at[1, plane, there, :],
                halo_sem, (phase, count + n), at(pass_step, 0),
            )))
            passed[-1].start()
            beside.append(send_sideways(wide, phase, plane, here, 4 * count + 2 * n, True))
        for n, (plane, part) in enumerate(pieces):
            here, there = piece_rows(near_start, part), piece_rows(far_start, part)
            for side, (column, step, turn) in enumerate(turns):
                corners[n][1 - side].wait_recv()
                passed.append(Copy(
                    remote(
                        wide.at[column, plane, here, :], wide.at[column, plane, there, :],
                        halo_sem, (phase, 10 * count + 2 * n + side), at(pass_step, 0),
                    ),
                    turn, turn,
                ))
                passed[-1].start()
        return passed

    def pass_far(wide, phase, state, passed):
        for n, (plane, part) in enumerate(pieces):
            passed[n].wait_recv()
            state[2].append(send_sideways(wide, phase, plane, piece_rows(far_start, part), 6 * count + 2 * n, True))

    def finish_gather(state, passed):
        direct, corners, beside = state
        for pair in beside:
            for copy in pair:
                copy.wait_recv()
        for copy in passed[count:]:
            copy.wait_recv()
        return direct + passed + [copy for pair in corners + beside for copy in pair]

    loads[0].wait()
    state = start_gather(extended, 0)

    loads[1].wait()
    loads[2].wait()
    for slot in range(slots):
        info[4, 2 * slot] = centres_ref[slot, 0]
        info[4, 2 * slot + 1] = centres_ref[slot, 1]
    info[4, 2 * slots] = live_ref[0]
    info_copies = [
        remote(info.at[4], info.at[8 - n], info_sem, (n,), at(k, c))
        for n, (k, c) in enumerate(AROUND) if n != 4
    ]
    for copy in info_copies:
        copy.start()

    for load in loads[3:6]:
        load.wait()
    gain, defect = gain_ref[...], mask_ref[...] == 1
    for slot in range(slots):
        corrected = patterns_ref[slot].astype(jnp.float32) * gain
        mean = 0.25 * (
            pltpu.roll(corrected, 1, 0) + pltpu.roll(corrected, size - 1, 0)
            + pltpu.roll(corrected, 1, 1) + pltpu.roll(corrected, size - 1, 1)
        )
        amplitude[slot] = jnp.sqrt(jnp.where(defect, mean, corrected))
    loads[6].wait()
    power = jnp.zeros((size, size), jnp.float32)
    for mode in range(modes):
        power = power + probe_ref[mode, :, :size] ** 2 + probe_ref[mode, :, size:] ** 2
    power_pad[...] = jnp.zeros_like(power_pad)
    for half in range(2):
        power_pad[half, tile : tile + size, :] = power[:, half * tile : (half + 1) * tile]
    for slot in range(slots):
        for column in range(3):
            for plane in range(2):
                zeros = jnp.zeros((tile, tile), jnp.float32)
                deposit[slot, column, plane, :tile, :] = zeros
                deposit[slot, column, plane, tile + size :, :] = zeros
    passed = pass_near(extended, 0, state)
    loads[7].wait()

    place = lax.broadcasted_iota(jnp.int32, (size, size), 0)
    taken = lax.broadcasted_iota(jnp.int32, (size, size), 1)
    half_size = size // 2
    by_row = jnp.where(place < half_size, 2 * place, 2 * place - (size - 1)) == taken
    by_column = jnp.where(taken < half_size, 2 * taken, 2 * taken - (size - 1)) == place
    by_row, by_column = by_row.astype(jnp.float32), by_column.astype(jnp.float32)
    for slot in range(slots):
        ordered = jnp.dot(amplitude[slot], by_column, precision=lax.Precision.HIGHEST)
        amplitude[slot] = jnp.dot(by_row, ordered, precision=lax.Precision.HIGHEST)

    for copy in info_copies:
        copy.wait()
    pass_far(extended, 0, state, passed)
    lane = lax.broadcasted_iota(jnp.int32, (tile, tile), 1)
    total = jnp.zeros((tile, tile), jnp.float32)
    for n, (k, c) in enumerate(AROUND):
        for slot in range(slots):
            row, column = info[n, 2 * slot], info[n, 2 * slot + 1]
            alive = (slot < info[n, 2 * slots]).astype(jnp.float32)
            rows = pl.ds(2 * tile - tile * k - row, tile)
            low, high = (pltpu.roll(power_pad[half, rows, :], column, 1) for half in range(2))
            if c == 0:
                moved = jnp.where(lane < column, low, high)
            elif c < 0:
                moved = jnp.where(lane < column, high, 0.0)
            else:
                moved = jnp.where(lane < column, 0.0, low)
            shifted[n, slot] = moved
            total = total + moved * alive
    coverage[...] = total
    sent = finish_gather(state, passed)

    wide_lane = lax.broadcasted_iota(jnp.int32, (size, tile), 1)

    def product(left, right):
        return jnp.dot(left, right, preferred_element_type=jnp.float32)

    def take_patch(slot):
        row, column = centres_ref[slot, 0], centres_ref[slot, 1]
        back_shift = lax.rem(tile - column, tile)
        close = wide_lane < tile - column
        for plane in range(2):
            first, second, third = (
                pltpu.roll(extended[block, plane, pl.ds(row, size), :], back_shift, 1) for block in range(3)
            )
            patch[slot, plane, :, :tile] = jnp.where(close, first, second)
            patch[slot, plane, :, tile:] = jnp.where(close, second, third)

    def exit_waves(slot):
        for mode in range(modes):
            real, imag = patch[slot, 0], patch[slot, 1]
            probe_real, probe_imag = probe_ref[mode, :, :size], probe_ref[mode, :, size:]
            for part, wave in enumerate((real * probe_real - imag * probe_imag, real * probe_imag + imag * probe_real)):
                low, high = wave[:, :tile], wave[:, tile:]
                first = part * tile
                waves[slot, mode, :, first : first + tile] = (low + high).astype(jnp.bfloat16)
                waves[slot, mode, :, size + first : size + first + tile] = (low - high).astype(jnp.bfloat16)

    def along_columns(slot):
        for mode in range(modes):
            for parity in range(2):
                half = product(waves[slot, mode, :, parity * size : (parity + 1) * size], table_ref[parity])
                lanes = slice(parity * tile, (parity + 1) * tile)
                for place, value in enumerate((half[:tile] + half[tile:], half[:tile] - half[tile:])):
                    value = value.astype(jnp.bfloat16)
                    stacked[slot, mode, place * size : place * size + tile, lanes] = value[:, :tile]
                    stacked[slot, mode, place * size + tile : (place + 1) * size, lanes] = value[:, tile:]

    def along_rows(slot):
        for mode in range(modes):
            for parity in range(2):
                rows = slice(parity * size, (parity + 1) * size)
                far[slot, mode, rows, :] = product(table_ref[2 + parity], stacked[slot, mode, rows, :])

    def revise(slot):
        for parity in range(2):
            parts = [slice(parity * size + part * tile, parity * size + (part + 1) * tile) for part in range(2)]
            model = jnp.zeros((tile, size), jnp.float32)
            for mode in range(modes):
                model = model + far[slot, mode, parts[0], :] ** 2 + far[slot, mode, parts[1], :] ** 2
            ratio = amplitude[slot, parity * tile : (parity + 1) * tile, :] * lax.rsqrt(jnp.maximum(model, 0.25))
            for mode in range(modes):
                for part in parts:
                    stacked[slot, mode, part, :] = (far[slot, mode, part, :] * ratio).astype(jnp.bfloat16)

    def back_along_rows(slot):
        for mode in range(modes):
            even = product(table_ref[0], stacked[slot, mode, :size, :])
            odd = product(table_ref[1], stacked[slot, mode, size:, :])
            for rows, value in ((slice(0, tile), even + odd), (slice(tile, size), even - odd)):
                value = value.astype(jnp.bfloat16)
                for parity in range(2):
                    lanes = slice(parity * tile, (parity + 1) * tile)
                    waves[slot, mode, rows, parity * size : parity * size + tile] = value[:tile, lanes]
                    waves[slot, mode, rows, parity * size + tile : (parity + 1) * size] = value[tile:, lanes]

    def back_along_columns(slot, start):
        rows = pl.ds(pl.multiple_of(start, tile), tile)
        placed_rows = pl.ds(pl.multiple_of(start + tile, tile), tile)
        even = product(waves[slot, :, rows, :size].reshape(modes * tile, size), table_ref[2])
        odd_part = product(waves[slot, :, rows, size:].reshape(modes * tile, size), table_ref[3])
        updates = []
        for half, wave in enumerate((even + odd_part, even - odd_part)):
            lanes = slice(half * tile, (half + 1) * tile)
            power = power_pad[half, placed_rows, :]
            real_sum, imag_sum = (-power * patch[slot, plane, rows, lanes] for plane in range(2))
            for mode in range(modes):
                real, imag = wave[mode * tile : (mode + 1) * tile, :tile], wave[mode * tile : (mode + 1) * tile, tile:]
                probe_real = probe_ref[mode, rows, lanes]
                probe_imag = probe_ref[mode, rows, size + half * tile : size + (half + 1) * tile]
                real_sum = real_sum + (real * probe_real + imag * probe_imag)
                imag_sum = imag_sum + (imag * probe_real - real * probe_imag)
            updates.append((real_sum, imag_sum))
        column = centres_ref[slot, 1]
        alive = jnp.where(slot < live_ref[0], 1.0, 0.0)
        before = lane < column
        for plane in range(2):
            low, high = (pltpu.roll(updates[half][plane] * alive, column, 1) for half in range(2))
            deposit[slot, 0, plane, placed_rows, :] = jnp.where(before, 0.0, low)
            deposit[slot, 1, plane, placed_rows, :] = jnp.where(before, low, high)
            deposit[slot, 2, plane, placed_rows, :] = jnp.where(before, high, 0.0)

    stages = (take_patch, exit_waves, along_columns, along_rows, revise, back_along_rows)

    row_id = lax.broadcasted_iota(jnp.int32, (8, tile), 0)

    def as_row(value, row):
        return jnp.where(row_id == row, jnp.sum(value, axis=0, keepdims=True), 0.0)

    live_number = live_ref[0].astype(jnp.float32)

    def sum_start(table, mine, base, count, where, iteration):
        copies = []
        for other in range(1, count):
            block = table.at[iteration, mine]
            copies.append(remote(block, block, sums_sem, (iteration, base + other), where(other)))
            copies[-1].start()
        return copies

    energy_copies, scales = [[] for _ in range(ITERS)], []

    def put_results(iteration):
        for copy in energy_copies[iteration]:
            copy.wait()
        step, scale = scales[iteration]
        steps_out[iteration] = step[0, 0]
        energy = jnp.sum(jnp.sum(energy_recv[iteration], axis=0), axis=1, keepdims=True) * scale
        for slot in range(slots):
            alive = (slot < live_ref[0]).astype(jnp.float32)
            energies_out[iteration, slot] = energy[slot, 0] * alive

    for iteration in range(ITERS):
        for stage in stages:
            for slot in range(slots):
                stage(slot)
        for slot in range(slots):
            back_along_columns(slot, tile * odd)

        def gathered(column, plane, start, length):
            summed = None
            for slot in range(slots):
                term = deposit[slot, column, plane, pl.ds(start + tile - centres_ref[slot, 0], length), :]
                summed = term if summed is None else summed + term
            return summed

        sides, corners = {}, []
        outer = [(name, *piece) for name in ("far", "near") for piece in pieces]
        starts = {"far": far_start, "near": near_start, "middle": tile}
        order = [(place, *entry) for place, entry in enumerate(outer + [("middle", 0, None), ("middle", 1, None)])]

        def send_out(place, name, plane, part):
            if name == "middle":
                rows, start, length = middle, tile, tile
            else:
                rows, start, length = piece_rows(starts[name], part), starts[name] + part * depth, depth
            pair = []
            for side, (column, step, turn) in enumerate(turns):
                fold[iteration, column, plane, rows, :] = gathered(column, plane, start, length)
                if name == "far":
                    corners.append(Copy(
                        remote(
                            fold.at[iteration, column, plane, rows, :],
                            corner_z.at[iteration, side, plane, piece_rows(0, part), :],
                            fold_sem, (iteration, 8 * count + 2 * place + side), at(-pass_step, 0),
                        ),
                        turn, turn,
                    ))
                    corners[-1].start()
                copy = Copy(
                    remote(
                        fold.at[iteration, column, plane, rows, :], fold_x.at[iteration, side, plane, rows, :],
                        fold_sem, (iteration, 2 * place + side), at(0, step),
                    ),
                    *(() if name == "middle" else ((on_right, on_left), (on_left, on_right))[side]),
                )
                copy.start()
                pair.append(copy)
            sides[name, plane, part] = pair

        for entry in order[:count]:
            send_out(*entry)
        for slot in range(slots):
            back_along_columns(slot, tile * (1 - odd))
        for entry in order[count:]:
            send_out(*entry)
        for name in starts:
            for plane in range(2):
                fold[iteration, 1, plane, pl.ds(starts[name], tile), :] = gathered(1, plane, starts[name], tile)

        def add_sides(name, plane, part):
            rows = middle if name == "middle" else piece_rows(starts[name], part)
            for side, copy in enumerate(sides[name, plane, part]):
                def add(side=side):
                    fold[iteration, 1, plane, rows, :] += fold_x[iteration, side, plane, rows, :]

                copy.wait_recv()
                when(None if name == "middle" else (on_left, on_right)[side], add)

        passed_on, folds, straight = [], [], []
        for n, (plane, part) in enumerate(pieces):
            add_sides("far", plane, part)
            passed_on.append(remote(
                fold.at[iteration, 1, plane, piece_rows(far_start, part), :],
                fold_z.at[iteration, plane, piece_rows(0, part), :],
                fold_sem, (iteration, 6 * count + n), at(-pass_step, 0),
            ))
            passed_on[n].start()
        for n, (plane, part) in enumerate(pieces):
            here, rows = piece_rows(0, part), piece_rows(near_start, part)
            for side, (column, step, turn) in enumerate(turns):
                def add_corner(plane=plane, side=side, column=column, here=here, rows=rows):
                    fold[iteration, column, plane, rows, :] += corner_z[iteration, side, plane, here, :]

                corners[2 * n + side].wait_recv()
                when(turn, add_corner)
                straight.append(Copy(
                    remote(
                        fold.at[iteration, column, plane, rows, :], corner_y.at[iteration, side, plane, here, :],
                        fold_sem, (iteration, 10 * count + 2 * n + side), at(pair_step, step),
                    ),
                    turn, turns[1 - side][2],
                ))
                straight[-1].start()
        for n, (plane, part) in enumerate(pieces):
            here, rows = piece_rows(0, part), piece_rows(near_start, part)
            add_sides("near", plane, part)
            passed_on[n].wait_recv()
            fold[iteration, 1, plane, rows, :] += fold_z[iteration, plane, here, :]
            folds.append(remote(
                fold.at[iteration, 1, plane, rows, :], fold_y.at[iteration, plane, here, :],
                fold_sem, (iteration, 7 * count + n), at(pair_step, 0),
            ))
            folds[n].start()
        for plane in range(2):
            add_sides("middle", plane, None)
        for n, (plane, part) in enumerate(pieces):
            here, rows = piece_rows(0, part), piece_rows(tile, part)
            for side in range(2):
                def add_straight(plane=plane, side=side, here=here, rows=rows):
                    fold[iteration, 1, plane, rows, :] += corner_y[iteration, side, plane, here, :]

                straight[2 * n + side].wait_recv()
                when(turns[1 - side][2], add_straight)
        cover = coverage[...]
        gradient, moved = [], []
        for plane in range(2):
            for part in range(PARTS):
                folds[plane * PARTS + part].wait_recv()
            gradient.append(fold[iteration, 1, plane, middle, :] + fold_y[iteration, plane])
            moved.append(gradient[plane] / (cover + 0.5))
            direction_ext[iteration, 1, plane, middle, :] = moved[plane]
        last = iteration == ITERS - 1
        if not last:
            state = start_gather(direction_ext.at[iteration], 1 + iteration)

        squares = moved[0] * moved[0] + moved[1] * moved[1]
        sums_x[iteration, my_scan] = (
            as_row(moved[0] * gradient[0] + moved[1] * gradient[1], 0)
            + as_row(cover * squares, 1) + jnp.where(row_id == 2, live_number, 0.0)
        )
        first_sums = sum_start(sums_x, my_scan, 0, n_scan, lambda other: at(0, other), iteration)
        if not last:
            passed = pass_near(direction_ext.at[iteration], 1 + iteration, state)
        for n, (k, c) in enumerate(AROUND):
            block = jnp.zeros((8, tile), jnp.float32)
            for slot in range(slots):
                block = block + as_row(squares * shifted[n, slot], slot)
            if n == 4:
                energy_recv[iteration, n] = block
            else:
                energy_send[iteration, n] = block
                copy = remote(
                    energy_send.at[iteration, n], energy_recv.at[iteration, n],
                    energy_sem, (iteration, n), at(k, c),
                )
                copy.start()
                energy_copies[iteration].append(copy)
        if last:
            for earlier in range(iteration):
                put_results(earlier)
        for copy in first_sums:
            copy.wait()
        sums_y[iteration, my_obj] = jnp.sum(sums_x[iteration], axis=0)
        second_sums = sum_start(sums_y, my_obj, n_scan, n_obj, lambda other: at(other, 0), iteration)
        if not last:
            pass_far(direction_ext.at[iteration], 1 + iteration, state, passed)
        for copy in sent + [copy for pair in sides.values() for copy in pair]:
            copy.wait_send()
        for copy in folds + passed_on + corners + straight:
            copy.wait_send()
        for copy in second_sums:
            copy.wait()
        everywhere = jnp.sum(sums_y[iteration], axis=0)
        rows = jnp.sum(everywhere, axis=1, keepdims=True)
        step = rows[0:1] / rows[1:2]
        scales.append((step, rows[2:3] * (1.0 / tile) / rows[1:2]))
        if not last:
            sent = finish_gather(state, passed)
            extended[...] = extended[...] + step.reshape(1, 1, 1, 1) * direction_ext[iteration]
        else:
            object_out[...] = (
                extended[1, :, middle, :] + step.reshape(1, 1, 1) * direction_ext[iteration, 1, :, middle, :]
            )
    put_results(ITERS - 1)


def on_device(n_scan, n_obj, object_field, probe_modes, patterns, gain_map, defect_mask, probe_centres, live_counts):
    tile = object_field.shape[1]
    modes, size = probe_modes.shape[0], probe_modes.shape[1]
    slots = patterns.shape[0]
    extent = tile + size
    table = transform_tables(size)
    f32 = jnp.float32
    vmem, smem = pl.BlockSpec(memory_space=pltpu.VMEM), pl.BlockSpec(memory_space=pltpu.SMEM)
    hbm = pl.BlockSpec(memory_space=pltpu.HBM)
    flops = ITERS * slots * modes * 4 * 2 * (2 * size) * size * size
    outputs = pl.pallas_call(
        functools.partial(kernel, n_scan, n_obj),
        out_shape=(
            jax.ShapeDtypeStruct(object_field.shape, f32),
            jax.ShapeDtypeStruct((ITERS,), f32),
            jax.ShapeDtypeStruct((ITERS, slots), f32),
        ),
        in_specs=[hbm] * 8,
        out_specs=(vmem, smem, smem),
        scratch_shapes=[
            pltpu.VMEM(probe_modes.shape, f32),
            pltpu.VMEM(patterns.shape, patterns.dtype),
            pltpu.VMEM(gain_map.shape, f32),
            pltpu.VMEM(defect_mask.shape, jnp.int32),
            pltpu.VMEM(table.shape, table.dtype),
            pltpu.SMEM(probe_centres.shape, jnp.int32),
            pltpu.SMEM(live_counts.shape, jnp.int32),
            pltpu.SMEM((9, 128), jnp.int32),
            pltpu.VMEM((3, 2, extent, tile), f32),
            pltpu.VMEM((ITERS, 3, 2, extent, tile), f32),
            pltpu.VMEM((slots, size, size), f32),
            pltpu.VMEM((2, size + 2 * tile, tile), f32),
            pltpu.VMEM((9, slots, tile, tile), f32),
            pltpu.VMEM((tile, tile), f32),
            pltpu.VMEM((slots, 2, size, size), f32),
            pltpu.VMEM((slots, modes, size, 2 * size), jnp.bfloat16),
            pltpu.VMEM((slots, modes, 2 * size, size), jnp.bfloat16),
            pltpu.VMEM((slots, modes, 2 * size, size), f32),
            pltpu.VMEM((slots, 3, 2, size + 2 * tile, tile), f32),
            pltpu.VMEM((ITERS, 3, 2, extent, tile), f32),
            pltpu.VMEM((ITERS, 2, 2, extent, tile), f32),
            pltpu.VMEM((ITERS, 2, tile, tile), f32),
            pltpu.VMEM((ITERS, 2, tile, tile), f32),
            pltpu.VMEM((ITERS, 2, 2, tile, tile), f32),
            pltpu.VMEM((ITERS, 2, 2, tile, tile), f32),
            pltpu.VMEM((ITERS, 9, 8, tile), f32),
            pltpu.VMEM((ITERS, 9, 8, tile), f32),
            pltpu.VMEM((ITERS, n_scan, 8, tile), f32),
            pltpu.VMEM((ITERS, n_obj, 8, tile), f32),
            pltpu.SemaphoreType.DMA((8,)),
            pltpu.SemaphoreType.DMA((2, 9)),
            pltpu.SemaphoreType.DMA((2, ITERS, 24 * PARTS)),
            pltpu.SemaphoreType.DMA((2, ITERS, 24 * PARTS)),
            pltpu.SemaphoreType.DMA((2, ITERS, 9)),
            pltpu.SemaphoreType.DMA((2, ITERS, n_scan + n_obj)),
        ],
        compiler_params=pltpu.CompilerParams(
            collective_id=0, has_side_effects=True, vmem_limit_bytes=55000 * 1024
        ),
        cost_estimate=pl.CostEstimate(flops=flops, bytes_accessed=8 * 1024 * 1024, transcendentals=0),
    )(object_field, probe_modes, patterns, gain_map, defect_mask, table, probe_centres, live_counts)
    return tuple(outputs)


def solution(mesh):
    placed = (
        P(None, "obj", "scan"),
        P(),
        P(("scan", "obj"), None, None),
        P(),
        P(),
        P(("scan", "obj"), None),
        P(("scan", "obj")),
    )
    return jax.shard_map(
        functools.partial(on_device, mesh.shape["scan"], mesh.shape["obj"]),
        mesh=mesh,
        in_specs=placed,
        out_specs=(P(None, "obj", "scan"), P(), P(None, ("scan", "obj"))),
        check_vma=False,
    )
```

```python
import functools

import jax
import jax.numpy as jnp
import numpy as np
from jax import lax
from jax.experimental import pallas as pl
from jax.experimental.pallas import tpu as pltpu
from jax.sharding import PartitionSpec as P

ITERS = 2
PARTS = 2
MESH = pl.DeviceIdType.MESH
AROUND = [(k, c) for k in (-1, 0, 1) for c in (-1, 0, 1)]


def transform_tables(size):
    indices = np.arange(size, dtype=np.int32)
    phase = (indices[:, None] * indices[None, :] % size).astype(np.float32)
    angles = phase * np.float32(2.0 * 3.141592653589793 / size)
    norm = np.float32(size ** (-0.5))
    cosine, sine = np.cos(angles) * norm, np.sin(angles) * norm
    tables = []
    for first in range(2):
        c, s = cosine[: size // 2, first::2], sine[: size // 2, first::2]
        tables.append(np.block([[c, -s], [s, c]]))
    for first in range(2):
        c, s = cosine[first::2, : size // 2], sine[first::2, : size // 2]
        tables.append(np.block([[c, s], [-s, c]]))
    return jnp.asarray(np.stack(tables)).astype(jnp.bfloat16)


def kernel(
    n_scan, n_obj,
    object_hbm, probe_hbm, patterns_hbm, gain_hbm, mask_hbm, table_hbm, centres_hbm, live_hbm,
    object_out, steps_out, energies_out,
    probe_ref, patterns_ref, gain_ref, mask_ref, table_ref, centres_ref, live_ref,
    info, extended, direction_ext, amplitude, power_pad, shifted, coverage, patch, waves, stacked, far,
    deposit, fold, fold_x, fold_y, fold_z, corner_y, corner_z, energy_send, energy_recv, sums_x, sums_y,
    load_sem, info_sem, halo_sem, fold_sem, energy_sem, sums_sem,
):
    tile = object_hbm.shape[1]
    size = gain_ref.shape[0]
    modes = probe_ref.shape[0]
    slots = patterns_ref.shape[0]
    my_scan, my_obj = lax.axis_index("scan"), lax.axis_index("obj")
    top, middle, bottom = pl.ds(0, tile), pl.ds(tile, tile), pl.ds(2 * tile, tile)

    def at(k, c):
        return {
            "scan": lax.rem(my_scan + (c + n_scan), n_scan),
            "obj": lax.rem(my_obj + (k + n_obj), n_obj),
        }

    def remote(source, target, sems, index, device):
        return pltpu.make_async_remote_copy(
            src_ref=source, dst_ref=target, send_sem=sems.at[(0,) + index],
            recv_sem=sems.at[(1,) + index], device_id=device, device_id_type=MESH,
        )

    pairs = (
        (object_hbm, extended.at[1, :, middle, :]), (centres_hbm, centres_ref), (live_hbm, live_ref),
        (patterns_hbm, patterns_ref), (gain_hbm, gain_ref), (mask_hbm, mask_ref),
        (probe_hbm, probe_ref), (table_hbm, table_ref),
    )
    loads = [
        pltpu.make_async_copy(source, target, load_sem.at[n]) for n, (source, target) in enumerate(pairs)
    ]
    run = n_scan // 2
    my_run, my_place = my_scan // run, lax.rem(my_scan, run)
    in_run = [
        {"scan": my_run * run + lax.rem(my_place + other, run), "obj": my_obj} for other in range(1, run)
    ]
    across = [at(k, c) for c in (0, run) for k in range(n_obj) if k or c]
    partners = in_run + across + [at(0, -1), at(0, 1)] + [at(k, c) for k, c in AROUND if k and c]
    barrier = pltpu.get_barrier_semaphore()
    for partner in partners:
        pl.semaphore_signal(barrier, inc=1, device_id=partner, device_id_type=MESH)
    for load in loads:
        load.start()
    pl.semaphore_wait(barrier, len(partners))

    odd = lax.rem(my_obj, 2)
    near_start = pl.multiple_of(2 * tile * (1 - odd), tile)
    far_start = pl.multiple_of(2 * tile * odd, tile)
    near, far_rows = pl.ds(near_start, tile), pl.ds(far_start, tile)
    pair_step, pass_step = 1 - 2 * odd, 2 - 4 * odd

    turn_right, turn_left = my_place == run - 1, my_place == 0
    on_right, on_left = jnp.logical_not(turn_right), jnp.logical_not(turn_left)
    turns = ((2, 1, turn_right), (0, -1, turn_left))

    def when(condition, act):
        if condition is None:
            act()
        else:
            pl.when(condition)(act)

    class Copy:
        def __init__(self, copy, sends=None, receives=None):
            self.start = lambda: when(sends, copy.start)
            self.wait_send = lambda: when(sends, copy.wait_send)
            self.wait_recv = lambda: when(receives, copy.wait_recv)

        def wait(self):
            self.wait_recv()
            self.wait_send()

    def send_sideways(wide, phase, plane, rows, first, corner):
        mine = wide.at[1, plane, rows, :]
        pair = (
            Copy(
                remote(mine, wide.at[0, plane, rows, :], halo_sem, (phase, first), at(0, 1)),
                *((on_right, on_left) if corner else ()),
            ),
            Copy(
                remote(mine, wide.at[2, plane, rows, :], halo_sem, (phase, first + 1), at(0, -1)),
                *((on_left, on_right) if corner else ()),
            ),
        )
        for copy in pair:
            copy.start()
        return pair

    depth = tile // PARTS
    pieces = [(plane, part) for plane in range(2) for part in range(PARTS)]
    count = len(pieces)

    def piece_rows(start, part):
        return pl.ds(pl.multiple_of(start + part * depth, depth), depth)

    def start_gather(wide, phase):
        direct, corners = [], []
        for n, (plane, part) in enumerate(pieces):
            mine = wide.at[1, plane, piece_rows(tile, part), :]
            there = piece_rows(far_start, part)
            direct.append(remote(mine, wide.at[1, plane, there, :], halo_sem, (phase, n), at(pair_step, 0)))
            direct[n].start()
            corners.append([
                Copy(
                    remote(
                        mine, wide.at[2 - column, plane, there, :],
                        halo_sem, (phase, 8 * count + 2 * n + side), at(pair_step, step),
                    ),
                    turn, turns[1 - side][2],
                )
                for side, (column, step, turn) in enumerate(turns)
            ])
            for copy in corners[n]:
                copy.start()
        beside = [send_sideways(wide, phase, plane, middle, 2 * count + 2 * plane, False) for plane in range(2)]
        return direct, corners, beside

    def pass_near(wide, phase, state):
        direct, corners, beside = state
        passed = []
        for n, (plane, part) in enumerate(pieces):
            here, there = piece_rows(near_start, part), piece_rows(far_start, part)
            direct[n].wait_recv()
            passed.append(Copy(remote(
                wide.at[1, plane, here, :], wide.at[1, plane, there, :],
                halo_sem, (phase, count + n), at(pass_step, 0),
            )))
            passed[-1].start()
            beside.append(send_sideways(wide, phase, plane, here, 4 * count + 2 * n, True))
        for n, (plane, part) in enumerate(pieces):
            here, there = piece_rows(near_start, part), piece_rows(far_start, part)
            for side, (column, step, turn) in enumerate(turns):
                corners[n][1 - side].wait_recv()
                passed.append(Copy(
                    remote(
                        wide.at[column, plane, here, :], wide.at[column, plane, there, :],
                        halo_sem, (phase, 10 * count + 2 * n + side), at(pass_step, 0),
                    ),
                    turn, turn,
                ))
                passed[-1].start()
        return passed

    def pass_far(wide, phase, state, passed):
        for n, (plane, part) in enumerate(pieces):
            passed[n].wait_recv()
            state[2].append(send_sideways(wide, phase, plane, piece_rows(far_start, part), 6 * count + 2 * n, True))

    def finish_gather(state, passed):
        direct, corners, beside = state
        for pair in beside:
            for copy in pair:
                copy.wait_recv()
        for copy in passed[count:]:
            copy.wait_recv()
        return direct + passed + [copy for pair in corners + beside for copy in pair]

    loads[0].wait()
    state = start_gather(extended, 0)

    loads[1].wait()
    loads[2].wait()
    for slot in range(slots):
        info[4, 2 * slot] = centres_ref[slot, 0]
        info[4, 2 * slot + 1] = centres_ref[slot, 1]
    info[4, 2 * slots] = live_ref[0]
    info_copies = [
        remote(info.at[4], info.at[8 - n], info_sem, (n,), at(k, c))
        for n, (k, c) in enumerate(AROUND) if n != 4
    ]
    for copy in info_copies:
        copy.start()

    for load in loads[3:6]:
        load.wait()
    gain, defect = gain_ref[...], mask_ref[...] == 1
    for slot in range(slots):
        corrected = patterns_ref[slot].astype(jnp.float32) * gain
        mean = 0.25 * (
            pltpu.roll(corrected, 1, 0) + pltpu.roll(corrected, size - 1, 0)
            + pltpu.roll(corrected, 1, 1) + pltpu.roll(corrected, size - 1, 1)
        )
        amplitude[slot] = jnp.sqrt(jnp.where(defect, mean, corrected))
    loads[6].wait()
    power = jnp.zeros((size, size), jnp.float32)
    for mode in range(modes):
        power = power + probe_ref[mode, :, :size] ** 2 + probe_ref[mode, :, size:] ** 2
    power_pad[...] = jnp.zeros_like(power_pad)
    for half in range(2):
        power_pad[half, tile : tile + size, :] = power[:, half * tile : (half + 1) * tile]
    for slot in range(slots):
        for column in range(3):
            for plane in range(2):
                zeros = jnp.zeros((tile, tile), jnp.float32)
                deposit[slot, column, plane, :tile, :] = zeros
                deposit[slot, column, plane, tile + size :, :] = zeros
    passed = pass_near(extended, 0, state)
    loads[7].wait()

    place = lax.broadcasted_iota(jnp.int32, (size, size), 0)
    taken = lax.broadcasted_iota(jnp.int32, (size, size), 1)
    half_size = size // 2
    by_row = jnp.where(place < half_size, 2 * place, 2 * place - (size - 1)) == taken
    by_column = jnp.where(taken < half_size, 2 * taken, 2 * taken - (size - 1)) == place
    by_row, by_column = by_row.astype(jnp.float32), by_column.astype(jnp.float32)
    for slot in range(slots):
        ordered = jnp.dot(amplitude[slot], by_column, precision=lax.Precision.HIGHEST)
        amplitude[slot] = jnp.dot(by_row, ordered, precision=lax.Precision.HIGHEST)

    for copy in info_copies:
        copy.wait()
    pass_far(extended, 0, state, passed)
    lane = lax.broadcasted_iota(jnp.int32, (tile, tile), 1)
    total = jnp.zeros((tile, tile), jnp.float32)
    for n, (k, c) in enumerate(AROUND):
        for slot in range(slots):
            row, column = info[n, 2 * slot], info[n, 2 * slot + 1]
            alive = (slot < info[n, 2 * slots]).astype(jnp.float32)
            rows = pl.ds(2 * tile - tile * k - row, tile)
            low, high = (pltpu.roll(power_pad[half, rows, :], column, 1) for half in range(2))
            if c == 0:
                moved = jnp.where(lane < column, low, high)
            elif c < 0:
                moved = jnp.where(lane < column, high, 0.0)
            else:
                moved = jnp.where(lane < column, 0.0, low)
            shifted[n, slot] = moved
            total = total + moved * alive
    coverage[...] = total
    sent = finish_gather(state, passed)

    wide_lane = lax.broadcasted_iota(jnp.int32, (size, tile), 1)

    def product(left, right):
        return jnp.dot(left, right, preferred_element_type=jnp.float32)

    def take_patch(slot):
        row, column = centres_ref[slot, 0], centres_ref[slot, 1]
        back_shift = lax.rem(tile - column, tile)
        close = wide_lane < tile - column
        for plane in range(2):
            first, second, third = (
                pltpu.roll(extended[block, plane, pl.ds(row, size), :], back_shift, 1) for block in range(3)
            )
            patch[slot, plane, :, :tile] = jnp.where(close, first, second)
            patch[slot, plane, :, tile:] = jnp.where(close, second, third)

    def exit_waves(slot):
        for mode in range(modes):
            real, imag = patch[slot, 0], patch[slot, 1]
            probe_real, probe_imag = probe_ref[mode, :, :size], probe_ref[mode, :, size:]
            for part, wave in enumerate((real * probe_real - imag * probe_imag, real * probe_imag + imag * probe_real)):
                low, high = wave[:, :tile], wave[:, tile:]
                first = part * tile
                waves[slot, mode, :, first : first + tile] = (low + high).astype(jnp.bfloat16)
                waves[slot, mode, :, size + first : size + first + tile] = (low - high).astype(jnp.bfloat16)

    def along_columns(slot):
        for mode in range(modes):
            for parity in range(2):
                half = product(waves[slot, mode, :, parity * size : (parity + 1) * size], table_ref[parity])
                lanes = slice(parity * tile, (parity + 1) * tile)
                for place, value in enumerate((half[:tile] + half[tile:], half[:tile] - half[tile:])):
                    value = value.astype(jnp.bfloat16)
                    stacked[slot, mode, place * size : place * size + tile, lanes] = value[:, :tile]
                    stacked[slot, mode, place * size + tile : (place + 1) * size, lanes] = value[:, tile:]

    def along_rows(slot):
        for mode in range(modes):
            for parity in range(2):
                rows = slice(parity * size, (parity + 1) * size)
                far[slot, mode, rows, :] = product(table_ref[2 + parity], stacked[slot, mode, rows, :])

    def revise(slot):
        for parity in range(2):
            parts = [slice(parity * size + part * tile, parity * size + (part + 1) * tile) for part in range(2)]
            model = jnp.zeros((tile, size), jnp.float32)
            for mode in range(modes):
                model = model + far[slot, mode, parts[0], :] ** 2 + far[slot, mode, parts[1], :] ** 2
            ratio = amplitude[slot, parity * tile : (parity + 1) * tile, :] * lax.rsqrt(jnp.maximum(model, 0.25))
            for mode in range(modes):
                for part in parts:
                    stacked[slot, mode, part, :] = (far[slot, mode, part, :] * ratio).astype(jnp.bfloat16)

    def back_along_rows(slot):
        for mode in range(modes):
            even = product(table_ref[0], stacked[slot, mode, :size, :])
            odd = product(table_ref[1], stacked[slot, mode, size:, :])
            for rows, value in ((slice(0, tile), even + odd), (slice(tile, size), even - odd)):
                value = value.astype(jnp.bfloat16)
                for parity in range(2):
                    lanes = slice(parity * tile, (parity + 1) * tile)
                    waves[slot, mode, rows, parity * size : parity * size + tile] = value[:tile, lanes]
                    waves[slot, mode, rows, parity * size + tile : (parity + 1) * size] = value[tile:, lanes]

    def back_along_columns(slot, start):
        rows = pl.ds(pl.multiple_of(start, tile), tile)
        placed_rows = pl.ds(pl.multiple_of(start + tile, tile), tile)
        even = product(waves[slot, :, rows, :size].reshape(modes * tile, size), table_ref[2])
        odd_part = product(waves[slot, :, rows, size:].reshape(modes * tile, size), table_ref[3])
        updates = []
        for half, wave in enumerate((even + odd_part, even - odd_part)):
            lanes = slice(half * tile, (half + 1) * tile)
            power = power_pad[half, placed_rows, :]
            real_sum, imag_sum = (-power * patch[slot, plane, rows, lanes] for plane in range(2))
            for mode in range(modes):
                real, imag = wave[mode * tile : (mode + 1) * tile, :tile], wave[mode * tile : (mode + 1) * tile, tile:]
                probe_real = probe_ref[mode, rows, lanes]
                probe_imag = probe_ref[mode, rows, size + half * tile : size + (half + 1) * tile]
                real_sum = real_sum + (real * probe_real + imag * probe_imag)
                imag_sum = imag_sum + (imag * probe_real - real * probe_imag)
            updates.append((real_sum, imag_sum))
        column = centres_ref[slot, 1]
        alive = jnp.where(slot < live_ref[0], 1.0, 0.0)
        before = lane < column
        for plane in range(2):
            low, high = (pltpu.roll(updates[half][plane] * alive, column, 1) for half in range(2))
            deposit[slot, 0, plane, placed_rows, :] = jnp.where(before, 0.0, low)
            deposit[slot, 1, plane, placed_rows, :] = jnp.where(before, low, high)
            deposit[slot, 2, plane, placed_rows, :] = jnp.where(before, high, 0.0)

    stages = (take_patch, exit_waves, along_columns, along_rows, revise, back_along_rows)

    row_id = lax.broadcasted_iota(jnp.int32, (8, tile), 0)

    def as_row(value, row):
        return jnp.where(row_id == row, jnp.sum(value, axis=0, keepdims=True), 0.0)

    live_number = live_ref[0].astype(jnp.float32)

    def sum_start(table, mine, base, devices, iteration):
        copies = []
        for n, device in enumerate(devices):
            block = table.at[iteration, mine]
            copies.append(remote(block, block, sums_sem, (iteration, base + n), device))
            copies[-1].start()
        return copies

    lane_id = lax.broadcasted_iota(jnp.int32, (1, tile), 1)

    def whole(value):
        return jnp.sum(jnp.sum(value, axis=0, keepdims=True), axis=1, keepdims=True)

    energy_copies, scales = [[] for _ in range(ITERS)], []

    def put_results(iteration):
        for copy in energy_copies[iteration]:
            copy.wait()
        step, scale = scales[iteration]
        steps_out[iteration] = step[0, 0]
        energy = jnp.sum(jnp.sum(energy_recv[iteration], axis=0), axis=1, keepdims=True) * scale
        for slot in range(slots):
            alive = (slot < live_ref[0]).astype(jnp.float32)
            energies_out[iteration, slot] = energy[slot, 0] * alive

    for iteration in range(ITERS):
        for stage in stages:
            for slot in range(slots):
                stage(slot)
        for slot in range(slots):
            back_along_columns(slot, tile * odd)

        def gathered(column, plane, start, length):
            summed = None
            for slot in range(slots):
                term = deposit[slot, column, plane, pl.ds(start + tile - centres_ref[slot, 0], length), :]
                summed = term if summed is None else summed + term
            return summed

        sides, corners = {}, []
        outer = [(name, *piece) for name in ("far", "near") for piece in pieces]
        starts = {"far": far_start, "near": near_start, "middle": tile}
        order = [(place, *entry) for place, entry in enumerate(outer + [("middle", 0, None), ("middle", 1, None)])]

        def send_out(place, name, plane, part):
            if name == "middle":
                rows, start, length = middle, tile, tile
            else:
                rows, start, length = piece_rows(starts[name], part), starts[name] + part * depth, depth
            pair = []
            for side, (column, step, turn) in enumerate(turns):
                fold[iteration, column, plane, rows, :] = gathered(column, plane, start, length)
                if name == "far":
                    corners.append(Copy(
                        remote(
                            fold.at[iteration, column, plane, rows, :],
                            corner_z.at[iteration, side, plane, piece_rows(0, part), :],
                            fold_sem, (iteration, 8 * count + 2 * place + side), at(-pass_step, 0),
                        ),
                        turn, turn,
                    ))
                    corners[-1].start()
                copy = Copy(
                    remote(
                        fold.at[iteration, column, plane, rows, :], fold_x.at[iteration, side, plane, rows, :],
                        fold_sem, (iteration, 2 * place + side), at(0, step),
                    ),
                    *(() if name == "middle" else ((on_right, on_left), (on_left, on_right))[side]),
                )
                copy.start()
                pair.append(copy)
            sides[name, plane, part] = pair

        for entry in order[:count]:
            send_out(*entry)
        for slot in range(slots):
            back_along_columns(slot, tile * (1 - odd))
        for entry in order[count:]:
            send_out(*entry)
        for name in starts:
            for plane in range(2):
                fold[iteration, 1, plane, pl.ds(starts[name], tile), :] = gathered(1, plane, starts[name], tile)

        def add_sides(name, plane, part):
            rows = middle if name == "middle" else piece_rows(starts[name], part)
            for side, copy in enumerate(sides[name, plane, part]):
                def add(side=side):
                    fold[iteration, 1, plane, rows, :] += fold_x[iteration, side, plane, rows, :]

                copy.wait_recv()
                when(None if name == "middle" else (on_left, on_right)[side], add)

        passed_on, folds, straight = [], [], []
        for n, (plane, part) in enumerate(pieces):
            add_sides("far", plane, part)
            passed_on.append(remote(
                fold.at[iteration, 1, plane, piece_rows(far_start, part), :],
                fold_z.at[iteration, plane, piece_rows(0, part), :],
                fold_sem, (iteration, 6 * count + n), at(-pass_step, 0),
            ))
            passed_on[n].start()
        for n, (plane, part) in enumerate(pieces):
            here, rows = piece_rows(0, part), piece_rows(near_start, part)
            for side, (column, step, turn) in enumerate(turns):
                def add_corner(plane=plane, side=side, column=column, here=here, rows=rows):
                    fold[iteration, column, plane, rows, :] += corner_z[iteration, side, plane, here, :]

                corners[2 * n + side].wait_recv()
                when(turn, add_corner)
                straight.append(Copy(
                    remote(
                        fold.at[iteration, column, plane, rows, :], corner_y.at[iteration, side, plane, here, :],
                        fold_sem, (iteration, 10 * count + 2 * n + side), at(pair_step, step),
                    ),
                    turn, turns[1 - side][2],
                ))
                straight[-1].start()
        for n, (plane, part) in enumerate(pieces):
            here, rows = piece_rows(0, part), piece_rows(near_start, part)
            add_sides("near", plane, part)
            passed_on[n].wait_recv()
            fold[iteration, 1, plane, rows, :] += fold_z[iteration, plane, here, :]
            folds.append(remote(
                fold.at[iteration, 1, plane, rows, :], fold_y.at[iteration, plane, here, :],
                fold_sem, (iteration, 7 * count + n), at(pair_step, 0),
            ))
            folds[n].start()
        for plane in range(2):
            add_sides("middle", plane, None)
        for n, (plane, part) in enumerate(pieces):
            here, rows = piece_rows(0, part), piece_rows(tile, part)
            for side in range(2):
                def add_straight(plane=plane, side=side, here=here, rows=rows):
                    fold[iteration, 1, plane, rows, :] += corner_y[iteration, side, plane, here, :]

                straight[2 * n + side].wait_recv()
                when(turns[1 - side][2], add_straight)
        cover = coverage[...]
        gradient, moved = [], []
        for plane in range(2):
            for part in range(PARTS):
                folds[plane * PARTS + part].wait_recv()
            gradient.append(fold[iteration, 1, plane, middle, :] + fold_y[iteration, plane])
            moved.append(gradient[plane] / (cover + 0.5))
            direction_ext[iteration, 1, plane, middle, :] = moved[plane]
        last = iteration == ITERS - 1
        if not last:
            state = start_gather(direction_ext.at[iteration], 1 + iteration)

        squares = moved[0] * moved[0] + moved[1] * moved[1]
        numerator = whole(moved[0] * gradient[0] + moved[1] * gradient[1])
        denominator = whole(cover * squares)
        sums_x[iteration, my_place] = jnp.where(
            lane_id == 0, numerator, jnp.where(lane_id == 1, denominator, jnp.where(lane_id == 2, live_number, 0.0))
        )
        first_sums = sum_start(sums_x, my_place, 0, in_run, iteration)
        if not last:
            passed = pass_near(direction_ext.at[iteration], 1 + iteration, state)
        for n, (k, c) in enumerate(AROUND):
            block = jnp.zeros((8, tile), jnp.float32)
            for slot in range(slots):
                block = block + as_row(squares * shifted[n, slot], slot)
            if n == 4:
                energy_recv[iteration, n] = block
            else:
                energy_send[iteration, n] = block
                copy = remote(
                    energy_send.at[iteration, n], energy_recv.at[iteration, n],
                    energy_sem, (iteration, n), at(k, c),
                )
                copy.start()
                energy_copies[iteration].append(copy)
        if last:
            for earlier in range(iteration):
                put_results(earlier)
        for copy in first_sums:
            copy.wait()
        mine = my_run * n_obj + my_obj
        sums_y[iteration, mine] = jnp.sum(sums_x[iteration], axis=0)
        second_sums = sum_start(sums_y, mine, run, across, iteration)
        if not last:
            pass_far(direction_ext.at[iteration], 1 + iteration, state, passed)
        for copy in sent + [copy for pair in sides.values() for copy in pair]:
            copy.wait_send()
        for copy in folds + passed_on + corners + straight:
            copy.wait_send()
        for copy in second_sums:
            copy.wait()
        everywhere = jnp.sum(sums_y[iteration], axis=0)
        numerator, denominator, live_total = (everywhere[:, n : n + 1] for n in range(3))
        step = numerator / denominator
        scales.append((step, live_total / denominator))
        if not last:
            sent = finish_gather(state, passed)
            extended[...] = extended[...] + step.reshape(1, 1, 1, 1) * direction_ext[iteration]
        else:
            object_out[...] = (
                extended[1, :, middle, :] + step.reshape(1, 1, 1) * direction_ext[iteration, 1, :, middle, :]
            )
    put_results(ITERS - 1)


def on_device(n_scan, n_obj, object_field, probe_modes, patterns, gain_map, defect_mask, probe_centres, live_counts):
    tile = object_field.shape[1]
    modes, size = probe_modes.shape[0], probe_modes.shape[1]
    slots = patterns.shape[0]
    extent = tile + size
    table = transform_tables(size)
    f32 = jnp.float32
    vmem, smem = pl.BlockSpec(memory_space=pltpu.VMEM), pl.BlockSpec(memory_space=pltpu.SMEM)
    hbm = pl.BlockSpec(memory_space=pltpu.HBM)
    flops = ITERS * slots * modes * 4 * 2 * (2 * size) * size * size
    outputs = pl.pallas_call(
        functools.partial(kernel, n_scan, n_obj),
        out_shape=(
            jax.ShapeDtypeStruct(object_field.shape, f32),
            jax.ShapeDtypeStruct((ITERS,), f32),
            jax.ShapeDtypeStruct((ITERS, slots), f32),
        ),
        in_specs=[hbm] * 8,
        out_specs=(vmem, smem, smem),
        scratch_shapes=[
            pltpu.VMEM(probe_modes.shape, f32),
            pltpu.VMEM(patterns.shape, patterns.dtype),
            pltpu.VMEM(gain_map.shape, f32),
            pltpu.VMEM(defect_mask.shape, jnp.int32),
            pltpu.VMEM(table.shape, table.dtype),
            pltpu.SMEM(probe_centres.shape, jnp.int32),
            pltpu.SMEM(live_counts.shape, jnp.int32),
            pltpu.SMEM((9, 128), jnp.int32),
            pltpu.VMEM((3, 2, extent, tile), f32),
            pltpu.VMEM((ITERS, 3, 2, extent, tile), f32),
            pltpu.VMEM((slots, size, size), f32),
            pltpu.VMEM((2, size + 2 * tile, tile), f32),
            pltpu.VMEM((9, slots, tile, tile), f32),
            pltpu.VMEM((tile, tile), f32),
            pltpu.VMEM((slots, 2, size, size), f32),
            pltpu.VMEM((slots, modes, size, 2 * size), jnp.bfloat16),
            pltpu.VMEM((slots, modes, 2 * size, size), jnp.bfloat16),
            pltpu.VMEM((slots, modes, 2 * size, size), f32),
            pltpu.VMEM((slots, 3, 2, size + 2 * tile, tile), f32),
            pltpu.VMEM((ITERS, 3, 2, extent, tile), f32),
            pltpu.VMEM((ITERS, 2, 2, extent, tile), f32),
            pltpu.VMEM((ITERS, 2, tile, tile), f32),
            pltpu.VMEM((ITERS, 2, tile, tile), f32),
            pltpu.VMEM((ITERS, 2, 2, tile, tile), f32),
            pltpu.VMEM((ITERS, 2, 2, tile, tile), f32),
            pltpu.VMEM((ITERS, 9, 8, tile), f32),
            pltpu.VMEM((ITERS, 9, 8, tile), f32),
            pltpu.VMEM((ITERS, n_scan // 2, 1, tile), f32),
            pltpu.VMEM((ITERS, 2 * n_obj, 1, tile), f32),
            pltpu.SemaphoreType.DMA((8,)),
            pltpu.SemaphoreType.DMA((2, 9)),
            pltpu.SemaphoreType.DMA((2, ITERS, 24 * PARTS)),
            pltpu.SemaphoreType.DMA((2, ITERS, 24 * PARTS)),
            pltpu.SemaphoreType.DMA((2, ITERS, 9)),
            pltpu.SemaphoreType.DMA((2, ITERS, n_scan // 2 + 2 * n_obj)),
        ],
        compiler_params=pltpu.CompilerParams(
            collective_id=0, has_side_effects=True, vmem_limit_bytes=55000 * 1024
        ),
        cost_estimate=pl.CostEstimate(flops=flops, bytes_accessed=8 * 1024 * 1024, transcendentals=0),
    )(object_field, probe_modes, patterns, gain_map, defect_mask, table, probe_centres, live_counts)
    return tuple(outputs)


def solution(mesh):
    placed = (
        P(None, "obj", "scan"),
        P(),
        P(("scan", "obj"), None, None),
        P(),
        P(),
        P(("scan", "obj"), None),
        P(("scan", "obj")),
    )
    return jax.shard_map(
        functools.partial(on_device, mesh.shape["scan"], mesh.shape["obj"]),
        mesh=mesh,
        in_specs=placed,
        out_specs=(P(None, "obj", "scan"), P(), P(None, ("scan", "obj"))),
        check_vma=False,
    )
```

```python
import functools

import jax
import jax.numpy as jnp
import numpy as np
from jax import lax
from jax.experimental import pallas as pl
from jax.experimental.pallas import tpu as pltpu
from jax.sharding import PartitionSpec as P

ITERS = 2
PARTS = 2
MESH = pl.DeviceIdType.MESH
AROUND = [(k, c) for k in (-1, 0, 1) for c in (-1, 0, 1)]


def transform_tables(size):
    indices = np.arange(size, dtype=np.int32)
    phase = (indices[:, None] * indices[None, :] % size).astype(np.float32)
    angles = phase * np.float32(2.0 * 3.141592653589793 / size)
    norm = np.float32(size ** (-0.5))
    cosine, sine = np.cos(angles) * norm, np.sin(angles) * norm
    tables = []
    for first in range(2):
        c, s = cosine[: size // 2, first::2], sine[: size // 2, first::2]
        tables.append(np.block([[c, -s], [s, c]]))
    for first in range(2):
        c, s = cosine[first::2, : size // 2], sine[first::2, : size // 2]
        tables.append(np.block([[c, s], [-s, c]]))
    return jnp.asarray(np.stack(tables)).astype(jnp.bfloat16)


def kernel(
    n_scan, n_obj,
    object_hbm, probe_hbm, patterns_hbm, gain_hbm, mask_hbm, table_hbm, centres_hbm, live_hbm,
    object_out, steps_out, energies_out,
    probe_ref, patterns_ref, gain_ref, mask_ref, table_ref, centres_ref, live_ref,
    info, extended, direction_ext, amplitude, power_pad, shifted, coverage, patch, waves, stacked, far,
    deposit, fold, fold_x, fold_y, fold_z, corner_y, corner_z, energy_send, energy_recv, sums_x, sums_y,
    load_sem, info_sem, halo_sem, fold_sem, energy_sem, sums_sem,
):
    tile = object_hbm.shape[1]
    size = gain_ref.shape[0]
    modes = probe_ref.shape[0]
    slots = patterns_ref.shape[0]
    my_scan, my_obj = lax.axis_index("scan"), lax.axis_index("obj")
    top, middle, bottom = pl.ds(0, tile), pl.ds(tile, tile), pl.ds(2 * tile, tile)

    def at(k, c):
        return {
            "scan": lax.rem(my_scan + (c + n_scan), n_scan),
            "obj": lax.rem(my_obj + (k + n_obj), n_obj),
        }

    def remote(source, target, sems, index, device):
        return pltpu.make_async_remote_copy(
            src_ref=source, dst_ref=target, send_sem=sems.at[(0,) + index],
            recv_sem=sems.at[(1,) + index], device_id=device, device_id_type=MESH,
        )

    pairs = (
        (object_hbm, extended.at[1, :, middle, :]), (centres_hbm, centres_ref), (live_hbm, live_ref),
        (patterns_hbm, patterns_ref), (gain_hbm, gain_ref), (mask_hbm, mask_ref),
        (probe_hbm, probe_ref), (table_hbm, table_ref),
    )
    loads = [
        pltpu.make_async_copy(source, target, load_sem.at[n]) for n, (source, target) in enumerate(pairs)
    ]
    run = n_scan // 2
    my_run, my_place = my_scan // run, lax.rem(my_scan, run)
    in_run = [
        {"scan": my_run * run + lax.rem(my_place + other, run), "obj": my_obj} for other in range(1, run)
    ]
    across = [at(k, c) for c in (0, run) for k in range(n_obj) if k or c]
    partners = in_run + across + [at(0, -1), at(0, 1)] + [at(k, c) for k, c in AROUND if k and c]
    barrier = pltpu.get_barrier_semaphore()
    for partner in partners:
        pl.semaphore_signal(barrier, inc=1, device_id=partner, device_id_type=MESH)
    for load in loads:
        load.start()
    pl.semaphore_wait(barrier, len(partners))

    odd = lax.rem(my_obj, 2)
    near_start = pl.multiple_of(2 * tile * (1 - odd), tile)
    far_start = pl.multiple_of(2 * tile * odd, tile)
    near, far_rows = pl.ds(near_start, tile), pl.ds(far_start, tile)
    pair_step, pass_step = 1 - 2 * odd, 2 - 4 * odd

    turn_right, turn_left = my_place == run - 1, my_place == 0
    on_right, on_left = jnp.logical_not(turn_right), jnp.logical_not(turn_left)
    turns = ((2, 1, turn_right), (0, -1, turn_left))

    def when(condition, act):
        if condition is None:
            act()
        else:
            pl.when(condition)(act)

    class Copy:
        def __init__(self, copy, sends=None, receives=None):
            self.start = lambda: when(sends, copy.start)
            self.wait_send = lambda: when(sends, copy.wait_send)
            self.wait_recv = lambda: when(receives, copy.wait_recv)

        def wait(self):
            self.wait_recv()
            self.wait_send()

    def send_sideways(wide, phase, plane, rows, first, corner):
        mine = wide.at[1, plane, rows, :]
        pair = (
            Copy(
                remote(mine, wide.at[0, plane, rows, :], halo_sem, (phase, first), at(0, 1)),
                *((on_right, on_left) if corner else ()),
            ),
            Copy(
                remote(mine, wide.at[2, plane, rows, :], halo_sem, (phase, first + 1), at(0, -1)),
                *((on_left, on_right) if corner else ()),
            ),
        )
        for copy in pair:
            copy.start()
        return pair

    depth = tile // PARTS
    pieces = [(plane, part) for plane in range(2) for part in range(PARTS)]
    count = len(pieces)

    def piece_rows(start, part):
        return pl.ds(pl.multiple_of(start + part * depth, depth), depth)

    def start_gather(wide, phase):
        direct, corners = [], []
        for n, (plane, part) in enumerate(pieces):
            mine = wide.at[1, plane, piece_rows(tile, part), :]
            there = piece_rows(far_start, part)
            direct.append(remote(mine, wide.at[1, plane, there, :], halo_sem, (phase, n), at(pair_step, 0)))
            direct[n].start()
            corners.append([
                Copy(
                    remote(
                        mine, wide.at[2 - column, plane, there, :],
                        halo_sem, (phase, 8 * count + 2 * n + side), at(pair_step, step),
                    ),
                    turn, turns[1 - side][2],
                )
                for side, (column, step, turn) in enumerate(turns)
            ])
            for copy in corners[n]:
                copy.start()
        beside = [send_sideways(wide, phase, plane, middle, 2 * count + 2 * plane, False) for plane in range(2)]
        return direct, corners, beside

    def pass_near(wide, phase, state):
        direct, corners, beside = state
        passed = []
        for n, (plane, part) in enumerate(pieces):
            here, there = piece_rows(near_start, part), piece_rows(far_start, part)
            direct[n].wait_recv()
            passed.append(Copy(remote(
                wide.at[1, plane, here, :], wide.at[1, plane, there, :],
                halo_sem, (phase, count + n), at(pass_step, 0),
            )))
            passed[-1].start()
            beside.append(send_sideways(wide, phase, plane, here, 4 * count + 2 * n, True))
        for n, (plane, part) in enumerate(pieces):
            here, there = piece_rows(near_start, part), piece_rows(far_start, part)
            for side, (column, step, turn) in enumerate(turns):
                corners[n][1 - side].wait_recv()
                passed.append(Copy(
                    remote(
                        wide.at[column, plane, here, :], wide.at[column, plane, there, :],
                        halo_sem, (phase, 10 * count + 2 * n + side), at(pass_step, 0),
                    ),
                    turn, turn,
                ))
                passed[-1].start()
        return passed

    def pass_far(wide, phase, state, passed):
        for n, (plane, part) in enumerate(pieces):
            passed[n].wait_recv()
            state[2].append(send_sideways(wide, phase, plane, piece_rows(far_start, part), 6 * count + 2 * n, True))

    def finish_gather(state, passed):
        direct, corners, beside = state
        for pair in beside:
            for copy in pair:
                copy.wait_recv()
        for copy in passed[count:]:
            copy.wait_recv()
        return direct + passed + [copy for pair in corners + beside for copy in pair]

    loads[0].wait()
    state = start_gather(extended, 0)

    loads[1].wait()
    loads[2].wait()
    for slot in range(slots):
        info[4, 2 * slot] = centres_ref[slot, 0]
        info[4, 2 * slot + 1] = centres_ref[slot, 1]
    info[4, 2 * slots] = live_ref[0]
    info_copies = [
        remote(info.at[4], info.at[8 - n], info_sem, (n,), at(k, c))
        for n, (k, c) in enumerate(AROUND) if n != 4
    ]
    for copy in info_copies:
        copy.start()

    for load in loads[3:6]:
        load.wait()
    gain, defect = gain_ref[...], mask_ref[...] == 1
    for slot in range(slots):
        corrected = patterns_ref[slot].astype(jnp.float32) * gain
        mean = 0.25 * (
            pltpu.roll(corrected, 1, 0) + pltpu.roll(corrected, size - 1, 0)
            + pltpu.roll(corrected, 1, 1) + pltpu.roll(corrected, size - 1, 1)
        )
        amplitude[slot] = jnp.sqrt(jnp.where(defect, mean, corrected))
    loads[6].wait()
    power = jnp.zeros((size, size), jnp.float32)
    for mode in range(modes):
        power = power + probe_ref[mode, :, :size] ** 2 + probe_ref[mode, :, size:] ** 2
    power_pad[...] = jnp.zeros_like(power_pad)
    for half in range(2):
        power_pad[half, tile : tile + size, :] = power[:, half * tile : (half + 1) * tile]
    for slot in range(slots):
        for column in range(3):
            for plane in range(2):
                zeros = jnp.zeros((tile, tile), jnp.float32)
                deposit[slot, column, plane, :tile, :] = zeros
                deposit[slot, column, plane, tile + size :, :] = zeros
    passed = pass_near(extended, 0, state)
    loads[7].wait()

    place = lax.broadcasted_iota(jnp.int32, (size, size), 0)
    taken = lax.broadcasted_iota(jnp.int32, (size, size), 1)
    half_size = size // 2
    by_row = jnp.where(place < half_size, 2 * place, 2 * place - (size - 1)) == taken
    by_column = jnp.where(taken < half_size, 2 * taken, 2 * taken - (size - 1)) == place
    by_row, by_column = by_row.astype(jnp.float32), by_column.astype(jnp.float32)
    for slot in range(slots):
        ordered = jnp.dot(amplitude[slot], by_column, precision=lax.Precision.HIGHEST)
        amplitude[slot] = jnp.dot(by_row, ordered, precision=lax.Precision.HIGHEST)

    for copy in info_copies:
        copy.wait()
    pass_far(extended, 0, state, passed)
    lane = lax.broadcasted_iota(jnp.int32, (tile, tile), 1)
    total = jnp.zeros((tile, tile), jnp.float32)
    for n, (k, c) in enumerate(AROUND):
        for slot in range(slots):
            row, column = info[n, 2 * slot], info[n, 2 * slot + 1]
            alive = (slot < info[n, 2 * slots]).astype(jnp.float32)
            rows = pl.ds(2 * tile - tile * k - row, tile)
            low, high = (pltpu.roll(power_pad[half, rows, :], column, 1) for half in range(2))
            if c == 0:
                moved = jnp.where(lane < column, low, high)
            elif c < 0:
                moved = jnp.where(lane < column, high, 0.0)
            else:
                moved = jnp.where(lane < column, 0.0, low)
            shifted[n, slot] = moved
            total = total + moved * alive
    coverage[...] = total
    sent = finish_gather(state, passed)

    wide_lane = lax.broadcasted_iota(jnp.int32, (size, tile), 1)

    def product(left, right):
        return jnp.dot(left, right, preferred_element_type=jnp.float32)

    def take_patch(slot):
        row, column = centres_ref[slot, 0], centres_ref[slot, 1]
        back_shift = lax.rem(tile - column, tile)
        close = wide_lane < tile - column
        for plane in range(2):
            first, second, third = (
                pltpu.roll(extended[block, plane, pl.ds(row, size), :], back_shift, 1) for block in range(3)
            )
            patch[slot, plane, :, :tile] = jnp.where(close, first, second)
            patch[slot, plane, :, tile:] = jnp.where(close, second, third)

    def exit_waves(slot):
        for mode in range(modes):
            real, imag = patch[slot, 0], patch[slot, 1]
            probe_real, probe_imag = probe_ref[mode, :, :size], probe_ref[mode, :, size:]
            for part, wave in enumerate((real * probe_real - imag * probe_imag, real * probe_imag + imag * probe_real)):
                low, high = wave[:, :tile], wave[:, tile:]
                first = part * tile
                waves[slot, mode, :, first : first + tile] = (low + high).astype(jnp.bfloat16)
                waves[slot, mode, :, size + first : size + first + tile] = (low - high).astype(jnp.bfloat16)

    def along_columns(slot):
        for mode in range(modes):
            for parity in range(2):
                half = product(waves[slot, mode, :, parity * size : (parity + 1) * size], table_ref[parity])
                lanes = slice(parity * tile, (parity + 1) * tile)
                for place, value in enumerate((half[:tile] + half[tile:], half[:tile] - half[tile:])):
                    value = value.astype(jnp.bfloat16)
                    stacked[slot, mode, place * size : place * size + tile, lanes] = value[:, :tile]
                    stacked[slot, mode, place * size + tile : (place + 1) * size, lanes] = value[:, tile:]

    def along_rows(slot):
        for mode in range(modes):
            for parity in range(2):
                rows = slice(parity * size, (parity + 1) * size)
                far[slot, mode, rows, :] = product(table_ref[2 + parity], stacked[slot, mode, rows, :])

    def revise(slot):
        for parity in range(2):
            parts = [slice(parity * size + part * tile, parity * size + (part + 1) * tile) for part in range(2)]
            model = jnp.zeros((tile, size), jnp.float32)
            for mode in range(modes):
                model = model + far[slot, mode, parts[0], :] ** 2 + far[slot, mode, parts[1], :] ** 2
            ratio = amplitude[slot, parity * tile : (parity + 1) * tile, :] * lax.rsqrt(jnp.maximum(model, 0.25))
            for mode in range(modes):
                for part in parts:
                    stacked[slot, mode, part, :] = (far[slot, mode, part, :] * ratio).astype(jnp.bfloat16)

    def back_along_rows(slot):
        for mode in range(modes):
            even = product(table_ref[0], stacked[slot, mode, :size, :])
            odd = product(table_ref[1], stacked[slot, mode, size:, :])
            for rows, value in ((slice(0, tile), even + odd), (slice(tile, size), even - odd)):
                value = value.astype(jnp.bfloat16)
                for parity in range(2):
                    lanes = slice(parity * tile, (parity + 1) * tile)
                    waves[slot, mode, rows, parity * size : parity * size + tile] = value[:tile, lanes]
                    waves[slot, mode, rows, parity * size + tile : (parity + 1) * size] = value[tile:, lanes]

    def back_along_columns(slot, start):
        rows = pl.ds(pl.multiple_of(start, tile), tile)
        placed_rows = pl.ds(pl.multiple_of(start + tile, tile), tile)
        even = product(waves[slot, :, rows, :size].reshape(modes * tile, size), table_ref[2])
        odd_part = product(waves[slot, :, rows, size:].reshape(modes * tile, size), table_ref[3])
        updates = []
        for half, wave in enumerate((even + odd_part, even - odd_part)):
            lanes = slice(half * tile, (half + 1) * tile)
            power = power_pad[half, placed_rows, :]
            real_sum, imag_sum = (-power * patch[slot, plane, rows, lanes] for plane in range(2))
            for mode in range(modes):
                real, imag = wave[mode * tile : (mode + 1) * tile, :tile], wave[mode * tile : (mode + 1) * tile, tile:]
                probe_real = probe_ref[mode, rows, lanes]
                probe_imag = probe_ref[mode, rows, size + half * tile : size + (half + 1) * tile]
                real_sum = real_sum + (real * probe_real + imag * probe_imag)
                imag_sum = imag_sum + (imag * probe_real - real * probe_imag)
            updates.append((real_sum, imag_sum))
        column = centres_ref[slot, 1]
        alive = jnp.where(slot < live_ref[0], 1.0, 0.0)
        before = lane < column
        for plane in range(2):
            low, high = (pltpu.roll(updates[half][plane] * alive, column, 1) for half in range(2))
            deposit[slot, 0, plane, placed_rows, :] = jnp.where(before, 0.0, low)
            deposit[slot, 1, plane, placed_rows, :] = jnp.where(before, low, high)
            deposit[slot, 2, plane, placed_rows, :] = jnp.where(before, high, 0.0)

    stages = (take_patch, exit_waves, along_columns, along_rows, revise, back_along_rows)

    row_id = lax.broadcasted_iota(jnp.int32, (8, tile), 0)

    def as_row(value, row):
        return jnp.where(row_id == row, jnp.sum(value, axis=0, keepdims=True), 0.0)

    live_number = live_ref[0].astype(jnp.float32)

    def sum_start(table, mine, base, devices, iteration):
        copies = []
        for n, device in enumerate(devices):
            block = table.at[iteration, mine]
            copies.append(remote(block, block, sums_sem, (iteration, base + n), device))
            copies[-1].start()
        return copies

    lane_id = lax.broadcasted_iota(jnp.int32, (1, tile), 1)

    def whole(value):
        return jnp.sum(jnp.sum(value, axis=0, keepdims=True), axis=1, keepdims=True)

    energy_copies, scales = [[] for _ in range(ITERS)], []

    def raw_energies(iteration):
        for copy in energy_copies[iteration]:
            copy.wait()
        total = jnp.sum(jnp.sum(energy_recv[iteration], axis=0), axis=1, keepdims=True)
        in_row = jnp.sum(jnp.where(row_id == lane[:8], total, 0.0), axis=0, keepdims=True)
        return jnp.where(lane_id < live_ref[0], in_row, 0.0)

    for iteration in range(ITERS):
        for stage in stages:
            for slot in range(slots):
                stage(slot)
        for slot in range(slots):
            back_along_columns(slot, tile * odd)

        def gathered(column, plane, start, length):
            summed = None
            for slot in range(slots):
                term = deposit[slot, column, plane, pl.ds(start + tile - centres_ref[slot, 0], length), :]
                summed = term if summed is None else summed + term
            return summed

        sides, corners = {}, []
        outer = [(name, *piece) for name in ("far", "near") for piece in pieces]
        starts = {"far": far_start, "near": near_start, "middle": tile}
        order = [(place, *entry) for place, entry in enumerate(outer + [("middle", 0, None), ("middle", 1, None)])]

        def send_out(place, name, plane, part):
            if name == "middle":
                rows, start, length = middle, tile, tile
            else:
                rows, start, length = piece_rows(starts[name], part), starts[name] + part * depth, depth
            pair = []
            for side, (column, step, turn) in enumerate(turns):
                fold[iteration, column, plane, rows, :] = gathered(column, plane, start, length)
                if name == "far":
                    corners.append(Copy(
                        remote(
                            fold.at[iteration, column, plane, rows, :],
                            corner_z.at[iteration, side, plane, piece_rows(0, part), :],
                            fold_sem, (iteration, 8 * count + 2 * place + side), at(-pass_step, 0),
                        ),
                        turn, turn,
                    ))
                    corners[-1].start()
                copy = Copy(
                    remote(
                        fold.at[iteration, column, plane, rows, :], fold_x.at[iteration, side, plane, rows, :],
                        fold_sem, (iteration, 2 * place + side), at(0, step),
                    ),
                    *(() if name == "middle" else ((on_right, on_left), (on_left, on_right))[side]),
                )
                copy.start()
                pair.append(copy)
            sides[name, plane, part] = pair

        for entry in order[:count]:
            send_out(*entry)
        for slot in range(slots):
            back_along_columns(slot, tile * (1 - odd))
        for entry in order[count:]:
            send_out(*entry)
        for name in starts:
            for plane in range(2):
                fold[iteration, 1, plane, pl.ds(starts[name], tile), :] = gathered(1, plane, starts[name], tile)

        def add_sides(name, plane, part):
            rows = middle if name == "middle" else piece_rows(starts[name], part)
            for side, copy in enumerate(sides[name, plane, part]):
                def add(side=side):
                    fold[iteration, 1, plane, rows, :] += fold_x[iteration, side, plane, rows, :]

                copy.wait_recv()
                when(None if name == "middle" else (on_left, on_right)[side], add)

        passed_on, folds, straight = [], [], []
        for n, (plane, part) in enumerate(pieces):
            add_sides("far", plane, part)
            passed_on.append(remote(
                fold.at[iteration, 1, plane, piece_rows(far_start, part), :],
                fold_z.at[iteration, plane, piece_rows(0, part), :],
                fold_sem, (iteration, 6 * count + n), at(-pass_step, 0),
            ))
            passed_on[n].start()
        for n, (plane, part) in enumerate(pieces):
            here, rows = piece_rows(0, part), piece_rows(near_start, part)
            for side, (column, step, turn) in enumerate(turns):
                def add_corner(plane=plane, side=side, column=column, here=here, rows=rows):
                    fold[iteration, column, plane, rows, :] += corner_z[iteration, side, plane, here, :]

                corners[2 * n + side].wait_recv()
                when(turn, add_corner)
                straight.append(Copy(
                    remote(
                        fold.at[iteration, column, plane, rows, :], corner_y.at[iteration, side, plane, here, :],
                        fold_sem, (iteration, 10 * count + 2 * n + side), at(pair_step, step),
                    ),
                    turn, turns[1 - side][2],
                ))
                straight[-1].start()
        for n, (plane, part) in enumerate(pieces):
            here, rows = piece_rows(0, part), piece_rows(near_start, part)
            add_sides("near", plane, part)
            passed_on[n].wait_recv()
            fold[iteration, 1, plane, rows, :] += fold_z[iteration, plane, here, :]
            folds.append(remote(
                fold.at[iteration, 1, plane, rows, :], fold_y.at[iteration, plane, here, :],
                fold_sem, (iteration, 7 * count + n), at(pair_step, 0),
            ))
            folds[n].start()
        for plane in range(2):
            add_sides("middle", plane, None)
        for n, (plane, part) in enumerate(pieces):
            here, rows = piece_rows(0, part), piece_rows(tile, part)
            for side in range(2):
                def add_straight(plane=plane, side=side, here=here, rows=rows):
                    fold[iteration, 1, plane, rows, :] += corner_y[iteration, side, plane, here, :]

                straight[2 * n + side].wait_recv()
                when(turns[1 - side][2], add_straight)
        cover = coverage[...]
        gradient, moved = [], []
        for plane in range(2):
            for part in range(PARTS):
                folds[plane * PARTS + part].wait_recv()
            gradient.append(fold[iteration, 1, plane, middle, :] + fold_y[iteration, plane])
            moved.append(gradient[plane] / (cover + 0.5))
            direction_ext[iteration, 1, plane, middle, :] = moved[plane]
        last = iteration == ITERS - 1
        if not last:
            state = start_gather(direction_ext.at[iteration], 1 + iteration)

        squares = moved[0] * moved[0] + moved[1] * moved[1]
        numerator = whole(moved[0] * gradient[0] + moved[1] * gradient[1])
        denominator = whole(cover * squares)
        sums_x[iteration, my_place] = jnp.where(
            lane_id == 0, numerator, jnp.where(lane_id == 1, denominator, jnp.where(lane_id == 2, live_number, 0.0))
        )
        first_sums = sum_start(sums_x, my_place, 0, in_run, iteration)
        if not last:
            passed = pass_near(direction_ext.at[iteration], 1 + iteration, state)
        for n, (k, c) in enumerate(AROUND):
            block = jnp.zeros((8, tile), jnp.float32)
            for slot in range(slots):
                block = block + as_row(squares * shifted[n, slot], slot)
            if n == 4:
                energy_recv[iteration, n] = block
            else:
                energy_send[iteration, n] = block
                copy = remote(
                    energy_send.at[iteration, n], energy_recv.at[iteration, n],
                    energy_sem, (iteration, n), at(k, c),
                )
                copy.start()
                energy_copies[iteration].append(copy)
        for copy in first_sums:
            copy.wait()
        mine = my_run * n_obj + my_obj
        sums_y[iteration, mine] = jnp.sum(sums_x[iteration], axis=0)
        second_sums = sum_start(sums_y, mine, run, across, iteration)
        if not last:
            pass_far(direction_ext.at[iteration], 1 + iteration, state, passed)
        for copy in sent + [copy for pair in sides.values() for copy in pair]:
            copy.wait_send()
        for copy in folds + passed_on + corners + straight:
            copy.wait_send()
        if last:
            raw = [raw_energies(each) for each in range(ITERS)]
        for copy in second_sums:
            copy.wait()
        everywhere = jnp.sum(sums_y[iteration], axis=0)
        numerator, denominator, live_total = (everywhere[:, n : n + 1] for n in range(3))
        step = numerator / denominator
        scales.append((step, live_total / denominator))
        if not last:
            sent = finish_gather(state, passed)
            extended[...] = extended[...] + step.reshape(1, 1, 1, 1) * direction_ext[iteration]
        else:
            object_out[...] = (
                extended[1, :, middle, :] + step.reshape(1, 1, 1) * direction_ext[iteration, 1, :, middle, :]
            )
    step_row = jnp.zeros((1, tile), jnp.float32)
    for iteration in range(ITERS):
        step, scale = scales[iteration]
        step_row = jnp.where(lane_id == iteration, step, step_row)
        energies_out[iteration : iteration + 1, :] = (raw[iteration] * scale)[:, :slots]
    steps_out[...] = step_row[0, :ITERS]


def on_device(n_scan, n_obj, object_field, probe_modes, patterns, gain_map, defect_mask, probe_centres, live_counts):
    tile = object_field.shape[1]
    modes, size = probe_modes.shape[0], probe_modes.shape[1]
    slots = patterns.shape[0]
    extent = tile + size
    table = transform_tables(size)
    f32 = jnp.float32
    vmem = pl.BlockSpec(memory_space=pltpu.VMEM)
    hbm = pl.BlockSpec(memory_space=pltpu.HBM)
    flops = ITERS * slots * modes * 4 * 2 * (2 * size) * size * size
    outputs = pl.pallas_call(
        functools.partial(kernel, n_scan, n_obj),
        out_shape=(
            jax.ShapeDtypeStruct(object_field.shape, f32),
            jax.ShapeDtypeStruct((ITERS,), f32),
            jax.ShapeDtypeStruct((ITERS, slots), f32),
        ),
        in_specs=[hbm] * 8,
        out_specs=(vmem, vmem, vmem),
        scratch_shapes=[
            pltpu.VMEM(probe_modes.shape, f32),
            pltpu.VMEM(patterns.shape, patterns.dtype),
            pltpu.VMEM(gain_map.shape, f32),
            pltpu.VMEM(defect_mask.shape, jnp.int32),
            pltpu.VMEM(table.shape, table.dtype),
            pltpu.SMEM(probe_centres.shape, jnp.int32),
            pltpu.SMEM(live_counts.shape, jnp.int32),
            pltpu.SMEM((9, 128), jnp.int32),
            pltpu.VMEM((3, 2, extent, tile), f32),
            pltpu.VMEM((ITERS, 3, 2, extent, tile), f32),
            pltpu.VMEM((slots, size, size), f32),
            pltpu.VMEM((2, size + 2 * tile, tile), f32),
            pltpu.VMEM((9, slots, tile, tile), f32),
            pltpu.VMEM((tile, tile), f32),
            pltpu.VMEM((slots, 2, size, size), f32),
            pltpu.VMEM((slots, modes, size, 2 * size), jnp.bfloat16),
            pltpu.VMEM((slots, modes, 2 * size, size), jnp.bfloat16),
            pltpu.VMEM((slots, modes, 2 * size, size), f32),
            pltpu.VMEM((slots, 3, 2, size + 2 * tile, tile), f32),
            pltpu.VMEM((ITERS, 3, 2, extent, tile), f32),
            pltpu.VMEM((ITERS, 2, 2, extent, tile), f32),
            pltpu.VMEM((ITERS, 2, tile, tile), f32),
            pltpu.VMEM((ITERS, 2, tile, tile), f32),
            pltpu.VMEM((ITERS, 2, 2, tile, tile), f32),
            pltpu.VMEM((ITERS, 2, 2, tile, tile), f32),
            pltpu.VMEM((ITERS, 9, 8, tile), f32),
            pltpu.VMEM((ITERS, 9, 8, tile), f32),
            pltpu.VMEM((ITERS, n_scan // 2, 1, tile), f32),
            pltpu.VMEM((ITERS, 2 * n_obj, 1, tile), f32),
            pltpu.SemaphoreType.DMA((8,)),
            pltpu.SemaphoreType.DMA((2, 9)),
            pltpu.SemaphoreType.DMA((2, ITERS, 24 * PARTS)),
            pltpu.SemaphoreType.DMA((2, ITERS, 24 * PARTS)),
            pltpu.SemaphoreType.DMA((2, ITERS, 9)),
            pltpu.SemaphoreType.DMA((2, ITERS, n_scan // 2 + 2 * n_obj)),
        ],
        compiler_params=pltpu.CompilerParams(
            collective_id=0, has_side_effects=True, vmem_limit_bytes=55000 * 1024
        ),
        cost_estimate=pl.CostEstimate(flops=flops, bytes_accessed=8 * 1024 * 1024, transcendentals=0),
    )(object_field, probe_modes, patterns, gain_map, defect_mask, table, probe_centres, live_counts)
    return tuple(outputs)


def solution(mesh):
    placed = (
        P(None, "obj", "scan"),
        P(),
        P(("scan", "obj"), None, None),
        P(),
        P(),
        P(("scan", "obj"), None),
        P(("scan", "obj")),
    )
    return jax.shard_map(
        functools.partial(on_device, mesh.shape["scan"], mesh.shape["obj"]),
        mesh=mesh,
        in_specs=placed,
        out_specs=(P(None, "obj", "scan"), P(), P(None, ("scan", "obj"))),
        check_vma=False,
    )
```

```python
import functools

import jax
import jax.numpy as jnp
import numpy as np
from jax import lax
from jax.experimental import pallas as pl
from jax.experimental.pallas import tpu as pltpu
from jax.sharding import PartitionSpec as P

ITERS = 2
PARTS = 2
MESH = pl.DeviceIdType.MESH
AROUND = [(k, c) for k in (-1, 0, 1) for c in (-1, 0, 1)]


def transform_tables(size):
    indices = np.arange(size, dtype=np.int32)
    phase = (indices[:, None] * indices[None, :] % size).astype(np.float32)
    angles = phase * np.float32(2.0 * 3.141592653589793 / size)
    norm = np.float32(size ** (-0.5))
    cosine, sine = np.cos(angles) * norm, np.sin(angles) * norm
    tables = []
    for first in range(2):
        c, s = cosine[: size // 2, first::2], sine[: size // 2, first::2]
        tables.append(np.block([[c, -s], [s, c]]))
    for first in range(2):
        c, s = cosine[first::2, : size // 2], sine[first::2, : size // 2]
        tables.append(np.block([[c, s], [-s, c]]))
    return jnp.asarray(np.stack(tables)).astype(jnp.bfloat16)


def kernel(
    n_scan, n_obj,
    object_hbm, probe_hbm, patterns_hbm, gain_hbm, mask_hbm, table_hbm, centres_hbm, live_hbm,
    object_out, steps_out, energies_out,
    probe_ref, patterns_ref, gain_ref, mask_ref, table_ref, centres_ref, live_ref,
    info, extended, direction_ext, amplitude, power_pad, shifted, coverage, patch, waves, stacked, far,
    deposit, fold, fold_x, fold_y, fold_z, corner_y, corner_z, energy_send, energy_recv, sums_x, sums_y,
    load_sem, info_sem, halo_sem, fold_sem, energy_sem, sums_sem,
):
    tile = object_hbm.shape[1]
    size = gain_ref.shape[0]
    modes = probe_ref.shape[0]
    slots = patterns_ref.shape[0]
    my_scan, my_obj = lax.axis_index("scan"), lax.axis_index("obj")
    top, middle, bottom = pl.ds(0, tile), pl.ds(tile, tile), pl.ds(2 * tile, tile)

    def at(k, c):
        return {
            "scan": lax.rem(my_scan + (c + n_scan), n_scan),
            "obj": lax.rem(my_obj + (k + n_obj), n_obj),
        }

    def remote(source, target, sems, index, device):
        return pltpu.make_async_remote_copy(
            src_ref=source, dst_ref=target, send_sem=sems.at[(0,) + index],
            recv_sem=sems.at[(1,) + index], device_id=device, device_id_type=MESH,
        )

    pairs = (
        (object_hbm, extended.at[1, :, middle, :]), (centres_hbm, centres_ref), (live_hbm, live_ref),
        (patterns_hbm, patterns_ref), (gain_hbm, gain_ref), (mask_hbm, mask_ref),
        (probe_hbm, probe_ref), (table_hbm, table_ref),
    )
    loads = [
        pltpu.make_async_copy(source, target, load_sem.at[n]) for n, (source, target) in enumerate(pairs)
    ]
    run = n_scan // 2
    my_run, my_place = my_scan // run, lax.rem(my_scan, run)
    in_run = [
        {"scan": my_run * run + lax.rem(my_place + other, run), "obj": my_obj} for other in range(1, run)
    ]
    across = [at(k, c) for c in (0, run) for k in range(n_obj) if k or c]
    partners = in_run + across + [at(0, -1), at(0, 1)] + [at(k, c) for k, c in AROUND if k and c]
    barrier = pltpu.get_barrier_semaphore()
    for partner in partners:
        pl.semaphore_signal(barrier, inc=1, device_id=partner, device_id_type=MESH)
    for load in loads:
        load.start()
    pl.semaphore_wait(barrier, len(partners))

    odd = lax.rem(my_obj, 2)
    near_start = pl.multiple_of(2 * tile * (1 - odd), tile)
    far_start = pl.multiple_of(2 * tile * odd, tile)
    near, far_rows = pl.ds(near_start, tile), pl.ds(far_start, tile)
    pair_step, pass_step = 1 - 2 * odd, 2 - 4 * odd

    turn_right, turn_left = my_place == run - 1, my_place == 0
    on_right, on_left = jnp.logical_not(turn_right), jnp.logical_not(turn_left)
    turns = ((2, 1, turn_right), (0, -1, turn_left))

    def when(condition, act):
        if condition is None:
            act()
        else:
            pl.when(condition)(act)

    class Copy:
        def __init__(self, copy, sends=None, receives=None):
            self.start = lambda: when(sends, copy.start)
            self.wait_send = lambda: when(sends, copy.wait_send)
            self.wait_recv = lambda: when(receives, copy.wait_recv)

        def wait(self):
            self.wait_recv()
            self.wait_send()

    def send_sideways(wide, phase, plane, rows, first, corner):
        mine = wide.at[1, plane, rows, :]
        pair = (
            Copy(
                remote(mine, wide.at[0, plane, rows, :], halo_sem, (phase, first), at(0, 1)),
                *((on_right, on_left) if corner else ()),
            ),
            Copy(
                remote(mine, wide.at[2, plane, rows, :], halo_sem, (phase, first + 1), at(0, -1)),
                *((on_left, on_right) if corner else ()),
            ),
        )
        for copy in pair:
            copy.start()
        return pair

    depth = tile // PARTS
    pieces = [(plane, part) for plane in range(2) for part in range(PARTS)]
    count = len(pieces)

    def piece_rows(start, part):
        return pl.ds(pl.multiple_of(start + part * depth, depth), depth)

    def start_gather(wide, phase):
        direct, corners = [], []
        for n, (plane, part) in enumerate(pieces):
            mine = wide.at[1, plane, piece_rows(tile, part), :]
            there = piece_rows(far_start, part)
            direct.append(remote(mine, wide.at[1, plane, there, :], halo_sem, (phase, n), at(pair_step, 0)))
            direct[n].start()
            corners.append([
                Copy(
                    remote(
                        mine, wide.at[2 - column, plane, there, :],
                        halo_sem, (phase, 8 * count + 2 * n + side), at(pair_step, step),
                    ),
                    turn, turns[1 - side][2],
                )
                for side, (column, step, turn) in enumerate(turns)
            ])
            for copy in corners[n]:
                copy.start()
        beside = [send_sideways(wide, phase, plane, middle, 2 * count + 2 * plane, False) for plane in range(2)]
        return direct, corners, beside

    def pass_near(wide, phase, state):
        direct, corners, beside = state
        passed = []
        for n, (plane, part) in enumerate(pieces):
            here, there = piece_rows(near_start, part), piece_rows(far_start, part)
            direct[n].wait_recv()
            passed.append(Copy(remote(
                wide.at[1, plane, here, :], wide.at[1, plane, there, :],
                halo_sem, (phase, count + n), at(pass_step, 0),
            )))
            passed[-1].start()
            beside.append(send_sideways(wide, phase, plane, here, 4 * count + 2 * n, True))
        for n, (plane, part) in enumerate(pieces):
            here, there = piece_rows(near_start, part), piece_rows(far_start, part)
            for side, (column, step, turn) in enumerate(turns):
                corners[n][1 - side].wait_recv()
                passed.append(Copy(
                    remote(
                        wide.at[column, plane, here, :], wide.at[column, plane, there, :],
                        halo_sem, (phase, 10 * count + 2 * n + side), at(pass_step, 0),
                    ),
                    turn, turn,
                ))
                passed[-1].start()
        return passed

    def pass_far(wide, phase, state, passed):
        for n, (plane, part) in enumerate(pieces):
            passed[n].wait_recv()
            state[2].append(send_sideways(wide, phase, plane, piece_rows(far_start, part), 6 * count + 2 * n, True))

    def finish_gather(state, passed):
        direct, corners, beside = state
        for pair in beside:
            for copy in pair:
                copy.wait_recv()
        for copy in passed[count:]:
            copy.wait_recv()
        return direct + passed + [copy for pair in corners + beside for copy in pair]

    loads[0].wait()
    state = start_gather(extended, 0)

    loads[1].wait()
    loads[2].wait()
    for slot in range(slots):
        info[4, 2 * slot] = centres_ref[slot, 0]
        info[4, 2 * slot + 1] = centres_ref[slot, 1]
    info[4, 2 * slots] = live_ref[0]
    info_copies = [
        remote(info.at[4], info.at[8 - n], info_sem, (n,), at(k, c))
        for n, (k, c) in enumerate(AROUND) if n != 4
    ]
    for copy in info_copies:
        copy.start()

    for load in loads[3:6]:
        load.wait()
    gain, defect = gain_ref[...], mask_ref[...] == 1
    for slot in range(slots):
        corrected = patterns_ref[slot].astype(jnp.float32) * gain
        mean = 0.25 * (
            pltpu.roll(corrected, 1, 0) + pltpu.roll(corrected, size - 1, 0)
            + pltpu.roll(corrected, 1, 1) + pltpu.roll(corrected, size - 1, 1)
        )
        amplitude[slot] = jnp.sqrt(jnp.where(defect, mean, corrected))
    loads[6].wait()
    power = jnp.zeros((size, size), jnp.float32)
    for mode in range(modes):
        power = power + probe_ref[mode, :, :size] ** 2 + probe_ref[mode, :, size:] ** 2
    power_pad[...] = jnp.zeros_like(power_pad)
    for half in range(2):
        power_pad[half, tile : tile + size, :] = power[:, half * tile : (half + 1) * tile]
    for slot in range(slots):
        for column in range(3):
            for plane in range(2):
                zeros = jnp.zeros((tile, tile), jnp.float32)
                deposit[slot, column, plane, :tile, :] = zeros
                deposit[slot, column, plane, tile + size :, :] = zeros
    passed = pass_near(extended, 0, state)
    loads[7].wait()

    place = lax.broadcasted_iota(jnp.int32, (size, size), 0)
    taken = lax.broadcasted_iota(jnp.int32, (size, size), 1)
    half_size = size // 2
    by_row = jnp.where(place < half_size, 2 * place, 2 * place - (size - 1)) == taken
    by_column = jnp.where(taken < half_size, 2 * taken, 2 * taken - (size - 1)) == place
    by_row, by_column = by_row.astype(jnp.float32), by_column.astype(jnp.float32)
    for slot in range(slots):
        ordered = jnp.dot(amplitude[slot], by_column, precision=lax.Precision.HIGHEST)
        amplitude[slot] = jnp.dot(by_row, ordered, precision=lax.Precision.HIGHEST)

    for copy in info_copies:
        copy.wait()
    pass_far(extended, 0, state, passed)
    lane = lax.broadcasted_iota(jnp.int32, (tile, tile), 1)
    total = jnp.zeros((tile, tile), jnp.float32)
    for n, (k, c) in enumerate(AROUND):
        for slot in range(slots):
            row, column = info[n, 2 * slot], info[n, 2 * slot + 1]
            alive = (slot < info[n, 2 * slots]).astype(jnp.float32)
            rows = pl.ds(2 * tile - tile * k - row, tile)
            low, high = (pltpu.roll(power_pad[half, rows, :], column, 1) for half in range(2))
            if c == 0:
                moved = jnp.where(lane < column, low, high)
            elif c < 0:
                moved = jnp.where(lane < column, high, 0.0)
            else:
                moved = jnp.where(lane < column, 0.0, low)
            shifted[n, slot] = moved
            total = total + moved * alive
    coverage[...] = total
    sent = finish_gather(state, passed)

    wide_lane = lax.broadcasted_iota(jnp.int32, (size, tile), 1)

    def product(left, right):
        return jnp.dot(left, right, preferred_element_type=jnp.float32)

    def take_patch(slot):
        row, column = centres_ref[slot, 0], centres_ref[slot, 1]
        back_shift = lax.rem(tile - column, tile)
        close = wide_lane < tile - column
        for plane in range(2):
            first, second, third = (
                pltpu.roll(extended[block, plane, pl.ds(row, size), :], back_shift, 1) for block in range(3)
            )
            patch[slot, plane, :, :tile] = jnp.where(close, first, second)
            patch[slot, plane, :, tile:] = jnp.where(close, second, third)

    def exit_waves(slot):
        for mode in range(modes):
            real, imag = patch[slot, 0], patch[slot, 1]
            probe_real, probe_imag = probe_ref[mode, :, :size], probe_ref[mode, :, size:]
            for part, wave in enumerate((real * probe_real - imag * probe_imag, real * probe_imag + imag * probe_real)):
                low, high = wave[:, :tile], wave[:, tile:]
                first = part * tile
                waves[slot, mode, :, first : first + tile] = (low + high).astype(jnp.bfloat16)
                waves[slot, mode, :, size + first : size + first + tile] = (low - high).astype(jnp.bfloat16)

    def along_columns(slot):
        for mode in range(modes):
            for parity in range(2):
                half = product(waves[slot, mode, :, parity * size : (parity + 1) * size], table_ref[parity])
                lanes = slice(parity * tile, (parity + 1) * tile)
                for place, value in enumerate((half[:tile] + half[tile:], half[:tile] - half[tile:])):
                    value = value.astype(jnp.bfloat16)
                    stacked[slot, mode, place * size : place * size + tile, lanes] = value[:, :tile]
                    stacked[slot, mode, place * size + tile : (place + 1) * size, lanes] = value[:, tile:]

    def along_rows(slot):
        for mode in range(modes):
            for parity in range(2):
                rows = slice(parity * size, (parity + 1) * size)
                far[slot, mode, rows, :] = product(table_ref[2 + parity], stacked[slot, mode, rows, :])

    def revise(slot):
        for parity in range(2):
            parts = [slice(parity * size + part * tile, parity * size + (part + 1) * tile) for part in range(2)]
            model = jnp.zeros((tile, size), jnp.float32)
            for mode in range(modes):
                model = model + far[slot, mode, parts[0], :] ** 2 + far[slot, mode, parts[1], :] ** 2
            ratio = amplitude[slot, parity * tile : (parity + 1) * tile, :] * lax.rsqrt(jnp.maximum(model, 0.25))
            for mode in range(modes):
                for part in parts:
                    stacked[slot, mode, part, :] = (far[slot, mode, part, :] * ratio).astype(jnp.bfloat16)

    def back_along_rows(slot):
        for mode in range(modes):
            even = product(table_ref[0], stacked[slot, mode, :size, :])
            odd = product(table_ref[1], stacked[slot, mode, size:, :])
            for rows, value in ((slice(0, tile), even + odd), (slice(tile, size), even - odd)):
                value = value.astype(jnp.bfloat16)
                for parity in range(2):
                    lanes = slice(parity * tile, (parity + 1) * tile)
                    waves[slot, mode, rows, parity * size : parity * size + tile] = value[:tile, lanes]
                    waves[slot, mode, rows, parity * size + tile : (parity + 1) * size] = value[tile:, lanes]

    def back_along_columns(slot, start):
        rows = pl.ds(pl.multiple_of(start, tile), tile)
        placed_rows = pl.ds(pl.multiple_of(start + tile, tile), tile)
        even = product(waves[slot, :, rows, :size].reshape(modes * tile, size), table_ref[2])
        odd_part = product(waves[slot, :, rows, size:].reshape(modes * tile, size), table_ref[3])
        updates = []
        for half, wave in enumerate((even + odd_part, even - odd_part)):
            lanes = slice(half * tile, (half + 1) * tile)
            power = power_pad[half, placed_rows, :]
            real_sum, imag_sum = (-power * patch[slot, plane, rows, lanes] for plane in range(2))
            for mode in range(modes):
                real, imag = wave[mode * tile : (mode + 1) * tile, :tile], wave[mode * tile : (mode + 1) * tile, tile:]
                probe_real = probe_ref[mode, rows, lanes]
                probe_imag = probe_ref[mode, rows, size + half * tile : size + (half + 1) * tile]
                real_sum = real_sum + (real * probe_real + imag * probe_imag)
                imag_sum = imag_sum + (imag * probe_real - real * probe_imag)
            updates.append((real_sum, imag_sum))
        column = centres_ref[slot, 1]
        alive = jnp.where(slot < live_ref[0], 1.0, 0.0)
        before = lane < column
        for plane in range(2):
            low, high = (pltpu.roll(updates[half][plane] * alive, column, 1) for half in range(2))
            deposit[slot, 0, plane, placed_rows, :] = jnp.where(before, 0.0, low)
            deposit[slot, 1, plane, placed_rows, :] = jnp.where(before, low, high)
            deposit[slot, 2, plane, placed_rows, :] = jnp.where(before, high, 0.0)

    stages = (take_patch, exit_waves, along_columns, along_rows, revise, back_along_rows)

    row_id = lax.broadcasted_iota(jnp.int32, (8, tile), 0)

    def as_row(value, row):
        return jnp.where(row_id == row, jnp.sum(value, axis=0, keepdims=True), 0.0)

    live_number = live_ref[0].astype(jnp.float32)

    def sum_start(table, mine, base, devices, iteration):
        copies = []
        for n, device in enumerate(devices):
            block = table.at[iteration, mine]
            copies.append(remote(block, block, sums_sem, (iteration, base + n), device))
            copies[-1].start()
        return copies

    lane_id = lax.broadcasted_iota(jnp.int32, (1, tile), 1)

    def whole(value):
        return jnp.sum(jnp.sum(value, axis=0, keepdims=True), axis=1, keepdims=True)

    energy_copies, scales = [[] for _ in range(ITERS)], []

    def raw_energies(iteration):
        for copy in energy_copies[iteration]:
            copy.wait()
        total = jnp.sum(jnp.sum(energy_recv[iteration, :, :slots, :], axis=0), axis=1, keepdims=True)
        in_row = jnp.sum(jnp.where(row_id[:slots] == lane[:slots], total, 0.0), axis=0, keepdims=True)
        return jnp.where(lane_id < live_ref[0], in_row, 0.0)

    for iteration in range(ITERS):
        for stage in stages:
            for slot in range(slots):
                stage(slot)
        for slot in range(slots):
            back_along_columns(slot, tile * odd)

        def gathered(column, plane, start, length):
            summed = None
            for slot in range(slots):
                term = deposit[slot, column, plane, pl.ds(start + tile - centres_ref[slot, 0], length), :]
                summed = term if summed is None else summed + term
            return summed

        sides, corners = {}, []
        outer = [(name, *piece) for name in ("far", "near") for piece in pieces]
        starts = {"far": far_start, "near": near_start, "middle": tile}
        order = [(place, *entry) for place, entry in enumerate(outer + [("middle", 0, None), ("middle", 1, None)])]

        def send_out(place, name, plane, part):
            if name == "middle":
                rows, start, length = middle, tile, tile
            else:
                rows, start, length = piece_rows(starts[name], part), starts[name] + part * depth, depth
            pair = []
            for side, (column, step, turn) in enumerate(turns):
                fold[iteration, column, plane, rows, :] = gathered(column, plane, start, length)
                if name == "far":
                    corners.append(Copy(
                        remote(
                            fold.at[iteration, column, plane, rows, :],
                            corner_z.at[iteration, side, plane, piece_rows(0, part), :],
                            fold_sem, (iteration, 8 * count + 2 * place + side), at(-pass_step, 0),
                        ),
                        turn, turn,
                    ))
                    corners[-1].start()
                copy = Copy(
                    remote(
                        fold.at[iteration, column, plane, rows, :], fold_x.at[iteration, side, plane, rows, :],
                        fold_sem, (iteration, 2 * place + side), at(0, step),
                    ),
                    *(() if name == "middle" else ((on_right, on_left), (on_left, on_right))[side]),
                )
                copy.start()
                pair.append(copy)
            sides[name, plane, part] = pair

        for entry in order[:count]:
            send_out(*entry)
        for slot in range(slots):
            back_along_columns(slot, tile * (1 - odd))
        for entry in order[count:]:
            send_out(*entry)
        for name in starts:
            for plane in range(2):
                fold[iteration, 1, plane, pl.ds(starts[name], tile), :] = gathered(1, plane, starts[name], tile)

        def add_sides(name, plane, part):
            rows = middle if name == "middle" else piece_rows(starts[name], part)
            for side, copy in enumerate(sides[name, plane, part]):
                def add(side=side):
                    fold[iteration, 1, plane, rows, :] += fold_x[iteration, side, plane, rows, :]

                copy.wait_recv()
                when(None if name == "middle" else (on_left, on_right)[side], add)

        passed_on, folds, straight = [], [], []
        for n, (plane, part) in enumerate(pieces):
            add_sides("far", plane, part)
            passed_on.append(remote(
                fold.at[iteration, 1, plane, piece_rows(far_start, part), :],
                fold_z.at[iteration, plane, piece_rows(0, part), :],
                fold_sem, (iteration, 6 * count + n), at(-pass_step, 0),
            ))
            passed_on[n].start()
        for n, (plane, part) in enumerate(pieces):
            here, rows = piece_rows(0, part), piece_rows(near_start, part)
            for side, (column, step, turn) in enumerate(turns):
                def add_corner(plane=plane, side=side, column=column, here=here, rows=rows):
                    fold[iteration, column, plane, rows, :] += corner_z[iteration, side, plane, here, :]

                corners[2 * n + side].wait_recv()
                when(turn, add_corner)
                straight.append(Copy(
                    remote(
                        fold.at[iteration, column, plane, rows, :], corner_y.at[iteration, side, plane, here, :],
                        fold_sem, (iteration, 10 * count + 2 * n + side), at(pair_step, step),
                    ),
                    turn, turns[1 - side][2],
                ))
                straight[-1].start()
        for n, (plane, part) in enumerate(pieces):
            here, rows = piece_rows(0, part), piece_rows(near_start, part)
            add_sides("near", plane, part)
            passed_on[n].wait_recv()
            fold[iteration, 1, plane, rows, :] += fold_z[iteration, plane, here, :]
            folds.append(remote(
                fold.at[iteration, 1, plane, rows, :], fold_y.at[iteration, plane, here, :],
                fold_sem, (iteration, 7 * count + n), at(pair_step, 0),
            ))
            folds[n].start()
        for plane in range(2):
            add_sides("middle", plane, None)
        for n, (plane, part) in enumerate(pieces):
            here, rows = piece_rows(0, part), piece_rows(tile, part)
            for side in range(2):
                def add_straight(plane=plane, side=side, here=here, rows=rows):
                    fold[iteration, 1, plane, rows, :] += corner_y[iteration, side, plane, here, :]

                straight[2 * n + side].wait_recv()
                when(turns[1 - side][2], add_straight)
        cover = coverage[...]
        gradient, moved = [], []
        for plane in range(2):
            for part in range(PARTS):
                folds[plane * PARTS + part].wait_recv()
            gradient.append(fold[iteration, 1, plane, middle, :] + fold_y[iteration, plane])
            moved.append(gradient[plane] / (cover + 0.5))
            direction_ext[iteration, 1, plane, middle, :] = moved[plane]
        last = iteration == ITERS - 1
        if not last:
            state = start_gather(direction_ext.at[iteration], 1 + iteration)

        squares = moved[0] * moved[0] + moved[1] * moved[1]
        numerator = whole(moved[0] * gradient[0] + moved[1] * gradient[1])
        denominator = whole(cover * squares)
        sums_x[iteration, my_place] = jnp.where(
            lane_id == 0, numerator, jnp.where(lane_id == 1, denominator, jnp.where(lane_id == 2, live_number, 0.0))
        )
        first_sums = sum_start(sums_x, my_place, 0, in_run, iteration)
        if not last:
            passed = pass_near(direction_ext.at[iteration], 1 + iteration, state)
        for n, (k, c) in enumerate(AROUND):
            block = jnp.zeros((8, tile), jnp.float32)
            for slot in range(slots):
                block = block + as_row(squares * shifted[n, slot], slot)
            if n == 4:
                energy_recv[iteration, n] = block
            else:
                energy_send[iteration, n] = block
                copy = remote(
                    energy_send.at[iteration, n, :slots, :], energy_recv.at[iteration, n, :slots, :],
                    energy_sem, (iteration, n), at(k, c),
                )
                copy.start()
                energy_copies[iteration].append(copy)
        for copy in first_sums:
            copy.wait()
        mine = my_run * n_obj + my_obj
        sums_y[iteration, mine] = jnp.sum(sums_x[iteration], axis=0)
        second_sums = sum_start(sums_y, mine, run, across, iteration)
        if not last:
            pass_far(direction_ext.at[iteration], 1 + iteration, state, passed)
        for copy in sent + [copy for pair in sides.values() for copy in pair]:
            copy.wait_send()
        for copy in folds + passed_on + corners + straight:
            copy.wait_send()
        if last:
            raw = [raw_energies(each) for each in range(ITERS)]
        for copy in second_sums:
            copy.wait()
        everywhere = jnp.sum(sums_y[iteration], axis=0)
        numerator, denominator, live_total = (everywhere[:, n : n + 1] for n in range(3))
        step = numerator / denominator
        scales.append((step, live_total / denominator))
        if not last:
            sent = finish_gather(state, passed)
            extended[...] = extended[...] + step.reshape(1, 1, 1, 1) * direction_ext[iteration]
        else:
            object_out[...] = (
                extended[1, :, middle, :] + step.reshape(1, 1, 1) * direction_ext[iteration, 1, :, middle, :]
            )
    step_row = jnp.zeros((1, tile), jnp.float32)
    for iteration in range(ITERS):
        step, scale = scales[iteration]
        step_row = jnp.where(lane_id == iteration, step, step_row)
        energies_out[iteration : iteration + 1, :] = (raw[iteration] * scale)[:, :slots]
    steps_out[...] = step_row[0, :ITERS]


def on_device(n_scan, n_obj, object_field, probe_modes, patterns, gain_map, defect_mask, probe_centres, live_counts):
    tile = object_field.shape[1]
    modes, size = probe_modes.shape[0], probe_modes.shape[1]
    slots = patterns.shape[0]
    extent = tile + size
    table = transform_tables(size)
    f32 = jnp.float32
    vmem = pl.BlockSpec(memory_space=pltpu.VMEM)
    hbm = pl.BlockSpec(memory_space=pltpu.HBM)
    flops = ITERS * slots * modes * 4 * 2 * (2 * size) * size * size
    outputs = pl.pallas_call(
        functools.partial(kernel, n_scan, n_obj),
        out_shape=(
            jax.ShapeDtypeStruct(object_field.shape, f32),
            jax.ShapeDtypeStruct((ITERS,), f32),
            jax.ShapeDtypeStruct((ITERS, slots), f32),
        ),
        in_specs=[hbm] * 8,
        out_specs=(vmem, vmem, vmem),
        scratch_shapes=[
            pltpu.VMEM(probe_modes.shape, f32),
            pltpu.VMEM(patterns.shape, patterns.dtype),
            pltpu.VMEM(gain_map.shape, f32),
            pltpu.VMEM(defect_mask.shape, jnp.int32),
            pltpu.VMEM(table.shape, table.dtype),
            pltpu.SMEM(probe_centres.shape, jnp.int32),
            pltpu.SMEM(live_counts.shape, jnp.int32),
            pltpu.SMEM((9, 128), jnp.int32),
            pltpu.VMEM((3, 2, extent, tile), f32),
            pltpu.VMEM((ITERS, 3, 2, extent, tile), f32),
            pltpu.VMEM((slots, size, size), f32),
            pltpu.VMEM((2, size + 2 * tile, tile), f32),
            pltpu.VMEM((9, slots, tile, tile), f32),
            pltpu.VMEM((tile, tile), f32),
            pltpu.VMEM((slots, 2, size, size), f32),
            pltpu.VMEM((slots, modes, size, 2 * size), jnp.bfloat16),
            pltpu.VMEM((slots, modes, 2 * size, size), jnp.bfloat16),
            pltpu.VMEM((slots, modes, 2 * size, size), f32),
            pltpu.VMEM((slots, 3, 2, size + 2 * tile, tile), f32),
            pltpu.VMEM((ITERS, 3, 2, extent, tile), f32),
            pltpu.VMEM((ITERS, 2, 2, extent, tile), f32),
            pltpu.VMEM((ITERS, 2, tile, tile), f32),
            pltpu.VMEM((ITERS, 2, tile, tile), f32),
            pltpu.VMEM((ITERS, 2, 2, tile, tile), f32),
            pltpu.VMEM((ITERS, 2, 2, tile, tile), f32),
            pltpu.VMEM((ITERS, 9, 8, tile), f32),
            pltpu.VMEM((ITERS, 9, 8, tile), f32),
            pltpu.VMEM((ITERS, n_scan // 2, 1, tile), f32),
            pltpu.VMEM((ITERS, 2 * n_obj, 1, tile), f32),
            pltpu.SemaphoreType.DMA((8,)),
            pltpu.SemaphoreType.DMA((2, 9)),
            pltpu.SemaphoreType.DMA((2, ITERS, 24 * PARTS)),
            pltpu.SemaphoreType.DMA((2, ITERS, 24 * PARTS)),
            pltpu.SemaphoreType.DMA((2, ITERS, 9)),
            pltpu.SemaphoreType.DMA((2, ITERS, n_scan // 2 + 2 * n_obj)),
        ],
        compiler_params=pltpu.CompilerParams(
            collective_id=0, has_side_effects=True, vmem_limit_bytes=55000 * 1024
        ),
        cost_estimate=pl.CostEstimate(flops=flops, bytes_accessed=8 * 1024 * 1024, transcendentals=0),
    )(object_field, probe_modes, patterns, gain_map, defect_mask, table, probe_centres, live_counts)
    return tuple(outputs)


def solution(mesh):
    placed = (
        P(None, "obj", "scan"),
        P(),
        P(("scan", "obj"), None, None),
        P(),
        P(),
        P(("scan", "obj"), None),
        P(("scan", "obj")),
    )
    return jax.shard_map(
        functools.partial(on_device, mesh.shape["scan"], mesh.shape["obj"]),
        mesh=mesh,
        in_specs=placed,
        out_specs=(P(None, "obj", "scan"), P(), P(None, ("scan", "obj"))),
        check_vma=False,
    )
```
